32 devices in a mesh: seq: 8 (over z, y), opt: 4 (over x, core).
Axes of the slice: x: 2, y: 2, z: 4, core: 2. Of those that a mesh axis runs over, the one named last changes fastest.
Arguments:
- inputs: bfloat16 [2, 4, 2048, 768], P(None, 'opt', 'seq'), may hold values from -6 to 6
- key_mask: int32 [2, 4, 2048], P(None, 'opt', 'seq'), may hold values 0 or 1
- lengths: int32 [2, 4], P(None, 'opt'), may hold values from 512 to 2048, as said below
- cotangent: bfloat16 [2, 4, 256, 1280], P(None, 'opt', 'seq'), may hold values from -6 to 6
- latents: float32 [256, 1280], replicated, may hold values from -6 to 6
- lat_vectors: float32 [6, 1280], replicated
- in_vectors: float32 [2, 768], replicated
- w_query: float32 [1280, 768], P('opt'), may hold values from -0.15625 to 0.15625
- w_key: float32 [768, 768], P('opt'), may hold values from -0.21875 to 0.21875
- w_value: float32 [768, 768], P('opt'), may hold values from -0.21875 to 0.21875
- w_out: float32 [768, 1280], P('opt'), may hold values from -3 to 3
- w_up: float32 [1280, 1280], P('opt'), may hold values from -0.15625 to 0.15625
- w_down: float32 [1280, 1280], P('opt'), may hold values from -0.15625 to 0.15625
- mom_query: float32 [1280, 768], P('opt')
- mom_key: float32 [768, 768], P('opt')
- mom_value: float32 [768, 768], P('opt')
- mom_out: float32 [768, 1280], P('opt')
- mom_up: float32 [1280, 1280], P('opt')
- mom_down: float32 [1280, 1280], P('opt')
- lat_first: float32 [6, 1280], replicated
- lat_second: float32 [6, 1280], replicated, as said below
- in_first: float32 [2, 768], replicated
- in_second: float32 [2, 768], replicated, as said below
- latent_first: float32 [256, 1280], replicated
- latent_second: float32 [256, 1280], replicated, as said below
Outputs:
- block_out: bfloat16 [2, 4, 256, 1280], P(None, 'opt', 'seq')
- input_grad: float32 [2, 4, 2048, 768], P(None, 'opt', 'seq')
- mom_query_new: float32 [1280, 768], P('opt')
- mom_key_new: float32 [768, 768], P('opt')
- mom_value_new: float32 [768, 768], P('opt')
- mom_out_new: float32 [768, 1280], P('opt')
- mom_up_new: float32 [1280, 1280], P('opt')
- mom_down_new: float32 [1280, 1280], P('opt')
- w_query_new: float32 [1280, 768], P('opt')
- w_key_new: float32 [768, 768], P('opt')
- w_value_new: float32 [768, 768], P('opt')
- w_out_new: float32 [768, 1280], P('opt')
- w_up_new: float32 [1280, 1280], P('opt')
- w_down_new: float32 [1280, 1280], P('opt')
- lat_first_new: float32 [6, 1280], replicated
- lat_second_new: float32 [6, 1280], replicated
- lat_vectors_new: float32 [6, 1280], replicated
- in_first_new: float32 [2, 768], replicated
- in_second_new: float32 [2, 768], replicated
- in_vectors_new: float32 [2, 768], replicated
- latent_first_new: float32 [256, 1280], replicated
- latent_second_new: float32 [256, 1280], replicated
- latents_new: float32 [256, 1280], replicated
The draws below stay inside these ranges and needn't reach their ends.
Inputs may be any that keep to these rules, and one draw needn't show every extreme that they name: `lengths`: among the 1 documents of each micro-batch on one index of opt, one has length exactly 2048. `lat_second`: every entry is positive. `in_second`: every entry is positive. `latent_second`: every entry is positive.
All inputs are finite; a program needn't handle non-finite values. No bound on the sum of `key_mask` on one device may be relied on, other than what follows from the above.
Results may differ from the reference program's by a relative error of at most 0.025.
Values may be sent and summed in bfloat16 or wider, within the bound.
A program may use at most 256 MiB of HBM per device.

```python
import math
import jax
import jax.numpy as jnp
from jax import lax

D_LAT = 1280
HEADS = 8
HEAD_DIM = 96
E_IN = 768
LATENTS = 256
LEN = 2048
MICRO = 2
DOC_MB = 1
DOCS = 4
STEP = 10
OUT_FAN = 4


def grad_scales():
    rows_root = math.sqrt(MICRO * DOCS * LATENTS)
    key_count = 0.55 * MICRO * DOCS * LEN
    back_out = 1.3 * math.sqrt(D_LAT / OUT_FAN)
    key_back = back_out * math.sqrt(LATENTS) * 3.0 / LEN * math.sqrt(key_count)
    spread_out = math.sqrt(0.0025 + 5.0 / LEN)
    return (rows_root, key_back, key_back, 1.3 * spread_out * rows_root, 0.6 * rows_root, 0.65 * rows_root, 1.4 * key_back, 1.6 * math.sqrt(MICRO * DOCS))


def ramp(count):
    return 0.6 * 3.0 ** (jnp.arange(count, dtype=jnp.float32) / max(count - 1, 1))


def moment_draw(key, rows, cols, size_scale):
    return jax.random.normal(key, (rows, cols), jnp.float32) * size_scale * ramp(rows)[:, None]


def second_draw(key, row_scales, cols):
    factor = jnp.exp(jax.random.uniform(key, (row_scales.shape[0], cols), jnp.float32, 0.0, math.log(4.0)))
    return 0.95 ** (-1) * 0.05 * row_scales[:, None] ** 2 * factor


def lat_scales():
    scales = grad_scales()
    return jnp.array([scales[0], scales[0], scales[4], scales[4], scales[4], scales[0]], jnp.float32)


def draw_lengths(key, part):
    key = jax.random.fold_in(key, 1)
    base = jax.random.randint(jax.random.fold_in(key, 2), (MICRO, DOCS), LEN // 4, LEN + 1)
    pick = jax.random.randint(jax.random.fold_in(key, 3), (MICRO, DOCS // DOC_MB), 0, DOC_MB)
    slot = jnp.arange(DOCS, dtype=jnp.int32) % DOC_MB
    block = jnp.arange(DOCS, dtype=jnp.int32) // DOC_MB
    full = slot[None, :] == pick[:, block]
    return jnp.where(full, LEN, base).astype(jnp.int32)


def draw_lat_vectors(key, part):
    key = jax.random.fold_in(key, 4)
    first_gain = ramp(D_LAT) * jax.random.uniform(jax.random.fold_in(key, 1), (D_LAT,), jnp.float32, 0.9, 1.1)
    second_gain = ramp(D_LAT) * jax.random.uniform(jax.random.fold_in(key, 2), (D_LAT,), jnp.float32, 0.9, 1.1)
    biases = 0.1 * jax.random.normal(jax.random.fold_in(key, 3), (4, D_LAT), jnp.float32)
    return jnp.stack([first_gain, biases[0], second_gain, biases[1], biases[2], biases[3]])


def draw_in_vectors(key, part):
    key = jax.random.fold_in(key, 5)
    gain_row = ramp(E_IN) * jax.random.uniform(jax.random.fold_in(key, 1), (E_IN,), jnp.float32, 0.9, 1.1)
    shift_row = 0.05 * jax.random.normal(jax.random.fold_in(key, 2), (E_IN,), jnp.float32)
    return jnp.stack([gain_row, shift_row])


def draw_mom_query(key, part):
    return moment_draw(jax.random.fold_in(key, 11), D_LAT, E_IN, grad_scales()[0])


def draw_mom_key(key, part):
    return moment_draw(jax.random.fold_in(key, 12), E_IN, E_IN, grad_scales()[1])


def draw_mom_value(key, part):
    return moment_draw(jax.random.fold_in(key, 13), E_IN, E_IN, grad_scales()[2])


def draw_mom_out(key, part):
    return moment_draw(jax.random.fold_in(key, 14), E_IN, D_LAT, grad_scales()[3])


def draw_mom_up(key, part):
    return moment_draw(jax.random.fold_in(key, 15), D_LAT, D_LAT, grad_scales()[4])


def draw_mom_down(key, part):
    return moment_draw(jax.random.fold_in(key, 16), D_LAT, D_LAT, grad_scales()[5])


def draw_lat_first(key, part):
    key = jax.random.fold_in(key, 21)
    return jax.random.normal(key, (6, D_LAT), jnp.float32) * lat_scales()[:, None] / 9.0


def draw_lat_second(key, part):
    return second_draw(jax.random.fold_in(key, 22), lat_scales(), D_LAT)


def draw_in_first(key, part):
    key = jax.random.fold_in(key, 23)
    return jax.random.normal(key, (2, E_IN), jnp.float32) * grad_scales()[6] / 9.0


def draw_in_second(key, part):
    return second_draw(jax.random.fold_in(key, 24), jnp.full((2,), grad_scales()[6], jnp.float32), E_IN)


def draw_latent_first(key, part):
    key = jax.random.fold_in(key, 25)
    return jax.random.normal(key, (LATENTS, D_LAT), jnp.float32) * grad_scales()[7] / 9.0


def draw_latent_second(key, part):
    return second_draw(jax.random.fold_in(key, 26), jnp.full((LATENTS,), grad_scales()[7], jnp.float32), D_LAT)


def touch_ends(values, rng, smallest, largest):
    longest = values.shape.index(max(values.shape))
    spots = []
    for shift in (0, 1):
        where = [jax.random.randint(jax.random.fold_in(rng, axis), (), 0, length) for axis, length in enumerate(values.shape)]
        where[longest] = (where[longest] + shift) % values.shape[longest]
        spots.append(tuple(where))
    return values.at[spots[0]].set(smallest).at[spots[1]].set(largest)


def level_of(own_key, shape, shards, low, high):
    level = 1.0
    for dim, blocks in shards:
        heights = jax.random.uniform(jax.random.fold_in(jax.random.fold_in(own_key, 6), dim), (blocks,), jnp.float32, low / len(shards), high / len(shards))
        level = level * jnp.repeat(jnp.exp(heights), shape[dim] // blocks).reshape((-1,) + (1,) * (len(shape) - 1 - dim))
    return level


def normal_values(own_key, dims, spread, most, cuts=(), kind=jnp.bfloat16):
    values = jax.random.normal(own_key, dims, jnp.float32) * spread
    if len(cuts) > 0:
        values = level_of(own_key, dims, cuts, -0.22, 0.18) * values
    return jnp.clip(values, min=-most, max=most).astype(kind)


def setup_inputs(seed: int = 0) -> dict:
    seeds = jax.random.split(jax.random.key(seed), 26)
    inputs = normal_values(seeds[0], (MICRO, DOCS, LEN, E_IN), 1.0, 6.0, ((1, 4), (2, 8)))
    key_mask = touch_ends((jax.random.randint(seeds[1], (MICRO, DOCS, LEN), 0, 8) < 7).astype(jnp.int32), jax.random.fold_in(seeds[1], 1), 0, 1)
    lengths = draw_lengths(jax.random.fold_in(seeds[25], 71), 0)
    cotangent = normal_values(seeds[3], (MICRO, DOCS, LATENTS, D_LAT), 1.0, 6.0, ((1, 4), (2, 8)))
    latents = normal_values(seeds[4], (LATENTS, D_LAT), 1.0, 6.0, (), jnp.float32)
    lat_vectors = draw_lat_vectors(jax.random.fold_in(seeds[25], 71), 0)
    in_vectors = draw_in_vectors(jax.random.fold_in(seeds[25], 71), 0)
    w_query = normal_values(seeds[7], (D_LAT, E_IN), D_LAT ** -0.5, 0.15625, ((0, 4),), jnp.float32)
    w_key = normal_values(seeds[8], (E_IN, E_IN), E_IN ** -0.5, 0.21875, ((0, 4),), jnp.float32)
    w_value = normal_values(seeds[9], (E_IN, E_IN), E_IN ** -0.5, 0.21875, ((0, 4),), jnp.float32)
    w_out = normal_values(seeds[10], (E_IN, D_LAT), OUT_FAN ** -0.5, 3.0, ((0, 4),), jnp.float32)
    w_up = normal_values(seeds[11], (D_LAT, D_LAT), D_LAT ** -0.5, 0.15625, ((0, 4),), jnp.float32)
    w_down = normal_values(seeds[12], (D_LAT, D_LAT), D_LAT ** -0.5, 0.15625, ((0, 4),), jnp.float32)
    mom_query = draw_mom_query(jax.random.fold_in(seeds[25], 71), 0)
    mom_key = draw_mom_key(jax.random.fold_in(seeds[25], 71), 0)
    mom_value = draw_mom_value(jax.random.fold_in(seeds[25], 71), 0)
    mom_out = draw_mom_out(jax.random.fold_in(seeds[25], 71), 0)
    mom_up = draw_mom_up(jax.random.fold_in(seeds[25], 71), 0)
    mom_down = draw_mom_down(jax.random.fold_in(seeds[25], 71), 0)
    lat_first = draw_lat_first(jax.random.fold_in(seeds[25], 71), 0)
    lat_second = draw_lat_second(jax.random.fold_in(seeds[25], 71), 0)
    in_first = draw_in_first(jax.random.fold_in(seeds[25], 71), 0)
    in_second = draw_in_second(jax.random.fold_in(seeds[25], 71), 0)
    latent_first = draw_latent_first(jax.random.fold_in(seeds[25], 71), 0)
    latent_second = draw_latent_second(jax.random.fold_in(seeds[25], 71), 0)
    return {"inputs": inputs, "key_mask": key_mask, "lengths": lengths, "cotangent": cotangent, "latents": latents, "lat_vectors": lat_vectors, "in_vectors": in_vectors, "w_query": w_query, "w_key": w_key, "w_value": w_value, "w_out": w_out, "w_up": w_up, "w_down": w_down, "mom_query": mom_query, "mom_key": mom_key, "mom_value": mom_value, "mom_out": mom_out, "mom_up": mom_up, "mom_down": mom_down, "lat_first": lat_first, "lat_second": lat_second, "in_first": in_first, "in_second": in_second, "latent_first": latent_first, "latent_second": latent_second}


@jax.custom_vjp
def low(v):
    return lax.optimization_barrier(v.astype(jnp.bfloat16)).astype(jnp.float32)

@jax.custom_vjp
def low_back(v):
    return v

def low_keep(v):
    return (low(v), None)

def low_pass(kept, grad):
    return (grad,)

def back_keep(v):
    return (v, None)

def back_low(kept, grad):
    return (low(grad),)
low.defvjp(low_keep, low_pass)
low_back.defvjp(back_keep, back_low)
highest = lax.Precision.HIGHEST
coef_one = 3.4445
coef_two = -4.775
coef_three = 2.0315

def matmul(left, right):
    return jnp.matmul(left, right, precision=highest)

def normalize(values, scale_vec, offset):
    center = lax.optimization_barrier(jnp.mean(values, axis=-1, keepdims=True))
    shifted = values - center
    inverse = lax.rsqrt(lax.optimization_barrier(jnp.mean(shifted * shifted, axis=-1, keepdims=True)) + 1e-05)
    return shifted * inverse * scale_vec + offset

def document(param_tree, token_rows, usable):
    latents, lat_vectors, in_vectors, w_query, w_key, w_value, w_out, w_up, w_down = param_tree
    queries = low(matmul(low(normalize(latents, lat_vectors[0], lat_vectors[1])), low(w_query)))
    normed = low(normalize(token_rows, in_vectors[0], in_vectors[1]))
    key_rows = low_back(low(matmul(normed, low(w_key))))
    value_rows = low_back(low(matmul(normed, low(w_value))))
    query_heads = queries.reshape(LATENTS, HEADS, HEAD_DIM)
    key_heads = key_rows.reshape(LEN, HEADS, HEAD_DIM)
    value_heads = value_rows.reshape(LEN, HEADS, HEAD_DIM)
    scores = low_back(jnp.einsum('nhd,shd->hns', query_heads, key_heads, precision=highest) * HEAD_DIM ** (-0.5))
    masked = jnp.where(usable[None, None, :], scores, -1e+30)
    row_max = lax.optimization_barrier(jnp.max(masked, axis=-1, keepdims=True))
    weights = jnp.exp(masked - row_max)
    row_sum = lax.optimization_barrier(jnp.sum(weights, axis=-1))
    summed = low_back(jnp.einsum('hns,shd->nhd', low(weights), value_heads, precision=highest))
    attended = (summed / row_sum.T[:, :, None]).reshape(LATENTS, E_IN)
    hidden = latents + low_back(matmul(low_back(low(attended)), low(w_out)))
    mlp_input = low(normalize(hidden, lat_vectors[2], lat_vectors[3]))
    pre_act = low_back(matmul(mlp_input, low(w_up)) + lat_vectors[4])
    activated = low(jax.nn.gelu(pre_act, approximate=False))
    return hidden + matmul(activated, low(w_down)) + lat_vectors[5]

def orthogonalize(moment):
    current = moment / (jnp.sqrt(jnp.sum(moment * moment)) + 1e-07)
    for sweep in range(5):
        gram = matmul(current.T, current)
        product = matmul(current, gram)
        current = coef_one * current + coef_two * product + coef_three * matmul(product, gram)
    return current

def adam_update(param, gradient, first, second, step_rate, decay):
    first_new = 0.9 * first + 0.1 * gradient
    second_new = 0.95 * second + 0.05 * gradient * gradient
    ratio = first_new / (1.0 - 0.9 ** STEP) / (jnp.sqrt(second_new / (1.0 - 0.95 ** STEP)) + 1e-08)
    return (first_new, second_new, param - step_rate * (ratio + decay * param))

def reference(inputs, key_mask, lengths, cotangent, latents, lat_vectors, in_vectors, w_query, w_key, w_value, w_out, w_up, w_down, mom_query, mom_key, mom_value, mom_out, mom_up, mom_down, lat_first, lat_second, in_first, in_second, latent_first, latent_second):
    params = (latents, lat_vectors, in_vectors, w_query, w_key, w_value, w_out, w_up, w_down)
    doc_count = MICRO * DOCS
    positions = jnp.arange(LEN, dtype=jnp.int32)

    def one_doc(running, record):
        token_rows, mask_row, length, cotan_row = record
        usable = (positions < length) & ((mask_row == 1) | (positions == 0))
        result, pullback = jax.vjp(lambda param_tree, token_vals: document(param_tree, token_vals, usable), params, token_rows.astype(jnp.float32))
        gradients, token_grad = pullback(cotan_row.astype(jnp.float32))
        running = jax.tree.map(jnp.add, running, gradients)
        return (running, (result.astype(jnp.bfloat16), token_grad))
    start_tree = jax.tree.map(jnp.zeros_like, params)
    records = (inputs.reshape(doc_count, LEN, E_IN), key_mask.reshape(doc_count, LEN), lengths.reshape(doc_count), cotangent.reshape(doc_count, LATENTS, D_LAT))
    totals, (outputs, in_grads) = lax.scan(one_doc, start_tree, records)
    latent_grad, lat_vec_grad, in_vec_grad = (totals[0], totals[1], totals[2])
    masters = (w_query, w_key, w_value, w_out, w_up, w_down)
    moments = (mom_query, mom_key, mom_value, mom_out, mom_up, mom_down)
    fans = (D_LAT, E_IN, E_IN, OUT_FAN, D_LAT, D_LAT)
    sides = (D_LAT, E_IN, E_IN, D_LAT, D_LAT, D_LAT)
    new_moments = []
    new_masters = []
    for master, moment, gradient, fan_in, long_side in zip(masters, moments, totals[3:], fans, sides):
        moment_new = 0.95 * moment + gradient
        step_rate = fan_in ** (-0.5)
        new_moments.append(moment_new)
        new_masters.append((1.0 - 0.1 * step_rate) * master - step_rate * long_side ** 0.5 * orthogonalize(moment_new))
    lat_m, lat_v, lat_p = adam_update(lat_vectors, lat_vec_grad, lat_first, lat_second, 0.6, 0.0)
    in_m, in_v, in_p = adam_update(in_vectors, in_vec_grad, in_first, in_second, 0.6, 0.0)
    latent_m, latent_v, latent_p = adam_update(latents, latent_grad, latent_first, latent_second, 1.0, 0.1)
    block_out = outputs.reshape(MICRO, DOCS, LATENTS, D_LAT)
    input_grad = in_grads.reshape(MICRO, DOCS, LEN, E_IN)
    return (block_out, input_grad, new_moments[0], new_moments[1], new_moments[2], new_moments[3], new_moments[4], new_moments[5], new_masters[0], new_masters[1], new_masters[2], new_masters[3], new_masters[4], new_masters[5], lat_m, lat_v, lat_p, in_m, in_v, in_p, latent_m, latent_v, latent_p)
```

```python
import jax
import jax.numpy as jnp
from jax import lax
from jax.experimental import pallas as pl
from jax.experimental.pallas import tpu as pltpu
from jax.sharding import PartitionSpec as P

D_LAT = 1280
HEADS = 8
HEAD_DIM = 96
E_IN = 768
STEP = 10
OUT_FAN = 4
TILE = 256


highest = lax.Precision.HIGHEST
coef_one = 3.4445
coef_two = -4.775
coef_three = 2.0315


def layer_norm(values, scale_vec, offset):
    center = jnp.mean(values, axis=-1, keepdims=True)
    shifted = values - center
    inverse = lax.rsqrt(jnp.mean(shifted * shifted, axis=-1, keepdims=True) + 1e-05)
    normal_hat = shifted * inverse
    return (normal_hat * scale_vec + offset, normal_hat, inverse)


def norm_back(grad_out, normal_hat, inverse, scale_vec):
    scaled = grad_out * scale_vec
    return inverse * (
        scaled
        - jnp.mean(scaled, axis=-1, keepdims=True)
        - normal_hat * jnp.mean(scaled * normal_hat, axis=-1, keepdims=True)
    )


def exact_gelu(values):
    return jax.nn.gelu(values, approximate=False)


def masked_scores(query_heads, key_heads, usable, score_scale):
    scores = (
        jnp.einsum("nhd,bshd->bhns", query_heads, key_heads, preferred_element_type=jnp.float32)
        * score_scale
    )
    return jnp.where(usable[:, None, None, :], scores, -1e30)


def newton_body(rows_ref, out_ref, wide, low, gram, poly, total):
    count, side = rows_ref.shape
    row_tiles, side_tiles = count // TILE, side // TILE
    total[0] = 0.0

    def add_squares(tile, carry):
        block = rows_ref[pl.ds(tile * TILE, TILE), :].astype(jnp.float32)
        total[0] = total[0] + jnp.sum(block * block)
        return carry

    lax.fori_loop(0, row_tiles, add_squares, 0)
    scale = 1.0 / (jnp.sqrt(jnp.full((1, 1), total[0], jnp.float32)) + 1e-07)

    def normalise(tile, carry):
        block = rows_ref[pl.ds(tile * TILE, TILE), :].astype(jnp.float32) * scale
        wide[pl.ds(tile * TILE, TILE), :] = block
        low[pl.ds(tile * TILE, TILE), :] = block.astype(jnp.bfloat16)
        return carry

    lax.fori_loop(0, row_tiles, normalise, 0)

    def sweep(index, carry):
        for i in range(side_tiles):
            own = slice(i * TILE, (i + 1) * TILE)
            for j in range(i, side_tiles):
                other = slice(j * TILE, (j + 1) * TILE)
                block = lax.dot_general(
                    low[:, own],
                    low[:, other],
                    (((0,), (0,)), ((), ())),
                    preferred_element_type=jnp.float32,
                )
                gram[own, other] = block.astype(jnp.bfloat16)
                if j > i:
                    gram[other, own] = block.T.astype(jnp.bfloat16)
        for i in range(side_tiles):
            own = slice(i * TILE, (i + 1) * TILE)
            block = coef_three * jnp.dot(
                gram[own, :], gram[:, i * TILE :], preferred_element_type=jnp.float32
            ) + coef_two * gram[own, i * TILE :].astype(jnp.float32)
            poly[own, i * TILE :] = block.astype(jnp.bfloat16)
            for j in range(i + 1, side_tiles):
                part = block[:, (j - i) * TILE : (j - i + 1) * TILE]
                poly[j * TILE : (j + 1) * TILE, own] = part.T.astype(jnp.bfloat16)

        def update(tile, inner):
            rows = pl.ds(tile * TILE, TILE)
            block = coef_one * wide[rows, :] + jnp.dot(
                low[rows, :], poly[...], preferred_element_type=jnp.float32
            )
            wide[rows, :] = block
            low[rows, :] = block.astype(jnp.bfloat16)
            return inner

        lax.fori_loop(0, row_tiles, update, 0)
        return carry

    lax.fori_loop(0, 5, sweep, 0)
    out_ref[...] = low[...]


def newton(rows):
    shape = rows.shape
    return pl.pallas_call(
        newton_body,
        out_shape=jax.ShapeDtypeStruct(shape, jnp.bfloat16),
        in_specs=[pl.BlockSpec(memory_space=pltpu.VMEM)],
        out_specs=pl.BlockSpec(memory_space=pltpu.VMEM),
        scratch_shapes=[
            pltpu.VMEM(shape, jnp.float32),
            pltpu.VMEM(shape, jnp.bfloat16),
            pltpu.VMEM((shape[1], shape[1]), jnp.bfloat16),
            pltpu.VMEM((shape[1], shape[1]), jnp.bfloat16),
            pltpu.SMEM((1,), jnp.float32),
        ],
        compiler_params=pltpu.CompilerParams(vmem_limit_bytes=60 * 2**20),
        name="newton",
    )(rows)


def adam_update(param, gradient, first, second, step_rate, decay):
    first_new = 0.9 * first + 0.1 * gradient
    second_new = 0.95 * second + 0.05 * gradient * gradient
    ratio = first_new / (1.0 - 0.9**STEP) / (jnp.sqrt(second_new / (1.0 - 0.95**STEP)) + 1e-08)
    return (first_new, second_new, param - step_rate * (ratio + decay * param))


def local(
    inputs,
    key_mask,
    lengths,
    cotangent,
    latents,
    lat_vectors,
    in_vectors,
    w_query,
    w_key,
    w_value,
    w_out,
    w_up,
    w_down,
    mom_query,
    mom_key,
    mom_value,
    mom_out,
    mom_up,
    mom_down,
    lat_first,
    lat_second,
    in_first,
    in_second,
    latent_first,
    latent_second,
):
    query_low, key_low, value_low, out_low, up_low, down_low = (
        lax.all_gather(w_query.astype(jnp.bfloat16), "opt", axis=0, tiled=True),
        lax.all_gather(w_key.astype(jnp.bfloat16), "opt", axis=0, tiled=True),
        lax.all_gather(w_value.astype(jnp.bfloat16), "opt", axis=0, tiled=True),
        lax.all_gather(w_out.astype(jnp.bfloat16), "opt", axis=0, tiled=True),
        lax.all_gather(w_up.astype(jnp.bfloat16), "opt", axis=0, tiled=True),
        lax.all_gather(w_down.astype(jnp.bfloat16), "opt", axis=0, tiled=True),
    )
    pair_low = jnp.concatenate([key_low, value_low], axis=1)
    seq_index = lax.axis_index("seq")
    seq_size = lax.axis_size("seq")
    opt_index = lax.axis_index("opt")
    opt_size = lax.axis_size("opt")
    micro_count, doc_local, span, width_in = inputs.shape
    lat_count, width_lat = latents.shape
    own_rows = lat_count // seq_size
    row_start = seq_index * own_rows
    score_scale = HEAD_DIM ** (-0.5)
    lat_normed, lat_hat, lat_inv = layer_norm(latents, lat_vectors[0], lat_vectors[1])
    lat_low = lat_normed.astype(jnp.bfloat16)
    query_rows = jnp.dot(lat_low, query_low, preferred_element_type=jnp.float32).astype(
        jnp.bfloat16
    )
    query_heads = query_rows.reshape(lat_count, HEADS, HEAD_DIM)
    own_latents = lax.dynamic_slice_in_dim(latents, row_start, own_rows, 0)
    positions = seq_index * span + jnp.arange(span, dtype=jnp.int32)
    grad_query_rows = jnp.zeros((lat_count, width_in), jnp.float32)
    grad_pair = jnp.zeros((width_in, 2 * width_in), jnp.float32)
    grad_out_w = jnp.zeros((width_in, width_lat), jnp.float32)
    grad_up_w = jnp.zeros((width_lat, width_lat), jnp.float32)
    grad_down_w = jnp.zeros((width_lat, width_lat), jnp.float32)
    mlp_gain = jnp.zeros((width_lat,), jnp.float32)
    mlp_shift = jnp.zeros((width_lat,), jnp.float32)
    bias_up = jnp.zeros((width_lat,), jnp.float32)
    bias_down = jnp.zeros((width_lat,), jnp.float32)
    in_gain = jnp.zeros((width_in,), jnp.float32)
    in_shift = jnp.zeros((width_in,), jnp.float32)
    latent_rest = jnp.zeros((own_rows, width_lat), jnp.float32)
    block_parts = []
    input_parts = []
    for micro_step in range(micro_count):
        tokens = inputs[micro_step]
        usable = (positions[None, :] < lengths[micro_step][:, None]) & (
            (key_mask[micro_step] == 1) | (positions[None, :] == 0)
        )
        in_normed, in_hat, in_inv = layer_norm(
            tokens.astype(jnp.float32), in_vectors[0], in_vectors[1]
        )
        in_low = in_normed.astype(jnp.bfloat16)
        pair_rows = jnp.einsum(
            "bse,ef->bsf", in_low, pair_low, preferred_element_type=jnp.float32
        ).astype(jnp.bfloat16)
        key_heads = pair_rows[:, :, :width_in].reshape(doc_local, span, HEADS, HEAD_DIM)
        value_heads = pair_rows[:, :, width_in:].reshape(doc_local, span, HEADS, HEAD_DIM)
        masked = masked_scores(query_heads, key_heads, usable, score_scale)
        row_max = lax.pmax(jnp.max(masked, axis=-1), "seq")
        weights = jnp.exp(masked - row_max[..., None])
        weights_low = weights.astype(jnp.bfloat16)
        summed, row_sum = (
            lax.psum(
                jnp.einsum(
                    "bhns,bshd->bnhd", weights_low, value_heads, preferred_element_type=jnp.float32
                ).astype(jnp.bfloat16),
                "seq",
            ).astype(jnp.float32),
            lax.psum(jnp.sum(weights, axis=-1).astype(jnp.bfloat16), "seq").astype(jnp.float32),
        )
        sum_heads = jnp.transpose(row_sum, (0, 2, 1))[..., None]
        attended = summed / sum_heads
        own_att = (
            lax.dynamic_slice_in_dim(attended, row_start, own_rows, 1)
            .reshape(doc_local, own_rows, width_in)
            .astype(jnp.bfloat16)
        )
        hidden = own_latents[None] + jnp.einsum(
            "bne,ef->bnf", own_att, out_low, preferred_element_type=jnp.float32
        )
        mlp_normed, mlp_hat, mlp_inv = layer_norm(hidden, lat_vectors[2], lat_vectors[3])
        mlp_low = mlp_normed.astype(jnp.bfloat16)
        pre_act = (
            jnp.einsum("bnf,fg->bng", mlp_low, up_low, preferred_element_type=jnp.float32)
            + lat_vectors[4]
        )
        activated, gelu_pull = jax.vjp(exact_gelu, pre_act)
        act_low = activated.astype(jnp.bfloat16)
        block_parts.append(
            (
                hidden
                + jnp.einsum("bng,gk->bnk", act_low, down_low, preferred_element_type=jnp.float32)
                + lat_vectors[5]
            ).astype(jnp.bfloat16)
        )
        back_rows = cotangent[micro_step]
        grad_down_w = grad_down_w + jnp.einsum(
            "bng,bnk->gk", act_low, back_rows, preferred_element_type=jnp.float32
        )
        bias_down = bias_down + jnp.sum(back_rows.astype(jnp.float32), axis=(0, 1))
        grad_act = jnp.einsum(
            "bnk,gk->bng", back_rows, down_low, preferred_element_type=jnp.float32
        )
        grad_pre = gelu_pull(grad_act)[0].astype(jnp.bfloat16)
        grad_up_w = grad_up_w + jnp.einsum(
            "bnf,bng->fg", mlp_low, grad_pre, preferred_element_type=jnp.float32
        )
        bias_up = bias_up + jnp.sum(grad_pre.astype(jnp.float32), axis=(0, 1))
        grad_mlp = jnp.einsum("bng,fg->bnf", grad_pre, up_low, preferred_element_type=jnp.float32)
        mlp_gain = mlp_gain + jnp.sum(grad_mlp * mlp_hat, axis=(0, 1))
        mlp_shift = mlp_shift + jnp.sum(grad_mlp, axis=(0, 1))
        grad_hidden = back_rows.astype(jnp.float32) + norm_back(
            grad_mlp, mlp_hat, mlp_inv, lat_vectors[2]
        )
        latent_rest = latent_rest + jnp.sum(grad_hidden, axis=0)
        grad_branch = grad_hidden.astype(jnp.bfloat16)
        grad_out_w = grad_out_w + jnp.einsum(
            "bne,bnf->ef", own_att, grad_branch, preferred_element_type=jnp.float32
        )
        grad_own = jnp.einsum(
            "bnf,ef->bne", grad_branch, out_low, preferred_element_type=jnp.float32
        ).astype(jnp.bfloat16)
        grad_att = (
            lax.all_gather(grad_own, "seq", axis=1, tiled=True)
            .astype(jnp.float32)
            .reshape(doc_local, lat_count, HEADS, HEAD_DIM)
        )
        grad_summed = (grad_att / sum_heads).astype(jnp.bfloat16)
        inner = jnp.transpose(jnp.sum(grad_att * attended, axis=-1) / sum_heads[..., 0], (0, 2, 1))
        grad_prob = jnp.einsum(
            "bnhd,bshd->bhns", grad_summed, value_heads, preferred_element_type=jnp.float32
        )
        grad_scores = (weights * (grad_prob - inner[..., None])).astype(jnp.bfloat16)
        grad_query_rows = grad_query_rows + score_scale * jnp.einsum(
            "bhns,bshd->nhd", grad_scores, key_heads, preferred_element_type=jnp.float32
        ).reshape(lat_count, width_in)
        grad_keys = (
            score_scale
            * jnp.einsum(
                "bhns,nhd->bshd", grad_scores, query_heads, preferred_element_type=jnp.float32
            )
        ).astype(jnp.bfloat16)
        grad_values = jnp.einsum(
            "bhns,bnhd->bshd", weights_low, grad_summed, preferred_element_type=jnp.float32
        ).astype(jnp.bfloat16)
        grad_pairs = jnp.concatenate(
            [
                grad_keys.reshape(doc_local, span, width_in),
                grad_values.reshape(doc_local, span, width_in),
            ],
            axis=-1,
        )
        grad_pair = grad_pair + jnp.einsum(
            "bse,bsf->ef", in_low, grad_pairs, preferred_element_type=jnp.float32
        )
        grad_in = jnp.einsum(
            "bsf,ef->bse", grad_pairs, pair_low, preferred_element_type=jnp.float32
        )
        in_gain = in_gain + jnp.sum(grad_in * in_hat, axis=(0, 1))
        in_shift = in_shift + jnp.sum(grad_in, axis=(0, 1))
        input_parts.append(norm_back(grad_in, in_hat, in_inv, in_vectors[0]))
    grad_query_w = jnp.matmul(lat_low.astype(jnp.float32).T, grad_query_rows, precision=highest)
    grad_lat = jnp.matmul(grad_query_rows, query_low.astype(jnp.float32).T, precision=highest)
    zero_index = jnp.zeros((), jnp.int32)
    latent_grad = norm_back(grad_lat, lat_hat, lat_inv, lat_vectors[0]) + lax.dynamic_update_slice(
        jnp.zeros_like(latents), latent_rest, (row_start, zero_index)
    )
    lat_vec_grad = jnp.stack(
        [
            jnp.sum(grad_lat * lat_hat, axis=0),
            jnp.sum(grad_lat, axis=0),
            mlp_gain,
            mlp_shift,
            bias_up,
            bias_down,
        ]
    )
    in_vec_grad = jnp.stack([in_gain, in_shift])
    weight_grads = (
        grad_query_w,
        grad_pair[:, :width_in],
        grad_pair[:, width_in:],
        grad_out_w,
        grad_up_w,
        grad_down_w,
    )
    masters = (w_query, w_key, w_value, w_out, w_up, w_down)
    moments = (mom_query, mom_key, mom_value, mom_out, mom_up, mom_down)
    first_here = jnp.where(seq_index == 0, 0.95, 0.0)
    with_moment = []
    for gradient, moment in zip(weight_grads, moments):
        start = opt_index * moment.shape[0]
        rows = lax.dynamic_slice_in_dim(gradient, start, moment.shape[0], 0) + first_here * moment
        with_moment.append(
            lax.dynamic_update_slice(gradient, rows, (start, zero_index)).astype(jnp.bfloat16)
        )
    summed_low = lax.psum(tuple(with_moment), ("seq", "opt"))
    lat_vec_sum, in_vec_sum, latent_sum = lax.psum(
        (lat_vec_grad, in_vec_grad, latent_grad), ("seq", "opt")
    )
    moments_new = [
        lax.dynamic_slice_in_dim(summed, opt_index * moment.shape[0], moment.shape[0], 0).astype(
            jnp.float32
        )
        for summed, moment in zip(summed_low, moments)
    ]

    def padded(index):
        def pick():
            matrix = summed_low[index].T if index == 3 else summed_low[index]
            return jnp.pad(
                matrix, ((0, width_lat - matrix.shape[0]), (0, width_lat - matrix.shape[1]))
            )

        return pick

    slot = seq_index % 8
    own_matrix = lax.switch(jnp.minimum(slot, 5), [padded(index) for index in range(6)])
    own_result = newton(own_matrix)
    own_result = lax.cond(slot == 3, lambda: own_result.T, lambda: own_result)
    mine = jnp.stack(
        [
            lax.dynamic_slice_in_dim(own_result, opt_index * height, width_lat // opt_size, 0)
            for height in (width_in // opt_size, width_lat // opt_size)
        ]
    )
    is_wide = (slot == 0) | (slot >= 4)
    mine = jnp.where(is_wide, mine[1], mine[0])
    spread = lax.all_gather(mine, "seq", axis=0, tiled=False)
    currents = [
        spread[index, : moment.shape[0], : moment.shape[1]].astype(jnp.float32)
        for index, moment in enumerate(moments)
    ]
    fans = (D_LAT, E_IN, E_IN, OUT_FAN, D_LAT, D_LAT)
    sides = (D_LAT, E_IN, E_IN, D_LAT, D_LAT, D_LAT)
    new_masters = []
    for master, current, fan_in, long_side in zip(masters, currents, fans, sides):
        step_rate = fan_in ** (-0.5)
        new_masters.append((1.0 - 0.1 * step_rate) * master - step_rate * long_side**0.5 * current)
    lat_m, lat_v, lat_p = adam_update(lat_vectors, lat_vec_sum, lat_first, lat_second, 0.6, 0.0)
    in_m, in_v, in_p = adam_update(in_vectors, in_vec_sum, in_first, in_second, 0.6, 0.0)
    latent_m, latent_v, latent_p = adam_update(
        latents, latent_sum, latent_first, latent_second, 1.0, 0.1
    )
    block_out = jnp.stack(block_parts)
    input_grad = jnp.stack(input_parts)
    return (
        block_out,
        input_grad,
        moments_new[0],
        moments_new[1],
        moments_new[2],
        moments_new[3],
        moments_new[4],
        moments_new[5],
        new_masters[0],
        new_masters[1],
        new_masters[2],
        new_masters[3],
        new_masters[4],
        new_masters[5],
        lat_m,
        lat_v,
        lat_p,
        in_m,
        in_v,
        in_p,
        latent_m,
        latent_v,
        latent_p,
    )


def solution(mesh):
    return jax.shard_map(
        local,
        mesh=mesh,
        in_specs=(
            P(None, "opt", "seq", None),
            P(None, "opt", "seq"),
            P(None, "opt"),
            P(None, "opt", "seq", None),
            P(),
            P(),
            P(),
            P("opt", None),
            P("opt", None),
            P("opt", None),
            P("opt", None),
            P("opt", None),
            P("opt", None),
            P("opt", None),
            P("opt", None),
            P("opt", None),
            P("opt", None),
            P("opt", None),
            P("opt", None),
            P(),
            P(),
            P(),
            P(),
            P(),
            P(),
        ),
        out_specs=(
            P(None, "opt", "seq", None),
            P(None, "opt", "seq", None),
            P("opt", None),
            P("opt", None),
            P("opt", None),
            P("opt", None),
            P("opt", None),
            P("opt", None),
            P("opt", None),
            P("opt", None),
            P("opt", None),
            P("opt", None),
            P("opt", None),
            P("opt", None),
            P(),
            P(),
            P(),
            P(),
            P(),
            P(),
            P(),
            P(),
            P(),
        ),
        check_vma=False,
    )
```

```python
import functools
import types

import jax
import jax.numpy as jnp
from jax import lax
from jax.experimental import pallas as pl
from jax.experimental.pallas import tpu as pltpu
from jax.sharding import PartitionSpec as P

D_LAT = 1280
HEADS = 8
HEAD_DIM = 96
E_IN = 768
STEP = 10
OUT_FAN = 4
TILE = 256
PARTS = 4
ORDER = (4, 5, 3, 0, 1, 2)
VMEM_LIMIT = 60 * 2**20
MESH = pl.DeviceIdType.MESH


highest = lax.Precision.HIGHEST
coef_one = 3.4445
coef_two = -4.775
coef_three = 2.0315


def layer_norm(values, scale_vec, offset):
    center = jnp.mean(values, axis=-1, keepdims=True)
    shifted = values - center
    inverse = lax.rsqrt(jnp.mean(shifted * shifted, axis=-1, keepdims=True) + 1e-05)
    normal_hat = shifted * inverse
    return (normal_hat * scale_vec + offset, normal_hat, inverse)


def norm_back(grad_out, normal_hat, inverse, scale_vec):
    scaled = grad_out * scale_vec
    return inverse * (
        scaled
        - jnp.mean(scaled, axis=-1, keepdims=True)
        - normal_hat * jnp.mean(scaled * normal_hat, axis=-1, keepdims=True)
    )


def exact_gelu(values):
    return jax.nn.gelu(values, approximate=False)


def masked_scores(query_heads, key_heads, usable, score_scale):
    scores = (
        jnp.einsum("nhd,bshd->bhns", query_heads, key_heads, preferred_element_type=jnp.float32)
        * score_scale
    )
    return jnp.where(usable[:, None, None, :], scores, -1e30)


def newton_body(rows_ref, out_ref, wide, low, gram, poly, total):
    count, side = rows_ref.shape
    row_tiles, side_tiles = count // TILE, side // TILE
    total[0] = 0.0

    def add_squares(tile, carry):
        block = rows_ref[pl.ds(tile * TILE, TILE), :].astype(jnp.float32)
        total[0] = total[0] + jnp.sum(block * block)
        return carry

    lax.fori_loop(0, row_tiles, add_squares, 0)
    scale = 1.0 / (jnp.sqrt(jnp.full((1, 1), total[0], jnp.float32)) + 1e-07)

    def normalise(tile, carry):
        block = rows_ref[pl.ds(tile * TILE, TILE), :].astype(jnp.float32) * scale
        wide[pl.ds(tile * TILE, TILE), :] = block
        low[pl.ds(tile * TILE, TILE), :] = block.astype(jnp.bfloat16)
        return carry

    lax.fori_loop(0, row_tiles, normalise, 0)

    def sweep(index, carry):
        for i in range(side_tiles):
            own = slice(i * TILE, (i + 1) * TILE)
            for j in range(i, side_tiles):
                other = slice(j * TILE, (j + 1) * TILE)
                block = lax.dot_general(
                    low[:, own],
                    low[:, other],
                    (((0,), (0,)), ((), ())),
                    preferred_element_type=jnp.float32,
                )
                gram[own, other] = block.astype(jnp.bfloat16)
                if j > i:
                    gram[other, own] = block.T.astype(jnp.bfloat16)
        for i in range(side_tiles):
            own = slice(i * TILE, (i + 1) * TILE)
            block = coef_three * jnp.dot(
                gram[own, :], gram[:, i * TILE :], preferred_element_type=jnp.float32
            ) + coef_two * gram[own, i * TILE :].astype(jnp.float32)
            poly[own, i * TILE :] = block.astype(jnp.bfloat16)
            for j in range(i + 1, side_tiles):
                part = block[:, (j - i) * TILE : (j - i + 1) * TILE]
                poly[j * TILE : (j + 1) * TILE, own] = part.T.astype(jnp.bfloat16)

        def update(tile, inner):
            rows = pl.ds(tile * TILE, TILE)
            block = coef_one * wide[rows, :] + jnp.dot(
                low[rows, :], poly[...], preferred_element_type=jnp.float32
            )
            wide[rows, :] = block
            low[rows, :] = block.astype(jnp.bfloat16)
            return inner

        lax.fori_loop(0, row_tiles, update, 0)
        return carry

    lax.fori_loop(0, 5, sweep, 0)
    out_ref[...] = low[...]


def newton(rows):
    shape = rows.shape
    return pl.pallas_call(
        newton_body,
        out_shape=jax.ShapeDtypeStruct(shape, jnp.bfloat16),
        in_specs=[pl.BlockSpec(memory_space=pltpu.VMEM)],
        out_specs=pl.BlockSpec(memory_space=pltpu.VMEM),
        scratch_shapes=[
            pltpu.VMEM(shape, jnp.float32),
            pltpu.VMEM(shape, jnp.bfloat16),
            pltpu.VMEM((shape[1], shape[1]), jnp.bfloat16),
            pltpu.VMEM((shape[1], shape[1]), jnp.bfloat16),
            pltpu.SMEM((1,), jnp.float32),
        ],
        compiler_params=pltpu.CompilerParams(vmem_limit_bytes=60 * 2**20),
        name="newton",
    )(rows)


CORE, X, Y, Z0, Z1 = range(5)
LEAD, ROWS, COLS = range(3)


def partners(seq, opt):
    bits = (opt % 2, opt // 2, seq % 2, (seq // 2) % 2, seq // 4)
    steps = ((0, 1), (0, 2), (1, 0), (2, 0), (4, 0))
    targets = [
        (seq + (1 - 2 * bit) * along_seq, opt + (1 - 2 * bit) * along_opt)
        for bit, (along_seq, along_opt) in zip(bits, steps)
    ]
    return bits, targets


def greet(targets):
    barrier = pltpu.get_barrier_semaphore()
    for target in targets:
        pl.semaphore_signal(barrier, inc=1, device_id=target, device_id_type=MESH)
    pl.semaphore_wait(barrier, len(targets))


class Courier:
    def __init__(self, send_sem, recv_sem):
        self.send_sem, self.recv_sem, self.started = send_sem, recv_sem, []

    def send(self, source, target_ref, device):
        index = len(self.started)
        copy = pltpu.make_async_remote_copy(
            src_ref=source,
            dst_ref=target_ref,
            send_sem=self.send_sem.at[index],
            recv_sem=self.recv_sem.at[index],
            device_id=device,
            device_id_type=MESH,
        )
        copy.start()
        self.started.append(copy)
        return copy

    def finish(self):
        for copy in self.started:
            copy.wait_send()


class Loader:
    def __init__(self, sem):
        self.sem, self.count = sem, 0

    def start(self, source, target):
        copy = pltpu.make_async_copy(source, target, self.sem.at[self.count])
        self.count += 1
        copy.start()
        return copy


def rows_at(start, count, unit=16):
    return pl.ds(pl.multiple_of(start, unit), count)


def lanes_at(start, count):
    return pl.ds(pl.multiple_of(start, 128), count)


def dot_nn(left, right):
    return jnp.dot(left, right, preferred_element_type=jnp.float32)


def dot_nt(left, right):
    return lax.dot_general(
        left, right, (((1,), (1,)), ((), ())), preferred_element_type=jnp.float32
    )


def dot_tn(left, right):
    return lax.dot_general(
        left, right, (((0,), (0,)), ((), ())), preferred_element_type=jnp.float32
    )


def named(keys, refs):
    return types.SimpleNamespace(**dict(zip(keys, refs)))


def low(values):
    return values.astype(jnp.bfloat16)


def wide(values):
    return values.astype(jnp.float32)


def head_lanes(first, shape):
    row = lax.broadcasted_iota(jnp.int32, shape, 0) - first
    column = lax.broadcasted_iota(jnp.int32, shape, 1)
    inside = (row >= 0) & (row < HEADS)
    inside &= (column >= row * HEAD_DIM) & (column < (row + 1) * HEAD_DIM)
    return inside.astype(jnp.float32)


def pass_body(keys, *refs):
    r = named(keys, refs)
    seq, opt = lax.axis_index("seq"), lax.axis_index("opt")
    bits, targets = partners(seq, opt)
    core, y = bits[CORE], bits[Y]
    opt_x = targets[X][1]
    ring = [((seq + step) % 8, opt) for step in range(1, 8)]
    micro, span = r.usable.shape[0], r.usable.shape[2]
    width = r.in_low.shape[1]
    lat_count, width_lat = r.latents.shape
    own = lat_count // 8
    scale = HEAD_DIM ** (-0.5)
    load = Loader(r.local)
    loads = [
        load.start(source, target)
        for source, target in (
            (r.w_key, r.f_key),
            (r.w_value, r.f_value),
            (r.w_query, r.f_query),
            (r.w_out, r.f_out),
            (r.w_up, r.f_up),
            (r.w_down, r.f_down),
        )
    ]
    greet([targets[CORE], targets[X], *ring])
    courier = Courier(r.send, r.recv)

    def begin(full, rows):
        block = full.at[rows_at(opt * rows, rows)]
        half = full.at[rows_at(opt * rows + y * (rows // 2), rows // 2)]
        return [
            courier.send(half, half, targets[X]),
            courier.send(block, block, targets[CORE]),
        ]

    def relay(full, rows, state):
        state[0].wait_recv()
        half = full.at[rows_at(opt_x * rows + y * (rows // 2), rows // 2)]
        state.append(courier.send(half, half, targets[Y]))
        state.append(courier.send(half, half, targets[CORE]))

    def relay_more(full, rows, state):
        state[2].wait_recv()
        half = full.at[rows_at(opt_x * rows + (1 - y) * (rows // 2), rows // 2)]
        state.append(courier.send(half, half, targets[CORE]))

    def complete(state):
        for index in (1, 3, 4):
            state[index].wait_recv()

    def place(full, source):
        rows = source.shape[0]

        def body(step, carry):
            at = rows_at(step * 32, 32)
            full[rows_at(opt * rows + step * 32, 32), :] = low(source[at, :])
            return carry

        lax.fori_loop(0, rows // 32, body, 0)
        return begin(full, rows)

    key_rows = r.f_key.shape[0]
    loads[0].wait()
    loads[1].wait()

    def place_pair(step, carry):
        at = rows_at(opt * key_rows + step * 32, 32)
        source = rows_at(step * 32, 32)
        r.pair_full[at, :width] = low(r.f_key[source, :])
        r.pair_full[at, width:] = low(r.f_value[source, :])
        return carry

    lax.fori_loop(0, key_rows // 32, place_pair, 0)
    pair_state = begin(r.pair_full, key_rows)

    def norm(values):
        shifted = values - jnp.mean(values, axis=-1, keepdims=True)
        inverse = lax.rsqrt(jnp.mean(shifted * shifted, axis=-1, keepdims=True) + 1e-05)
        return shifted * inverse, inverse

    def norm_in(step, carry):
        at = rows_at(step * 64, 64)
        hat, inverse = norm(wide(r.tokens[at, :]))
        r.in_hat[at, :] = hat
        r.in_inv[at, :] = inverse
        r.in_low[at, :] = low(hat * r.in_vectors[0:1, :] + r.in_vectors[1:2, :])
        return carry

    lax.fori_loop(0, r.in_low.shape[0] // 64, norm_in, 0)
    loads[2].wait()
    query_state = place(r.query_full, r.f_query)

    def norm_lat(step, carry):
        at = rows_at(step * 32, 32)
        hat, _ = norm(r.latents[at, :])
        r.lat_low[at, :] = low(hat * r.lat_vectors[0:1, :] + r.lat_vectors[1:2, :])
        return carry

    lax.fori_loop(0, lat_count // 32, norm_lat, 0)
    query_rows, out_rows, up_rows = (
        r.f_query.shape[0],
        r.f_out.shape[0],
        r.f_up.shape[0],
    )
    relay(r.pair_full, key_rows, pair_state)
    relay_more(r.pair_full, key_rows, pair_state)
    loads[3].wait()
    out_state = place(r.out_full, r.f_out)
    complete(pair_state)

    def project(step, carry):
        at = rows_at(step * 128, 128)
        r.pairs[at, :] = low(dot_nn(r.in_low[at, :], r.pair_full[...]))
        return carry

    lax.fori_loop(0, r.in_low.shape[0] // 128, project, 0)
    relay(r.query_full, query_rows, query_state)
    relay_more(r.query_full, query_rows, query_state)
    loads[4].wait()
    up_state = place(r.up_full, r.f_up)
    complete(query_state)

    def project_query(step, carry):
        at = rows_at(step * 128, 128)
        r.queries[at, :] = low(dot_nn(r.lat_low[at, :], r.query_full[...]))
        return carry

    lax.fori_loop(0, lat_count // 128, project_query, 0)

    to_owner = []
    for m in range(micro):
        at = slice(m * span, (m + 1) * span)
        usable = r.usable[m] > 0.5
        for h in range(HEADS):
            ch = slice(h * HEAD_DIM, (h + 1) * HEAD_DIM)
            ch_v = slice(width + h * HEAD_DIM, width + (h + 1) * HEAD_DIM)
            masked = jnp.where(
                usable, dot_nt(r.queries[:, ch], r.pairs[at, ch]) * scale, -1e30
            )
            top = jnp.max(masked, axis=1, keepdims=True)
            weights = jnp.exp(masked - top)
            sums = jnp.sum(weights, axis=1, keepdims=True)
            r.weights[m * HEADS + h] = weights
            lane = m * HEADS + h
            r.top[:, lane : lane + 1] = top
            r.lse[:, lane : lane + 1] = top + jnp.log(sums)
            r.part[m, :, ch] = low(dot_nn(low(weights), r.pairs[at, ch_v]) / sums)
        for target in ring:
            rows = rows_at(target[0] * own, own)
            to_owner.append(
                courier.send(r.part.at[m, rows], r.part_in.at[seq, m], target)
            )
        if m == 0:
            relay(r.out_full, out_rows, out_state)
            relay_more(r.out_full, out_rows, out_state)
            loads[5].wait()
            down_state = place(r.down_full, r.f_down)
    for target in ring:
        rows = rows_at(target[0] * own, own)
        to_owner.append(courier.send(r.lse.at[rows], r.lse_in.at[seq], target))
    mine = rows_at(seq * own, own)
    r.part_in[seq] = r.part[:, mine, :]
    r.lse_in[seq] = r.lse[mine, :]
    relay(r.up_full, up_rows, up_state)
    relay_more(r.up_full, up_rows, up_state)
    relay(r.down_full, up_rows, down_state)
    relay_more(r.down_full, up_rows, down_state)
    for copy in to_owner:
        copy.wait_recv()

    peak = r.lse_in[0]
    for peer in range(1, 8):
        peak = jnp.maximum(peak, r.lse_in[peer])
    total = jnp.exp(r.lse_in[0] - peak)
    for peer in range(1, 8):
        total = total + jnp.exp(r.lse_in[peer] - peak)
    lse_all = peak + jnp.log(total)
    spread_heads = [head_lanes(m * HEADS, (128, width)) for m in range(micro)]
    collect_heads = [head_lanes((micro + m) * HEADS, (128, width)) for m in range(micro)]
    for m in range(micro):
        rows = slice(m * own, (m + 1) * own)
        for peer in range(8):
            share = jnp.dot(
                jnp.exp(r.lse_in[peer] - lse_all),
                spread_heads[m],
                precision=highest,
                preferred_element_type=jnp.float32,
            ) * wide(r.part_in[peer, m])
            r.attended[rows, :] = share if peer == 0 else r.attended[rows, :] + share
    local_rows = rows_at(core * (micro * own), micro * own)
    att_low = low(r.attended[...])
    r.x_att[local_rows, :] = att_low
    back_rows = r.cotangent[...]
    r.x_cot[local_rows, :] = back_rows
    complete(out_state)
    own_latents = jnp.concatenate([r.latents[mine, :]] * micro, axis=0)
    r.hidden[...] = own_latents + dot_nn(att_low, r.out_full[...])
    mlp_hat, mlp_inv = norm(r.hidden[...])
    r.mlp_hat[...] = mlp_hat
    mlp_low = low(mlp_hat * r.lat_vectors[2:3, :] + r.lat_vectors[3:4, :])
    r.x_mlp[local_rows, :] = mlp_low
    complete(up_state)
    pre_act = dot_nn(mlp_low, r.up_full[...]) + r.lat_vectors[4:5, :]
    cdf = 0.5 * (1.0 + lax.erf(pre_act * 0.7071067811865476))
    act_low = low(pre_act * cdf)
    r.slope[...] = cdf + pre_act * jnp.exp(-0.5 * pre_act * pre_act) * 0.3989422804014327
    r.x_act[local_rows, :] = act_low
    complete(down_state)
    grad_pre = low(dot_nt(back_rows, r.down_full[...]) * r.slope[...])
    r.x_pre[local_rows, :] = grad_pre
    grad_mlp = dot_nt(grad_pre, r.up_full[...])
    mlp_hat = r.mlp_hat[...]
    r.vectors[...] = jnp.zeros_like(r.vectors)
    r.vectors[0:1, :] = jnp.sum(grad_mlp * mlp_hat, axis=0, keepdims=True)
    r.vectors[1:2, :] = jnp.sum(grad_mlp, axis=0, keepdims=True)
    r.vectors[2:3, :] = jnp.sum(wide(grad_pre), axis=0, keepdims=True)
    r.vectors[3:4, :] = jnp.sum(wide(back_rows), axis=0, keepdims=True)
    scaled = grad_mlp * r.lat_vectors[2:3, :]
    grad_hidden = wide(back_rows) + mlp_inv * (
        scaled
        - jnp.mean(scaled, axis=-1, keepdims=True)
        - mlp_hat * jnp.mean(scaled * mlp_hat, axis=-1, keepdims=True)
    )
    rest = grad_hidden[:own]
    for m in range(1, micro):
        rest = rest + grad_hidden[m * own : (m + 1) * own]
    r.rest[...] = low(rest)
    grad_branch = low(grad_hidden)
    r.x_branch[local_rows, :] = grad_branch
    grad_own = low(dot_nt(grad_branch, r.out_full[...]))
    products = wide(grad_own) * r.attended[...]
    back = jnp.where(
        lax.broadcasted_iota(jnp.int32, lse_all.shape, 1) < micro * HEADS, lse_all, 0.0
    )
    for m in range(micro):
        rows = slice(m * own, (m + 1) * own)
        r.grad_att[m, mine, :] = grad_own[rows]
        back = back + lax.dot_general(
            products[rows],
            collect_heads[m],
            (((1,), (1,)), ((), ())),
            precision=highest,
            preferred_element_type=jnp.float32,
        )
    r.back[mine, :] = back
    returns = []
    for target in ring:
        for view in (r.grad_att.at[:, mine], r.back.at[mine]):
            returns.append(courier.send(view, view, target))
    chip = []
    for array in (r.x_act, r.x_cot, r.x_mlp, r.x_pre, r.x_att, r.x_branch):
        view = array.at[local_rows]
        chip.append(courier.send(view, view, targets[CORE]))
    r.block_out[...] = low(
        r.hidden[...] + dot_nn(act_low, r.down_full[...]) + r.lat_vectors[5:6, :]
    )
    for copy in chip:
        copy.wait_recv()
    half = lanes_at(core * (width_lat // 2), width_lat // 2)
    for target, left, right in (
        (r.grad_down, r.x_act, r.x_cot),
        (r.grad_up, r.x_mlp, r.x_pre),
        (r.grad_out, r.x_att, r.x_branch),
    ):
        for tile in range(left.shape[1] // TILE):
            cols = slice(tile * TILE, (tile + 1) * TILE)
            target[cols, :] = low(dot_tn(left[:, cols], right[:, half]))
    for copy in returns:
        copy.wait_recv()

    for h in range(HEADS):
        ch = slice(h * HEAD_DIM, (h + 1) * HEAD_DIM)
        ch_v = slice(width + h * HEAD_DIM, width + (h + 1) * HEAD_DIM)
        grad_query = None
        for m in range(micro):
            at = slice(m * span, (m + 1) * span)
            lane = m * HEADS + h
            lane_in = (micro + m) * HEADS + h
            prob = r.weights[lane] * jnp.exp(
                r.top[:, lane : lane + 1] - r.back[:, lane : lane + 1]
            )
            grad_att = r.grad_att[m, :, ch]
            grad_prob = dot_nt(grad_att, r.pairs[at, ch_v])
            grad_scores = low(prob * (grad_prob - r.back[:, lane_in : lane_in + 1]))
            part = dot_nn(grad_scores, r.pairs[at, ch])
            grad_query = part if grad_query is None else grad_query + part
            r.grad_pairs[at, ch] = low(scale * dot_tn(grad_scores, r.queries[:, ch]))
            r.grad_pairs[at, ch_v] = low(dot_tn(low(prob), grad_att))
        r.grad_query[:, ch] = low(scale * grad_query)

    part_width = width // 2

    def pair_product(target, which):
        for kind in range(2):
            cols = lanes_at(kind * width + which * part_width, part_width)
            right = r.grad_pairs[:, cols]
            for tile in range(width // TILE):
                rows = slice(tile * TILE, (tile + 1) * TILE)
                target[rows, kind * part_width : (kind + 1) * part_width] = low(
                    dot_tn(r.in_low[:, rows], right)
                )

    pair_product(r.pair_other, 1 - core)
    pair_copy = courier.send(r.pair_other, r.pair_in, targets[CORE])
    pair_product(r.grad_pair, core)
    r.in_sums[...] = jnp.zeros_like(r.in_sums)

    def norm_in_back(step, carry):
        at = rows_at(step * 64, 64)
        grad_in = dot_nt(r.grad_pairs[at, :], r.pair_full[...])
        hat = r.in_hat[at, :]
        r.in_sums[0:1, :] = r.in_sums[0:1, :] + jnp.sum(grad_in * hat, axis=0, keepdims=True)
        r.in_sums[1:2, :] = r.in_sums[1:2, :] + jnp.sum(grad_in, axis=0, keepdims=True)
        scaled = grad_in * r.in_vectors[0:1, :]
        r.input_grad[at, :] = r.in_inv[at, :] * (
            scaled
            - jnp.mean(scaled, axis=-1, keepdims=True)
            - hat * jnp.mean(scaled * hat, axis=-1, keepdims=True)
        )
        return carry

    lax.fori_loop(0, r.in_low.shape[0] // 64, norm_in_back, 0)
    r.vectors[4:6, :width] = r.in_sums[0:2, :]
    pair_copy.wait_recv()
    add_into(r.grad_pair, r.pair_in)
    courier.finish()


def run_pass(tokens, usable, cotangent, latents, lat_vectors, in_vectors, weights):
    f32, bf16 = jnp.float32, jnp.bfloat16
    w_query, w_key, w_value, w_out, w_up, w_down = weights
    operands = dict(
        tokens=tokens,
        usable=usable,
        cotangent=cotangent,
        latents=latents,
        lat_vectors=lat_vectors,
        in_vectors=in_vectors,
        w_query=w_query,
        w_key=w_key,
        w_value=w_value,
        w_out=w_out,
        w_up=w_up,
        w_down=w_down,
    )
    count, width = tokens.shape
    micro, _, span = usable.shape
    lat_count, width_lat = latents.shape
    own = lat_count // 8
    rows = micro * own
    outputs = dict(
        block_out=((rows, width_lat), bf16),
        input_grad=((count, width), f32),
        grad_up=((width_lat, width_lat // 2), bf16),
        grad_down=((width_lat, width_lat // 2), bf16),
        grad_out=((width, width_lat // 2), bf16),
        grad_pair=((width, width), bf16),
        grad_query=((lat_count, width), bf16),
        vectors=((8, width_lat), f32),
        rest=((own, width_lat), bf16),
        lat_low=((lat_count, width_lat), bf16),
        query_full=((width_lat, width), bf16),
    )
    scratch = dict(
        f_query=(w_query.shape, f32),
        f_key=(w_key.shape, f32),
        f_value=(w_value.shape, f32),
        f_out=(w_out.shape, f32),
        f_up=(w_up.shape, f32),
        f_down=(w_down.shape, f32),
        pair_full=((width, 2 * width), bf16),
        out_full=((width, width_lat), bf16),
        up_full=((width_lat, width_lat), bf16),
        down_full=((width_lat, width_lat), bf16),
        in_low=((count, width), bf16),
        in_hat=((count, width), f32),
        in_inv=((count, 1), f32),
        in_sums=((8, width), f32),
        pairs=((count, 2 * width), bf16),
        queries=((lat_count, width), bf16),
        weights=((micro * HEADS, lat_count, span), f32),
        top=((lat_count, 128), f32),
        lse=((lat_count, 128), f32),
        part=((micro, lat_count, width), bf16),
        part_in=((8, micro, own, width), bf16),
        lse_in=((8, own, 128), f32),
        attended=((rows, width), f32),
        hidden=((rows, width_lat), f32),
        mlp_hat=((rows, width_lat), f32),
        slope=((rows, width_lat), f32),
        x_att=((2 * rows, width), bf16),
        x_branch=((2 * rows, width_lat), bf16),
        x_mlp=((2 * rows, width_lat), bf16),
        x_pre=((2 * rows, width_lat), bf16),
        x_act=((2 * rows, width_lat), bf16),
        x_cot=((2 * rows, width_lat), bf16),
        grad_att=((micro, lat_count, width), bf16),
        back=((lat_count, 128), f32),
        grad_pairs=((count, 2 * width), bf16),
        pair_other=((width, width), bf16),
        pair_in=((width, width), bf16),
    )
    copies = 5 * 5 + 7 * micro + 7 + 14 + 6 + 1
    sems = dict(
        send=pltpu.SemaphoreType.DMA((copies,)),
        recv=pltpu.SemaphoreType.DMA((copies,)),
        local=pltpu.SemaphoreType.DMA((6,)),
    )
    keys = (*operands, *outputs, *scratch, *sems)
    vmem, anywhere = pl.BlockSpec(memory_space=pltpu.VMEM), pl.BlockSpec(memory_space=pl.ANY)
    results = pl.pallas_call(
        functools.partial(pass_body, keys),
        out_shape=[jax.ShapeDtypeStruct(*spec) for spec in outputs.values()],
        in_specs=[vmem] * 6 + [anywhere] * 6,
        out_specs=[vmem] * len(outputs),
        scratch_shapes=[*(pltpu.VMEM(*spec) for spec in scratch.values()), *sems.values()],
        compiler_params=pltpu.CompilerParams(
            collective_id=2, has_side_effects=True, vmem_limit_bytes=VMEM_LIMIT
        ),
        name="pass",
    )(*operands.values())
    return named(outputs, results)


def cut(ref, kind, bit):
    if kind == LEAD:
        return ref.at[bit]
    rows, cols = ref.shape[-2:]
    lead = (slice(None),) * (len(ref.shape) - 2)
    if kind == ROWS:
        return ref.at[(*lead, rows_at(bit * (rows // 2), rows // 2), slice(None))]
    return ref.at[(*lead, slice(None), lanes_at(bit * (cols // 2), cols // 2))]


def half_shape(shape, kind):
    if kind == LEAD:
        return shape[1:]
    if kind == ROWS:
        return (*shape[:-2], shape[-2] // 2, shape[-1])
    return (*shape[:-1], shape[-1] // 2)


def add_into(total, term):
    def body(step, carry):
        at = rows_at(step * 16, 16)
        for lead in range(total.shape[0]) if len(total.shape) == 3 else (None,):
            where = (at, slice(None)) if lead is None else (lead, at, slice(None))
            total[where] = low(wide(total[where]) + wide(term[where]))
        return carry

    lax.fori_loop(0, total.shape[-2] // 16, body, 0)


ROUTES = (
    ((X, LEAD), (Y, ROWS), (Z0, ROWS), (Z1, ROWS)),
    ((Y, ROWS), (X, LEAD), (Z0, ROWS), (Z1, ROWS)),
    ((Z0, ROWS), (X, LEAD), (Y, ROWS), (Z1, ROWS)),
    ((Z0, ROWS), (Y, ROWS), (X, LEAD), (Z1, ROWS)),
    ((CORE, COLS), (X, ROWS), (Y, ROWS), (Z0, ROWS), (Z1, ROWS)),
)
UP, DOWN, PAIR, OUT, QUERY = range(5)
SLOTS = (3, 0, 7, 4, 2, 5)


def combine_body(keys, shapes, *refs):
    r = named(keys, refs)
    seq, opt = lax.axis_index("seq"), lax.axis_index("opt")
    bits, targets = partners(seq, opt)
    core, z0, z1, y = bits[CORE], bits[Z0], bits[Z1], bits[Y]
    load = Loader(r.local)
    moments = (r.mom_query, r.mom_key, r.mom_value, r.mom_out, r.mom_up, r.mom_down)
    held = (r.h_query, r.h_key, r.h_value, r.h_out, r.h_up, r.h_down)
    loads = [load.start(source, target) for source, target in zip(moments, held)]
    greet(targets)
    courier = Courier(r.send, r.recv)
    sums = [r.up, r.down, r.pair, r.out, r.query]
    first = 0
    stages = []
    for shape_list in shapes:
        stages.append([getattr(r, f"s{first + index}") for index in range(len(shape_list))])
        first += len(shape_list)
    pending = {}

    def give(which, stage):
        axis, kind = ROUTES[which][stage]
        pending[which] = courier.send(
            cut(sums[which], kind, 1 - bits[axis]), stages[which][stage], targets[axis]
        )

    def take(which, stage):
        axis, kind = ROUTES[which][stage]
        pending[which].wait_recv()
        add_into(stages[which][stage], cut(sums[which], kind, bits[axis]))
        sums[which] = stages[which][stage]

    give(QUERY, 0)
    for which in (PAIR, OUT, UP, DOWN):
        give(which, 0)
    r.vectors_sum[...] = r.vectors[...]
    vector_copy = courier.send(r.vectors, r.vectors_in.at[0], targets[CORE])
    rest_width = r.rest.shape[1] // 2
    column = lanes_at(core * rest_width, rest_width)
    rest_copy = courier.send(
        r.rest.at[:, lanes_at((1 - core) * rest_width, rest_width)], r.rest_in.at[0], targets[CORE]
    )
    take(QUERY, 0)
    give(QUERY, 1)
    vector_copy.wait_recv()
    r.vectors_sum[...] = r.vectors_sum[...] + r.vectors_in[0]
    rest_copy.wait_recv()
    r.rest_sum[...] = low(wide(r.rest[:, column]) + wide(r.rest_in[0]))
    rest_copy = courier.send(r.rest_sum, r.rest_in.at[1], targets[X])
    for stage in range(4):
        axis = (X, Y, Z0, Z1)[stage]
        r.vectors_out[stage] = r.vectors_sum[...]
        vector_copy = courier.send(
            r.vectors_out.at[stage], r.vectors_in.at[stage + 1], targets[axis]
        )
        if stage > 0:
            rest_copy.wait_recv()
            if stage == 1:
                r.rest_all[z1, z0, y, :, column] = low(wide(r.rest_sum[...]) + wide(r.rest_in[1]))
            every = slice(None)
            lead = ((z1, z0, y), (every, z0, y), (every, every, y))[stage - 1]
            view = r.rest_all.at[(*lead, every, column)]
            rest_copy = courier.send(view, view, targets[(Z1, Z0, Y)[stage - 1]])
        for which in (QUERY, PAIR, OUT, UP, DOWN):
            own_stage = stage + 1 if which == QUERY else stage
            take(which, own_stage)
            if stage < 3:
                give(which, own_stage + 1)
        vector_copy.wait_recv()
        r.vectors_sum[...] = r.vectors_sum[...] + r.vectors_in[stage + 1]
    rest_copy.wait_recv()
    view = r.rest_all.at[:, :, :, :, column]
    rest_copy = courier.send(view, view, targets[CORE])

    rows, width = sums[QUERY].shape
    query_column = lanes_at(core * width, width)
    start = (bits[X] * 8 + y * 4 + z0 * 2 + z1) * rows
    r.query_all[rows_at(start, rows), query_column] = sums[QUERY][...]
    query_steps = (
        (Z1, 1, start),
        (Z0, 2, start - z1 * rows),
        (Y, 4, start - (z1 + z0 * 2) * rows),
        (X, 8, bits[X] * (8 * rows)),
    )
    gathered = (r.g_up, r.g_down, r.g_pair, r.g_out)
    for which in range(4):
        high, mid = (y, z0) if which in (UP, DOWN) else (z0, y)
        rows = sums[which].shape[0]
        gathered[which][rows_at((high * 4 + mid * 2 + z1) * rows, rows), :] = sums[which][...]

    def query_step(step):
        axis, count, base = query_steps[step]
        view = r.query_all.at[rows_at(base, count * sums[QUERY].shape[0]), query_column]
        return courier.send(view, view, targets[axis])

    query_copy = None
    for step in range(3):
        if step > 0:
            query_copy.wait_recv()
        query_copy = query_step(step)
        for which in (UP, DOWN, PAIR, OUT):
            first_axis, last_axis = (Y, Z0) if which in (UP, DOWN) else (Z0, Y)
            high, mid = bits[first_axis], bits[last_axis]
            rows = sums[which].shape[0]
            if step > 0:
                pending[which].wait_recv()
            base, count = ((high * 4 + mid * 2 + z1, 1), (high * 4 + mid * 2, 2), (high * 4, 4))[
                step
            ]
            view = gathered[which].at[rows_at(base * rows, count * rows)]
            pending[which] = courier.send(
                view, view, targets[(Z1, last_axis, first_axis)[step]]
            )
    full = (r.n_up, r.n_down, r.n_pair, r.n_out)
    for which in (OUT, PAIR, DOWN, UP):
        pending[which].wait_recv()
        rows, cols = gathered[which].shape
        at = lanes_at(core * cols, cols)
        pending[which] = courier.send(
            gathered[which].at[rows_at((1 - core) * (rows // 2), rows // 2)],
            full[which].at[:, at],
            targets[CORE],
        )
        full[which][:, at] = gathered[which][rows_at(core * (rows // 2), rows // 2), :]
    query_copy.wait_recv()
    query_copy = query_step(3)
    query_copy.wait_recv()
    view = r.query_all.at[:, query_column]
    query_copy = courier.send(view, view, targets[CORE])
    height, side = r.whole.shape[1:]
    clear_rows = 32

    def clear(step, carry):
        r.whole[opt, rows_at(step * clear_rows, clear_rows), :] = jnp.zeros(
            (clear_rows, side), jnp.bfloat16
        )
        return carry

    lax.fori_loop(0, height // clear_rows, clear, 0)
    for copy in loads:
        copy.wait()
    for which in range(4):
        pending[which].wait_recv()
    query_copy.wait_recv()
    part = r.g_pair.shape[1] // 2
    r.new_query[...] = 0.95 * r.h_query[...] + dot_tn(r.lat_block[...], r.query_all[...])
    for kind, (target, moment) in enumerate(((r.new_key, r.h_key), (r.new_value, r.h_value))):
        for side_core in range(2):
            cols = slice(side_core * part, (side_core + 1) * part)
            source = side_core * (2 * part) + kind * part
            target[:, cols] = 0.95 * moment[:, cols] + wide(r.n_pair[:, source : source + part])
    for target, moment, source in (
        (r.new_out, r.h_out, r.n_out),
        (r.new_up, r.h_up, r.n_up),
        (r.new_down, r.h_down, r.n_down),
    ):
        target[...] = 0.95 * moment[...] + wide(source[...])

    news = (r.new_query, r.new_key, r.new_value, r.new_out, r.new_up, r.new_down)
    for new, slot in zip(news, SLOTS):

        @pl.when(seq == slot)
        def _(new=new):
            r.whole[opt, : new.shape[0], : new.shape[1]] = low(new[...])

    own = r.whole.at[opt]
    across = courier.send(own, own, targets[X])
    beside = courier.send(own, own, targets[CORE])
    across.wait_recv()
    other = r.whole.at[targets[X][1]]
    last = courier.send(other, other, targets[CORE])
    beside.wait_recv()
    last.wait_recv()
    rest_copy.wait_recv()
    courier.finish()


def combine(done, lat_block, moments, height):
    f32, bf16 = jnp.float32, jnp.bfloat16
    mom_query, mom_key, mom_value, mom_out, mom_up, mom_down = moments
    width_lat = done.grad_up.shape[0]
    halved = [
        grad.reshape(2, grad.shape[0] // 2, grad.shape[1])
        for grad in (done.grad_up, done.grad_down, done.grad_pair, done.grad_out)
    ]
    operands = dict(
        vectors=done.vectors,
        rest=done.rest,
        lat_block=lat_block,
        up=halved[0],
        down=halved[1],
        pair=halved[2],
        out=halved[3],
        query=done.grad_query,
        mom_query=mom_query,
        mom_key=mom_key,
        mom_value=mom_value,
        mom_out=mom_out,
        mom_up=mom_up,
        mom_down=mom_down,
    )
    outputs = dict(
        new_query=(mom_query.shape, f32),
        new_key=(mom_key.shape, f32),
        new_value=(mom_value.shape, f32),
        new_out=(mom_out.shape, f32),
        new_up=(mom_up.shape, f32),
        new_down=(mom_down.shape, f32),
        query_all=(done.grad_query.shape, bf16),
        vectors_sum=(done.vectors.shape, f32),
        rest_all=((2, 2, 2, *done.rest.shape), bf16),
        whole=((4, height, width_lat), bf16),
    )
    half_rest = (done.rest.shape[0], done.rest.shape[1] // 2)
    scratch = dict(
        vectors_in=((5, *done.vectors.shape), f32),
        vectors_out=((4, *done.vectors.shape), f32),
        rest_in=((2, *half_rest), bf16),
        rest_sum=(half_rest, bf16),
        h_query=(mom_query.shape, f32),
        h_key=(mom_key.shape, f32),
        h_value=(mom_value.shape, f32),
        h_out=(mom_out.shape, f32),
        h_up=(mom_up.shape, f32),
        h_down=(mom_down.shape, f32),
        g_up=(halved[0].shape[1:], bf16),
        g_down=(halved[1].shape[1:], bf16),
        g_pair=(halved[2].shape[1:], bf16),
        g_out=(halved[3].shape[1:], bf16),
        n_up=(mom_up.shape, bf16),
        n_down=(mom_down.shape, bf16),
        n_pair=((mom_key.shape[0], 2 * mom_key.shape[1]), bf16),
        n_out=(mom_out.shape, bf16),
    )
    shapes = []
    for array, route in zip((*halved, done.grad_query), ROUTES):
        shape, chain = array.shape, []
        for _, kind in route:
            shape = half_shape(shape, kind)
            chain.append(shape)
        shapes.append(chain)
    for index, shape in enumerate(sum(shapes, [])):
        scratch[f"s{index}"] = (shape, bf16)
    copies = 64
    sems = dict(
        send=pltpu.SemaphoreType.DMA((copies,)),
        recv=pltpu.SemaphoreType.DMA((copies,)),
        local=pltpu.SemaphoreType.DMA((6,)),
    )
    keys = (*operands, *outputs, *scratch, *sems)
    vmem, anywhere = pl.BlockSpec(memory_space=pltpu.VMEM), pl.BlockSpec(memory_space=pl.ANY)
    results = pl.pallas_call(
        functools.partial(combine_body, keys, shapes),
        out_shape=[jax.ShapeDtypeStruct(*spec) for spec in outputs.values()],
        in_specs=[vmem] * 8 + [anywhere] * 6,
        out_specs=[vmem] * len(outputs),
        scratch_shapes=[*(pltpu.VMEM(*spec) for spec in scratch.values()), *sems.values()],
        compiler_params=pltpu.CompilerParams(
            collective_id=0, has_side_effects=True, vmem_limit_bytes=VMEM_LIMIT
        ),
        name="combine",
    )(*operands.values())
    return named(outputs, results)


def spread_body(result_ref, *refs):
    count = len(SLOTS)
    outs = refs[:count]
    send_sem, recv_sem, local_sem = refs[count:]
    seq, opt = lax.axis_index("seq"), lax.axis_index("opt")
    y, z = seq % 2, seq // 2
    targets = partners(seq, opt)[1]
    depth = 4
    barrier = pltpu.get_barrier_semaphore()
    pl.semaphore_signal(barrier, inc=1, device_id=targets[Y], device_id_type=MESH)
    for step in (-1, 1):

        @pl.when((z + step >= 0) & (z + step < depth))
        def _(step=step):
            pl.semaphore_signal(
                barrier, inc=1, device_id=(seq + 2 * step, opt), device_id_type=MESH
            )

    inside = (z > 0) & (z < depth - 1)

    @pl.when(inside)
    def _():
        pl.semaphore_wait(barrier, 3)

    @pl.when(jnp.logical_not(inside))
    def _():
        pl.semaphore_wait(barrier, 2)

    def copy(which, part, way):
        index = which * PARTS + part
        out = outs[which]
        rows = out.shape[0] // PARTS
        view = out.at[pl.ds(part * rows, rows)]
        return pltpu.make_async_remote_copy(
            src_ref=view,
            dst_ref=view,
            send_sem=send_sem.at[way, index],
            recv_sem=recv_sem.at[index],
            device_id=((seq + 2, opt), (seq - 2, opt), targets[Y])[way],
            device_id_type=MESH,
        )

    for which, slot in enumerate(SLOTS):
        out = outs[which]

        @pl.when(seq == slot)
        def _(out=out):
            load = pltpu.make_async_copy(
                result_ref.at[opt, pl.ds(0, out.shape[0]), pl.ds(0, out.shape[1])], out, local_sem
            )
            load.start()
            load.wait()

    def ways(which, mine):
        slot_y, slot_z = SLOTS[which] % 2, SLOTS[which] // 2
        turn = (y == slot_y) & ((z == slot_z) if mine else (z != slot_z))
        return (
            turn & (z >= slot_z) & (z < depth - 1),
            turn & (z <= slot_z) & (z > 0),
            turn,
        )

    for mine in (True, False):
        for part in range(PARTS):
            for which in ORDER:
                on = ways(which, mine)
                if not mine:

                    @pl.when(on[2])
                    def _(which=which, part=part):
                        copy(which, part, 2).wait_recv()

                for way in range(3):

                    @pl.when(on[way])
                    def _(which=which, part=part, way=way):
                        copy(which, part, way).start()

    for part in range(PARTS):
        for which in ORDER:

            @pl.when(y != SLOTS[which] % 2)
            def _(which=which, part=part):
                copy(which, part, 2).wait_recv()

    for mine in (True, False):
        for part in range(PARTS):
            for which in ORDER:
                on = ways(which, mine)
                for way in range(3):

                    @pl.when(on[way])
                    def _(which=which, part=part, way=way):
                        copy(which, part, way).wait_send()


def spread(result, shapes):
    vmem = pl.BlockSpec(memory_space=pltpu.VMEM)
    count = len(SLOTS) * PARTS
    return pl.pallas_call(
        spread_body,
        out_shape=[jax.ShapeDtypeStruct(shape, jnp.bfloat16) for shape in shapes],
        in_specs=[pl.BlockSpec(memory_space=pl.ANY)],
        out_specs=[vmem] * len(SLOTS),
        scratch_shapes=[
            pltpu.SemaphoreType.DMA((3, count)),
            pltpu.SemaphoreType.DMA((count,)),
            pltpu.SemaphoreType.DMA,
        ],
        compiler_params=pltpu.CompilerParams(
            collective_id=1, has_side_effects=True, vmem_limit_bytes=VMEM_LIMIT
        ),
        name="spread",
    )(result)


def adam_update(param, gradient, first, second, step_rate, decay):
    first_new = 0.9 * first + 0.1 * gradient
    second_new = 0.95 * second + 0.05 * gradient * gradient
    ratio = first_new / (1.0 - 0.9**STEP) / (jnp.sqrt(second_new / (1.0 - 0.95**STEP)) + 1e-08)
    return (first_new, second_new, param - step_rate * (ratio + decay * param))


def local_small(
    inputs,
    key_mask,
    lengths,
    cotangent,
    latents,
    lat_vectors,
    in_vectors,
    w_query,
    w_key,
    w_value,
    w_out,
    w_up,
    w_down,
    mom_query,
    mom_key,
    mom_value,
    mom_out,
    mom_up,
    mom_down,
    lat_first,
    lat_second,
    in_first,
    in_second,
    latent_first,
    latent_second,
):
    seq_index, opt_index = lax.axis_index("seq"), lax.axis_index("opt")
    micro_count, _, span, width_in = inputs.shape
    lat_count, width_lat = latents.shape
    positions = seq_index * span + jnp.arange(span, dtype=jnp.int32)
    usable = (positions < lengths[:, :, None]) & ((key_mask == 1) | (positions == 0))
    masters = (w_query, w_key, w_value, w_out, w_up, w_down)
    moments = (mom_query, mom_key, mom_value, mom_out, mom_up, mom_down)
    done = run_pass(
        inputs.reshape(-1, width_in),
        usable.astype(jnp.float32),
        cotangent.reshape(-1, width_lat),
        latents,
        lat_vectors,
        in_vectors,
        masters,
    )
    height = w_up.shape[0]
    summed = combine(
        done,
        lax.dynamic_slice_in_dim(done.lat_low, opt_index * height, height, 1),
        moments,
        height,
    )
    moments_new = (
        summed.new_query,
        summed.new_key,
        summed.new_value,
        summed.new_out,
        summed.new_up,
        summed.new_down,
    )
    own_result = newton(summed.whole.reshape(-1, width_lat))
    currents = spread(
        own_result.reshape(summed.whole.shape), [moment.shape for moment in moments]
    )
    new_masters = update_masters(masters, currents)
    _, lat_hat, lat_inv = layer_norm(latents, lat_vectors[0], lat_vectors[1])
    grad_lat = jnp.dot(summed.query_all, done.query_full.T, preferred_element_type=jnp.float32)
    lat_vec_sum = jnp.concatenate(
        [
            jnp.sum(grad_lat * lat_hat, axis=0)[None],
            jnp.sum(grad_lat, axis=0)[None],
            summed.vectors_sum[:4],
        ]
    )
    in_vec_sum = summed.vectors_sum[4:6, :width_in]
    latent_sum = norm_back(grad_lat, lat_hat, lat_inv, lat_vectors[0]) + summed.rest_all.reshape(
        latents.shape
    ).astype(jnp.float32)
    return (
        done.block_out.reshape(cotangent.shape),
        done.input_grad.reshape(inputs.shape),
        *moments_new,
        *new_masters,
        *adam_update(lat_vectors, lat_vec_sum, lat_first, lat_second, 0.6, 0.0),
        *adam_update(in_vectors, in_vec_sum, in_first, in_second, 0.6, 0.0),
        *adam_update(latents, latent_sum, latent_first, latent_second, 1.0, 0.1),
    )


def update_masters(masters, currents):
    fans = (D_LAT, E_IN, E_IN, OUT_FAN, D_LAT, D_LAT)
    sides = (D_LAT, E_IN, E_IN, D_LAT, D_LAT, D_LAT)
    new_masters = []
    for master, current, fan_in, long_side in zip(masters, currents, fans, sides):
        step_rate = fan_in ** (-0.5)
        new_masters.append(
            (1.0 - 0.1 * step_rate) * master
            - step_rate * long_side**0.5 * current.astype(jnp.float32)
        )
    return new_masters


def local(
    inputs,
    key_mask,
    lengths,
    cotangent,
    latents,
    lat_vectors,
    in_vectors,
    w_query,
    w_key,
    w_value,
    w_out,
    w_up,
    w_down,
    mom_query,
    mom_key,
    mom_value,
    mom_out,
    mom_up,
    mom_down,
    lat_first,
    lat_second,
    in_first,
    in_second,
    latent_first,
    latent_second,
):
    query_low, key_low, value_low, out_low, up_low, down_low = (
        lax.all_gather(w_query.astype(jnp.bfloat16), "opt", axis=0, tiled=True),
        lax.all_gather(w_key.astype(jnp.bfloat16), "opt", axis=0, tiled=True),
        lax.all_gather(w_value.astype(jnp.bfloat16), "opt", axis=0, tiled=True),
        lax.all_gather(w_out.astype(jnp.bfloat16), "opt", axis=0, tiled=True),
        lax.all_gather(w_up.astype(jnp.bfloat16), "opt", axis=0, tiled=True),
        lax.all_gather(w_down.astype(jnp.bfloat16), "opt", axis=0, tiled=True),
    )
    pair_low = jnp.concatenate([key_low, value_low], axis=1)
    seq_index = lax.axis_index("seq")
    seq_size = lax.axis_size("seq")
    opt_index = lax.axis_index("opt")
    opt_size = lax.axis_size("opt")
    micro_count, doc_local, span, width_in = inputs.shape
    lat_count, width_lat = latents.shape
    own_rows = lat_count // seq_size
    row_start = seq_index * own_rows
    score_scale = HEAD_DIM ** (-0.5)
    lat_normed, lat_hat, lat_inv = layer_norm(latents, lat_vectors[0], lat_vectors[1])
    lat_low = lat_normed.astype(jnp.bfloat16)
    query_rows = jnp.dot(lat_low, query_low, preferred_element_type=jnp.float32).astype(
        jnp.bfloat16
    )
    query_heads = query_rows.reshape(lat_count, HEADS, HEAD_DIM)
    own_latents = lax.dynamic_slice_in_dim(latents, row_start, own_rows, 0)
    positions = seq_index * span + jnp.arange(span, dtype=jnp.int32)
    grad_query_rows = jnp.zeros((lat_count, width_in), jnp.float32)
    grad_pair = jnp.zeros((width_in, 2 * width_in), jnp.float32)
    grad_out_w = jnp.zeros((width_in, width_lat), jnp.float32)
    grad_up_w = jnp.zeros((width_lat, width_lat), jnp.float32)
    grad_down_w = jnp.zeros((width_lat, width_lat), jnp.float32)
    mlp_gain = jnp.zeros((width_lat,), jnp.float32)
    mlp_shift = jnp.zeros((width_lat,), jnp.float32)
    bias_up = jnp.zeros((width_lat,), jnp.float32)
    bias_down = jnp.zeros((width_lat,), jnp.float32)
    in_gain = jnp.zeros((width_in,), jnp.float32)
    in_shift = jnp.zeros((width_in,), jnp.float32)
    latent_rest = jnp.zeros((own_rows, width_lat), jnp.float32)
    block_parts = []
    input_parts = []
    for micro_step in range(micro_count):
        tokens = inputs[micro_step]
        usable = (positions[None, :] < lengths[micro_step][:, None]) & (
            (key_mask[micro_step] == 1) | (positions[None, :] == 0)
        )
        in_normed, in_hat, in_inv = layer_norm(
            tokens.astype(jnp.float32), in_vectors[0], in_vectors[1]
        )
        in_low = in_normed.astype(jnp.bfloat16)
        pair_rows = jnp.einsum(
            "bse,ef->bsf", in_low, pair_low, preferred_element_type=jnp.float32
        ).astype(jnp.bfloat16)
        key_heads = pair_rows[:, :, :width_in].reshape(doc_local, span, HEADS, HEAD_DIM)
        value_heads = pair_rows[:, :, width_in:].reshape(doc_local, span, HEADS, HEAD_DIM)
        masked = masked_scores(query_heads, key_heads, usable, score_scale)
        row_max = lax.pmax(jnp.max(masked, axis=-1), "seq")
        weights = jnp.exp(masked - row_max[..., None])
        weights_low = weights.astype(jnp.bfloat16)
        summed, row_sum = (
            lax.psum(
                jnp.einsum(
                    "bhns,bshd->bnhd", weights_low, value_heads, preferred_element_type=jnp.float32
                ).astype(jnp.bfloat16),
                "seq",
            ).astype(jnp.float32),
            lax.psum(jnp.sum(weights, axis=-1).astype(jnp.bfloat16), "seq").astype(jnp.float32),
        )
        sum_heads = jnp.transpose(row_sum, (0, 2, 1))[..., None]
        attended = summed / sum_heads
        own_att = (
            lax.dynamic_slice_in_dim(attended, row_start, own_rows, 1)
            .reshape(doc_local, own_rows, width_in)
            .astype(jnp.bfloat16)
        )
        hidden = own_latents[None] + jnp.einsum(
            "bne,ef->bnf", own_att, out_low, preferred_element_type=jnp.float32
        )
        mlp_normed, mlp_hat, mlp_inv = layer_norm(hidden, lat_vectors[2], lat_vectors[3])
        mlp_low = mlp_normed.astype(jnp.bfloat16)
        pre_act = (
            jnp.einsum("bnf,fg->bng", mlp_low, up_low, preferred_element_type=jnp.float32)
            + lat_vectors[4]
        )
        activated, gelu_pull = jax.vjp(exact_gelu, pre_act)
        act_low = activated.astype(jnp.bfloat16)
        block_parts.append(
            (
                hidden
                + jnp.einsum("bng,gk->bnk", act_low, down_low, preferred_element_type=jnp.float32)
                + lat_vectors[5]
            ).astype(jnp.bfloat16)
        )
        back_rows = cotangent[micro_step]
        grad_down_w = grad_down_w + jnp.einsum(
            "bng,bnk->gk", act_low, back_rows, preferred_element_type=jnp.float32
        )
        bias_down = bias_down + jnp.sum(back_rows.astype(jnp.float32), axis=(0, 1))
        grad_act = jnp.einsum(
            "bnk,gk->bng", back_rows, down_low, preferred_element_type=jnp.float32
        )
        grad_pre = gelu_pull(grad_act)[0].astype(jnp.bfloat16)
        grad_up_w = grad_up_w + jnp.einsum(
            "bnf,bng->fg", mlp_low, grad_pre, preferred_element_type=jnp.float32
        )
        bias_up = bias_up + jnp.sum(grad_pre.astype(jnp.float32), axis=(0, 1))
        grad_mlp = jnp.einsum("bng,fg->bnf", grad_pre, up_low, preferred_element_type=jnp.float32)
        mlp_gain = mlp_gain + jnp.sum(grad_mlp * mlp_hat, axis=(0, 1))
        mlp_shift = mlp_shift + jnp.sum(grad_mlp, axis=(0, 1))
        grad_hidden = back_rows.astype(jnp.float32) + norm_back(
            grad_mlp, mlp_hat, mlp_inv, lat_vectors[2]
        )
        latent_rest = latent_rest + jnp.sum(grad_hidden, axis=0)
        grad_branch = grad_hidden.astype(jnp.bfloat16)
        grad_out_w = grad_out_w + jnp.einsum(
            "bne,bnf->ef", own_att, grad_branch, preferred_element_type=jnp.float32
        )
        grad_own = jnp.einsum(
            "bnf,ef->bne", grad_branch, out_low, preferred_element_type=jnp.float32
        ).astype(jnp.bfloat16)
        grad_att = (
            lax.all_gather(grad_own, "seq", axis=1, tiled=True)
            .astype(jnp.float32)
            .reshape(doc_local, lat_count, HEADS, HEAD_DIM)
        )
        grad_summed = (grad_att / sum_heads).astype(jnp.bfloat16)
        inner = jnp.transpose(jnp.sum(grad_att * attended, axis=-1) / sum_heads[..., 0], (0, 2, 1))
        grad_prob = jnp.einsum(
            "bnhd,bshd->bhns", grad_summed, value_heads, preferred_element_type=jnp.float32
        )
        grad_scores = (weights * (grad_prob - inner[..., None])).astype(jnp.bfloat16)
        grad_query_rows = grad_query_rows + score_scale * jnp.einsum(
            "bhns,bshd->nhd", grad_scores, key_heads, preferred_element_type=jnp.float32
        ).reshape(lat_count, width_in)
        grad_keys = (
            score_scale
            * jnp.einsum(
                "bhns,nhd->bshd", grad_scores, query_heads, preferred_element_type=jnp.float32
            )
        ).astype(jnp.bfloat16)
        grad_values = jnp.einsum(
            "bhns,bnhd->bshd", weights_low, grad_summed, preferred_element_type=jnp.float32
        ).astype(jnp.bfloat16)
        grad_pairs = jnp.concatenate(
            [
                grad_keys.reshape(doc_local, span, width_in),
                grad_values.reshape(doc_local, span, width_in),
            ],
            axis=-1,
        )
        grad_pair = grad_pair + jnp.einsum(
            "bse,bsf->ef", in_low, grad_pairs, preferred_element_type=jnp.float32
        )
        grad_in = jnp.einsum(
            "bsf,ef->bse", grad_pairs, pair_low, preferred_element_type=jnp.float32
        )
        in_gain = in_gain + jnp.sum(grad_in * in_hat, axis=(0, 1))
        in_shift = in_shift + jnp.sum(grad_in, axis=(0, 1))
        input_parts.append(norm_back(grad_in, in_hat, in_inv, in_vectors[0]))
    grad_query_w = jnp.matmul(lat_low.astype(jnp.float32).T, grad_query_rows, precision=highest)
    grad_lat = jnp.matmul(grad_query_rows, query_low.astype(jnp.float32).T, precision=highest)
    zero_index = jnp.zeros((), jnp.int32)
    latent_grad = norm_back(grad_lat, lat_hat, lat_inv, lat_vectors[0]) + lax.dynamic_update_slice(
        jnp.zeros_like(latents), latent_rest, (row_start, zero_index)
    )
    lat_vec_grad = jnp.stack(
        [
            jnp.sum(grad_lat * lat_hat, axis=0),
            jnp.sum(grad_lat, axis=0),
            mlp_gain,
            mlp_shift,
            bias_up,
            bias_down,
        ]
    )
    in_vec_grad = jnp.stack([in_gain, in_shift])
    weight_grads = (
        grad_query_w,
        grad_pair[:, :width_in],
        grad_pair[:, width_in:],
        grad_out_w,
        grad_up_w,
        grad_down_w,
    )
    masters = (w_query, w_key, w_value, w_out, w_up, w_down)
    moments = (mom_query, mom_key, mom_value, mom_out, mom_up, mom_down)
    first_here = jnp.where(seq_index == 0, 0.95, 0.0)
    with_moment = []
    for gradient, moment in zip(weight_grads, moments):
        start = opt_index * moment.shape[0]
        rows = lax.dynamic_slice_in_dim(gradient, start, moment.shape[0], 0) + first_here * moment
        with_moment.append(
            lax.dynamic_update_slice(gradient, rows, (start, zero_index)).astype(jnp.bfloat16)
        )
    summed_low = lax.psum(tuple(with_moment), ("seq", "opt"))
    lat_vec_sum, in_vec_sum, latent_sum = lax.psum(
        (lat_vec_grad, in_vec_grad, latent_grad), ("seq", "opt")
    )
    moments_new = [
        lax.dynamic_slice_in_dim(summed, opt_index * moment.shape[0], moment.shape[0], 0).astype(
            jnp.float32
        )
        for summed, moment in zip(summed_low, moments)
    ]

    def padded(index):
        def pick():
            matrix = summed_low[index].T if index == 3 else summed_low[index]
            return jnp.pad(
                matrix, ((0, width_lat - matrix.shape[0]), (0, width_lat - matrix.shape[1]))
            )

        return pick

    slot = seq_index % 8
    own_matrix = lax.switch(jnp.minimum(slot, 5), [padded(index) for index in range(6)])
    own_result = newton(own_matrix)
    own_result = lax.cond(slot == 3, lambda: own_result.T, lambda: own_result)
    mine = jnp.stack(
        [
            lax.dynamic_slice_in_dim(own_result, opt_index * height, width_lat // opt_size, 0)
            for height in (width_in // opt_size, width_lat // opt_size)
        ]
    )
    is_wide = (slot == 0) | (slot >= 4)
    mine = jnp.where(is_wide, mine[1], mine[0])
    spread = lax.all_gather(mine, "seq", axis=0, tiled=False)
    currents = [
        spread[index, : moment.shape[0], : moment.shape[1]].astype(jnp.float32)
        for index, moment in enumerate(moments)
    ]
    new_masters = update_masters(masters, currents)
    lat_m, lat_v, lat_p = adam_update(lat_vectors, lat_vec_sum, lat_first, lat_second, 0.6, 0.0)
    in_m, in_v, in_p = adam_update(in_vectors, in_vec_sum, in_first, in_second, 0.6, 0.0)
    latent_m, latent_v, latent_p = adam_update(
        latents, latent_sum, latent_first, latent_second, 1.0, 0.1
    )
    block_out = jnp.stack(block_parts)
    input_grad = jnp.stack(input_parts)
    return (
        block_out,
        input_grad,
        moments_new[0],
        moments_new[1],
        moments_new[2],
        moments_new[3],
        moments_new[4],
        moments_new[5],
        new_masters[0],
        new_masters[1],
        new_masters[2],
        new_masters[3],
        new_masters[4],
        new_masters[5],
        lat_m,
        lat_v,
        lat_p,
        in_m,
        in_v,
        in_p,
        latent_m,
        latent_v,
        latent_p,
    )


def solution(mesh):
    small = (mesh.shape["seq"], mesh.shape["opt"]) == (8, 4)
    return jax.shard_map(
        local_small if small else local,
        mesh=mesh,
        in_specs=(
            P(None, "opt", "seq", None),
            P(None, "opt", "seq"),
            P(None, "opt"),
            P(None, "opt", "seq", None),
            P(),
            P(),
            P(),
            P("opt", None),
            P("opt", None),
            P("opt", None),
            P("opt", None),
            P("opt", None),
            P("opt", None),
            P("opt", None),
            P("opt", None),
            P("opt", None),
            P("opt", None),
            P("opt", None),
            P("opt", None),
            P(),
            P(),
            P(),
            P(),
            P(),
            P(),
        ),
        out_specs=(
            P(None, "opt", "seq", None),
            P(None, "opt", "seq", None),
            P("opt", None),
            P("opt", None),
            P("opt", None),
            P("opt", None),
            P("opt", None),
            P("opt", None),
            P("opt", None),
            P("opt", None),
            P("opt", None),
            P("opt", None),
            P("opt", None),
            P("opt", None),
            P(),
            P(),
            P(),
            P(),
            P(),
            P(),
            P(),
            P(),
            P(),
        ),
        check_vma=False,
    )
```

```python
import functools
import types

import jax
import jax.numpy as jnp
from jax import lax
from jax.experimental import pallas as pl
from jax.experimental.pallas import tpu as pltpu
from jax.sharding import PartitionSpec as P

D_LAT = 1280
HEADS = 8
HEAD_DIM = 96
E_IN = 768
STEP = 10
OUT_FAN = 4
TILE = 256
PARTS = 4
ORDER = (4, 5, 3, 0, 1, 2)
AHEAD = 2
POINTS = {0: (0, 0), 1: (4, 0), 2: (1, 0), 4: (0, 1), 5: (4, 1), 6: (1, 1)}
VMEM_LIMIT = 60 * 2**20
MESH = pl.DeviceIdType.MESH


highest = lax.Precision.HIGHEST
coef_one = 3.4445
coef_two = -4.775
coef_three = 2.0315


def layer_norm(values, scale_vec, offset):
    center = jnp.mean(values, axis=-1, keepdims=True)
    shifted = values - center
    inverse = lax.rsqrt(jnp.mean(shifted * shifted, axis=-1, keepdims=True) + 1e-05)
    normal_hat = shifted * inverse
    return (normal_hat * scale_vec + offset, normal_hat, inverse)


def norm_back(grad_out, normal_hat, inverse, scale_vec):
    scaled = grad_out * scale_vec
    return inverse * (
        scaled
        - jnp.mean(scaled, axis=-1, keepdims=True)
        - normal_hat * jnp.mean(scaled * normal_hat, axis=-1, keepdims=True)
    )


def exact_gelu(values):
    return jax.nn.gelu(values, approximate=False)


def masked_scores(query_heads, key_heads, usable, score_scale):
    scores = (
        jnp.einsum("nhd,bshd->bhns", query_heads, key_heads, preferred_element_type=jnp.float32)
        * score_scale
    )
    return jnp.where(usable[:, None, None, :], scores, -1e30)


def polynomial(low, gram, poly):
    side_tiles = gram.shape[0] // TILE
    for i in range(side_tiles):
        own = slice(i * TILE, (i + 1) * TILE)
        for j in range(i, side_tiles):
            other = slice(j * TILE, (j + 1) * TILE)
            block = lax.dot_general(
                low[:, own],
                low[:, other],
                (((0,), (0,)), ((), ())),
                preferred_element_type=jnp.float32,
            )
            gram[own, other] = block.astype(jnp.bfloat16)
            if j > i:
                gram[other, own] = block.T.astype(jnp.bfloat16)
    for i in range(side_tiles):
        own = slice(i * TILE, (i + 1) * TILE)
        block = coef_three * jnp.dot(
            gram[own, :], gram[:, i * TILE :], preferred_element_type=jnp.float32
        ) + coef_two * gram[own, i * TILE :].astype(jnp.float32)
        poly[own, i * TILE :] = block.astype(jnp.bfloat16)
        for j in range(i + 1, side_tiles):
            part = block[:, (j - i) * TILE : (j - i + 1) * TILE]
            poly[j * TILE : (j + 1) * TILE, own] = part.T.astype(jnp.bfloat16)


def newton_body(rows_ref, out_ref, wide, low, gram, poly, total):
    count, side = rows_ref.shape
    row_tiles = count // TILE
    total[0] = 0.0

    def add_squares(tile, carry):
        block = rows_ref[pl.ds(tile * TILE, TILE), :].astype(jnp.float32)
        total[0] = total[0] + jnp.sum(block * block)
        return carry

    lax.fori_loop(0, row_tiles, add_squares, 0)
    scale = 1.0 / (jnp.sqrt(jnp.full((1, 1), total[0], jnp.float32)) + 1e-07)

    def normalise(tile, carry):
        block = rows_ref[pl.ds(tile * TILE, TILE), :].astype(jnp.float32) * scale
        wide[pl.ds(tile * TILE, TILE), :] = block
        low[pl.ds(tile * TILE, TILE), :] = block.astype(jnp.bfloat16)
        return carry

    lax.fori_loop(0, row_tiles, normalise, 0)

    def sweep(index, carry):
        polynomial(low, gram, poly)

        def update(tile, inner):
            rows = pl.ds(tile * TILE, TILE)
            block = coef_one * wide[rows, :] + jnp.dot(
                low[rows, :], poly[...], preferred_element_type=jnp.float32
            )
            wide[rows, :] = block
            low[rows, :] = block.astype(jnp.bfloat16)
            return inner

        lax.fori_loop(0, row_tiles, update, 0)
        return carry

    lax.fori_loop(0, 5, sweep, 0)
    out_ref[...] = low[...]


def newton(rows):
    shape = rows.shape
    return pl.pallas_call(
        newton_body,
        out_shape=jax.ShapeDtypeStruct(shape, jnp.bfloat16),
        in_specs=[pl.BlockSpec(memory_space=pltpu.VMEM)],
        out_specs=pl.BlockSpec(memory_space=pltpu.VMEM),
        scratch_shapes=[
            pltpu.VMEM(shape, jnp.float32),
            pltpu.VMEM(shape, jnp.bfloat16),
            pltpu.VMEM((shape[1], shape[1]), jnp.bfloat16),
            pltpu.VMEM((shape[1], shape[1]), jnp.bfloat16),
            pltpu.SMEM((1,), jnp.float32),
        ],
        compiler_params=pltpu.CompilerParams(vmem_limit_bytes=60 * 2**20),
        name="newton",
    )(rows)


CORE, X, Y, Z0, Z1 = range(5)
LEAD, ROWS, COLS = range(3)
UP, DOWN, KEY, VALUE, OUT, QUERY = range(6)
ROUTES = (
    ((X, LEAD), (Y, ROWS), (Z0, ROWS), (Z1, ROWS)),
    ((Y, ROWS), (X, LEAD), (Z0, ROWS), (Z1, ROWS)),
    ((X, LEAD), (Y, ROWS), (Z0, ROWS), (Z1, ROWS)),
    ((Z0, ROWS), (X, LEAD), (Y, ROWS), (Z1, ROWS)),
    ((Z0, ROWS), (Y, ROWS), (X, LEAD), (Z1, ROWS)),
    ((CORE, COLS), (X, ROWS), (Y, ROWS), (Z0, ROWS), (Z1, ROWS)),
)
Y_FIRST = (UP, DOWN, KEY)
SLOTS = (3, 0, 7, 4, 2, 5)


def partners(seq, opt):
    bits = (opt % 2, opt // 2, seq % 2, (seq // 2) % 2, seq // 4)
    steps = ((0, 1), (0, 2), (1, 0), (2, 0), (4, 0))
    targets = [
        (seq + (1 - 2 * bit) * along_seq, opt + (1 - 2 * bit) * along_opt)
        for bit, (along_seq, along_opt) in zip(bits, steps)
    ]
    return bits, targets


def greet(targets):
    barrier = pltpu.get_barrier_semaphore()
    for target in targets:
        pl.semaphore_signal(barrier, inc=1, device_id=target, device_id_type=MESH)
    pl.semaphore_wait(barrier, len(targets))


class Courier:
    def __init__(self, send_sem, recv_sem):
        self.send_sem, self.recv_sem, self.started = send_sem, recv_sem, []

    def send(self, source, target_ref, device):
        index = len(self.started)
        copy = pltpu.make_async_remote_copy(
            src_ref=source,
            dst_ref=target_ref,
            send_sem=self.send_sem.at[index],
            recv_sem=self.recv_sem.at[index],
            device_id=device,
            device_id_type=MESH,
        )
        copy.start()
        self.started.append(copy)
        return copy

    def finish(self):
        for copy in self.started:
            copy.wait_send()


class Loader:
    def __init__(self, sem):
        self.sem, self.count = sem, 0

    def start(self, source, target):
        copy = pltpu.make_async_copy(source, target, self.sem.at[self.count])
        self.count += 1
        copy.start()
        return copy


def rows_at(start, count, unit=16):
    return pl.ds(pl.multiple_of(start, unit), count)


def lanes_at(start, count):
    return pl.ds(pl.multiple_of(start, 128), count)


def clear(ref):
    def body(step, carry):
        ref[rows_at(step * 32, 32), :] = jnp.zeros((32, ref.shape[1]), ref.dtype)
        return carry

    lax.fori_loop(0, ref.shape[0] // 32, body, 0)


def dot_nn(left, right):
    return jnp.dot(left, right, preferred_element_type=jnp.float32)


def dot_nt(left, right):
    return lax.dot_general(
        left, right, (((1,), (1,)), ((), ())), preferred_element_type=jnp.float32
    )


def dot_tn(left, right):
    return lax.dot_general(
        left, right, (((0,), (0,)), ((), ())), preferred_element_type=jnp.float32
    )


def named(keys, refs):
    return types.SimpleNamespace(**dict(zip(keys, refs)))


def low(values):
    return values.astype(jnp.bfloat16)


def wide(values):
    return values.astype(jnp.float32)


def norm(values):
    shifted = values - jnp.mean(values, axis=-1, keepdims=True)
    inverse = lax.rsqrt(jnp.mean(shifted * shifted, axis=-1, keepdims=True) + 1e-05)
    return shifted * inverse, inverse


def cut(ref, kind, bit):
    if kind == LEAD:
        return ref.at[bit]
    rows, cols = ref.shape[-2:]
    lead = (slice(None),) * (len(ref.shape) - 2)
    if kind == ROWS:
        return ref.at[(*lead, rows_at(bit * (rows // 2), rows // 2), slice(None))]
    return ref.at[(*lead, slice(None), lanes_at(bit * (cols // 2), cols // 2))]


def half_shape(shape, kind):
    if kind == LEAD:
        return shape[1:]
    if kind == ROWS:
        return (*shape[:-2], shape[-2] // 2, shape[-1])
    return (*shape[:-1], shape[-1] // 2)


def add_into(total, term):
    def body(step, carry):
        at = rows_at(step * 16, 16)
        for lead in range(total.shape[0]) if len(total.shape) == 3 else (None,):
            where = (at, slice(None)) if lead is None else (lead, at, slice(None))
            total[where] = low(wide(total[where]) + wide(term[where]))
        return carry

    lax.fori_loop(0, total.shape[-2] // 16, body, 0)


class Halving:
    def __init__(self, courier, bits, targets, sums, stages):
        self.courier, self.bits, self.targets = courier, bits, targets
        self.sums, self.stages, self.pending = sums, stages, {}

    def give(self, which, stage):
        axis, kind = ROUTES[which][stage]
        self.pending[which] = self.courier.send(
            cut(self.sums[which], kind, 1 - self.bits[axis]),
            self.stages[which][stage],
            self.targets[axis],
        )

    def take(self, which, stage):
        axis, kind = ROUTES[which][stage]
        self.pending[which].wait_recv()
        add_into(self.stages[which][stage], cut(self.sums[which], kind, self.bits[axis]))
        self.sums[which] = self.stages[which][stage]


def chain_of(which, shape):
    chain = []
    for _, kind in ROUTES[which]:
        shape = half_shape(shape, kind)
        chain.append(shape)
    return chain


def head_lanes(first, shape):
    row = lax.broadcasted_iota(jnp.int32, shape, 0) - first
    column = lax.broadcasted_iota(jnp.int32, shape, 1)
    inside = (row >= 0) & (row < HEADS)
    inside &= (column >= row * HEAD_DIM) & (column < (row + 1) * HEAD_DIM)
    return inside.astype(jnp.float32)


def pass_body(keys, *refs):
    r = named(keys, refs)
    seq, opt = lax.axis_index("seq"), lax.axis_index("opt")
    bits, targets = partners(seq, opt)
    core, y = bits[CORE], bits[Y]
    opt_x = targets[X][1]
    ring = [((seq + step) % 8, opt) for step in range(1, 8)]
    micro, span = r.usable.shape[0], r.usable.shape[2]
    width = r.in_low.shape[1]
    lat_count, width_lat = r.latents.shape
    own = lat_count // 8
    scale = HEAD_DIM ** (-0.5)
    load = Loader(r.local)
    loads = [
        load.start(source, target)
        for source, target in (
            (r.w_key, r.f_key),
            (r.w_value, r.f_value),
            (r.w_query, r.f_query),
            (r.w_out, r.f_out),
            (r.w_up, r.f_up),
            (r.w_down, r.f_down),
        )
    ]
    clear(r.base)
    greet([targets[CORE], targets[X], *ring])
    courier = Courier(r.send, r.recv)

    def begin(full, rows):
        block = full.at[rows_at(opt * rows, rows)]
        half = full.at[rows_at(opt * rows + y * (rows // 2), rows // 2)]
        return [
            courier.send(half, half, targets[X]),
            courier.send(block, block, targets[CORE]),
        ]

    def relay(full, rows, state):
        state[0].wait_recv()
        half = full.at[rows_at(opt_x * rows + y * (rows // 2), rows // 2)]
        state.append(courier.send(half, half, targets[Y]))
        state.append(courier.send(half, half, targets[CORE]))

    def relay_more(full, rows, state):
        state[2].wait_recv()
        half = full.at[rows_at(opt_x * rows + (1 - y) * (rows // 2), rows // 2)]
        state.append(courier.send(half, half, targets[CORE]))

    def complete(state):
        for index in (1, 3, 4):
            state[index].wait_recv()

    def place(full, source):
        rows = source.shape[0]

        def body(step, carry):
            at = rows_at(step * 32, 32)
            full[rows_at(opt * rows + step * 32, 32), :] = low(source[at, :])
            return carry

        lax.fori_loop(0, rows // 32, body, 0)

    key_rows = r.f_key.shape[0]
    loads[0].wait()
    loads[1].wait()

    def place_pair(step, carry):
        at = rows_at(opt * key_rows + step * 32, 32)
        source = rows_at(step * 32, 32)
        r.pair_full[at, :width] = low(r.f_key[source, :])
        r.pair_full[at, width:] = low(r.f_value[source, :])
        return carry

    lax.fori_loop(0, key_rows // 32, place_pair, 0)
    pair_state = begin(r.pair_full, key_rows)

    def norm_in(step, carry):
        at = rows_at(step * 64, 64)
        hat, inverse = norm(wide(r.tokens[at, :]))
        r.in_hat[at, :] = hat
        r.in_inv[at, :] = inverse
        r.in_low[at, :] = low(hat * r.in_vectors[0:1, :] + r.in_vectors[1:2, :])
        return carry

    lax.fori_loop(0, r.in_low.shape[0] // 64, norm_in, 0)
    def norm_lat(step, carry):
        at = rows_at(step * 32, 32)
        hat, _ = norm(r.latents[at, :])
        r.lat_low[at, :] = low(hat * r.lat_vectors[0:1, :] + r.lat_vectors[1:2, :])
        return carry

    lax.fori_loop(0, lat_count // 32, norm_lat, 0)
    query_rows, out_rows, up_rows = (
        r.f_query.shape[0],
        r.f_out.shape[0],
        r.f_up.shape[0],
    )
    for index in range(4):

        @pl.when(opt == index)
        def _(index=index):
            r.lat_block[...] = r.lat_low[:, index * up_rows : (index + 1) * up_rows]

    for index, (full, staged) in enumerate(
        (
            (r.query_full, r.f_query),
            (r.out_full, r.f_out),
            (r.up_full, r.f_up),
            (r.down_full, r.f_down),
        )
    ):
        loads[2 + index].wait()
        place(full, staged)
    relay(r.pair_full, key_rows, pair_state)
    query_state = begin(r.query_full, query_rows)
    relay_more(r.pair_full, key_rows, pair_state)
    complete(pair_state)

    def project(step, carry):
        at = rows_at(step * 128, 128)
        r.pairs[at, :] = low(dot_nn(r.in_low[at, :], r.pair_full[...]))
        return carry

    lax.fori_loop(0, r.in_low.shape[0] // 128, project, 0)
    relay(r.query_full, query_rows, query_state)
    out_state = begin(r.out_full, out_rows)
    relay_more(r.query_full, query_rows, query_state)
    complete(query_state)

    def project_query(step, carry):
        at = rows_at(step * 128, 128)
        r.queries[at, :] = low(dot_nn(r.lat_low[at, :], r.query_full[...]))
        return carry

    lax.fori_loop(0, lat_count // 128, project_query, 0)

    relay(r.out_full, out_rows, out_state)
    up_state = begin(r.up_full, up_rows)
    to_owner = []
    for m in range(micro):
        at = slice(m * span, (m + 1) * span)
        usable = r.usable[m] > 0.5
        for h in range(HEADS):
            ch = slice(h * HEAD_DIM, (h + 1) * HEAD_DIM)
            ch_v = slice(width + h * HEAD_DIM, width + (h + 1) * HEAD_DIM)
            masked = jnp.where(
                usable, dot_nt(r.queries[:, ch], r.pairs[at, ch]) * scale, -1e30
            )
            top = jnp.max(masked, axis=1, keepdims=True)
            weights = jnp.exp(masked - top)
            sums = jnp.sum(weights, axis=1, keepdims=True)
            r.weights[m * HEADS + h] = weights
            lane = m * HEADS + h
            r.top[:, lane : lane + 1] = top
            r.lse[:, lane : lane + 1] = top + jnp.log(sums)
            r.part[m, :, ch] = low(dot_nn(low(weights), r.pairs[at, ch_v]) / sums)
        for target in ring:
            rows = rows_at(target[0] * own, own)
            to_owner.append(
                courier.send(r.part.at[m, rows], r.part_in.at[seq, m], target)
            )
        if m == 0:
            relay_more(r.out_full, out_rows, out_state)
            relay(r.up_full, up_rows, up_state)
            down_state = begin(r.down_full, up_rows)
    for target in ring:
        rows = rows_at(target[0] * own, own)
        to_owner.append(courier.send(r.lse.at[rows], r.lse_in.at[seq], target))
    mine = rows_at(seq * own, own)
    r.part_in[seq] = r.part[:, mine, :]
    r.lse_in[seq] = r.lse[mine, :]
    relay_more(r.up_full, up_rows, up_state)
    relay(r.down_full, up_rows, down_state)
    for moment, staged, slot in zip(
        (r.mom_query, r.mom_key, r.mom_value, r.mom_out, r.mom_up, r.mom_down),
        (r.f_query, r.f_key, r.f_value, r.f_out, r.f_up, r.f_down),
        SLOTS,
    ):

        @pl.when(seq == slot)
        def _(moment=moment, staged=staged):
            copy = pltpu.make_async_copy(moment, staged, r.moment_sem)
            copy.start()
            copy.wait()
            r.base[rows_at(opt * up_rows, staged.shape[0]), : staged.shape[1]] = low(
                0.95 * staged[...]
            )

    own_base = r.base.at[rows_at(opt * up_rows, up_rows)]
    base_across = courier.send(own_base, own_base, targets[X])
    base_beside = courier.send(own_base, own_base, targets[CORE])
    relay_more(r.down_full, up_rows, down_state)
    for copy in to_owner:
        copy.wait_recv()

    peak = r.lse_in[0]
    for peer in range(1, 8):
        peak = jnp.maximum(peak, r.lse_in[peer])
    total = jnp.exp(r.lse_in[0] - peak)
    for peer in range(1, 8):
        total = total + jnp.exp(r.lse_in[peer] - peak)
    lse_all = peak + jnp.log(total)
    spread_heads = [head_lanes(m * HEADS, (128, width)) for m in range(micro)]
    collect_heads = [head_lanes((micro + m) * HEADS, (128, width)) for m in range(micro)]
    for m in range(micro):
        rows = slice(m * own, (m + 1) * own)
        for peer in range(8):
            share = jnp.dot(
                jnp.exp(r.lse_in[peer] - lse_all),
                spread_heads[m],
                precision=highest,
                preferred_element_type=jnp.float32,
            ) * wide(r.part_in[peer, m])
            r.attended[rows, :] = share if peer == 0 else r.attended[rows, :] + share
    local_rows = rows_at(core * (micro * own), micro * own)
    att_low = low(r.attended[...])
    r.x_att[local_rows, :] = att_low
    back_rows = r.cotangent[...]
    r.x_cot[local_rows, :] = back_rows
    complete(out_state)
    own_latents = jnp.concatenate([r.latents[mine, :]] * micro, axis=0)
    r.hidden[...] = own_latents + dot_nn(att_low, r.out_full[...])
    mlp_hat, mlp_inv = norm(r.hidden[...])
    r.mlp_hat[...] = mlp_hat
    mlp_low = low(mlp_hat * r.lat_vectors[2:3, :] + r.lat_vectors[3:4, :])
    r.x_mlp[local_rows, :] = mlp_low
    complete(up_state)
    pre_act = dot_nn(mlp_low, r.up_full[...]) + r.lat_vectors[4:5, :]
    cdf = 0.5 * (1.0 + lax.erf(pre_act * 0.7071067811865476))
    act_low = low(pre_act * cdf)
    r.slope[...] = cdf + pre_act * jnp.exp(-0.5 * pre_act * pre_act) * 0.3989422804014327
    r.x_act[local_rows, :] = act_low
    complete(down_state)
    grad_pre = low(dot_nt(back_rows, r.down_full[...]) * r.slope[...])
    r.x_pre[local_rows, :] = grad_pre
    grad_mlp = dot_nt(grad_pre, r.up_full[...])
    mlp_hat = r.mlp_hat[...]
    r.vectors[...] = jnp.zeros_like(r.vectors)
    r.vectors[0:1, :] = jnp.sum(grad_mlp * mlp_hat, axis=0, keepdims=True)
    r.vectors[1:2, :] = jnp.sum(grad_mlp, axis=0, keepdims=True)
    r.vectors[2:3, :] = jnp.sum(wide(grad_pre), axis=0, keepdims=True)
    r.vectors[3:4, :] = jnp.sum(wide(back_rows), axis=0, keepdims=True)
    scaled = grad_mlp * r.lat_vectors[2:3, :]
    grad_hidden = wide(back_rows) + mlp_inv * (
        scaled
        - jnp.mean(scaled, axis=-1, keepdims=True)
        - mlp_hat * jnp.mean(scaled * mlp_hat, axis=-1, keepdims=True)
    )
    rest = grad_hidden[:own]
    for m in range(1, micro):
        rest = rest + grad_hidden[m * own : (m + 1) * own]
    r.rest[...] = low(rest)
    grad_branch = low(grad_hidden)
    r.x_branch[local_rows, :] = grad_branch
    grad_own = low(dot_nt(grad_branch, r.out_full[...]))
    products = wide(grad_own) * r.attended[...]
    back = jnp.where(
        lax.broadcasted_iota(jnp.int32, lse_all.shape, 1) < micro * HEADS, lse_all, 0.0
    )
    for m in range(micro):
        rows = slice(m * own, (m + 1) * own)
        r.grad_att[m, mine, :] = grad_own[rows]
        back = back + lax.dot_general(
            products[rows],
            collect_heads[m],
            (((1,), (1,)), ((), ())),
            precision=highest,
            preferred_element_type=jnp.float32,
        )
    r.back[mine, :] = back
    returns = []
    for target in ring:
        for view in (r.grad_att.at[:, mine], r.back.at[mine]):
            returns.append(courier.send(view, view, target))
    chip = []
    for array in (r.x_act, r.x_cot, r.x_mlp, r.x_pre, r.x_att, r.x_branch):
        view = array.at[local_rows]
        chip.append(courier.send(view, view, targets[CORE]))
    r.block_out[...] = low(
        r.hidden[...] + dot_nn(act_low, r.down_full[...]) + r.lat_vectors[5:6, :]
    )
    for copy in chip:
        copy.wait_recv()
    half = lanes_at(core * (width_lat // 2), width_lat // 2)
    for target, left, right in (
        (r.grad_down, r.x_act, r.x_cot),
        (r.grad_up, r.x_mlp, r.x_pre),
        (r.grad_out, r.x_att, r.x_branch),
    ):
        for tile in range(left.shape[1] // 128):
            cols = slice(tile * 128, (tile + 1) * 128)
            x_half, first = divmod(tile * 128, target.shape[1])
            target[x_half, first : first + 128, :] = low(dot_tn(left[:, cols], right[:, half]))
    halving = Halving(
        courier,
        bits,
        targets,
        {UP: r.grad_up, DOWN: r.grad_down, OUT: r.grad_out},
        {
            UP: (r.up_0, r.up_1, r.up_2, r.piece_up),
            DOWN: (r.down_0, r.down_1, r.down_2, r.piece_down),
            OUT: (r.out_0, r.out_1, r.out_2, r.piece_out),
        },
    )
    for which in (UP, DOWN, OUT):
        halving.give(which, 0)
    for copy in returns:
        copy.wait_recv()

    for h in range(HEADS):
        if h in POINTS:
            which, stage = POINTS[h]
            halving.take(which, stage)
            halving.give(which, stage + 1)
        ch = slice(h * HEAD_DIM, (h + 1) * HEAD_DIM)
        ch_v = slice(width + h * HEAD_DIM, width + (h + 1) * HEAD_DIM)
        grad_query = None
        for m in range(micro):
            at = slice(m * span, (m + 1) * span)
            lane = m * HEADS + h
            lane_in = (micro + m) * HEADS + h
            prob = r.weights[lane] * jnp.exp(
                r.top[:, lane : lane + 1] - r.back[:, lane : lane + 1]
            )
            grad_att = r.grad_att[m, :, ch]
            grad_prob = dot_nt(grad_att, r.pairs[at, ch_v])
            grad_scores = low(prob * (grad_prob - r.back[:, lane_in : lane_in + 1]))
            part = dot_nn(grad_scores, r.pairs[at, ch])
            grad_query = part if grad_query is None else grad_query + part
            r.grad_pairs[at, ch] = low(scale * dot_tn(grad_scores, r.queries[:, ch]))
            r.grad_pairs[at, ch_v] = low(dot_tn(low(prob), grad_att))
        r.grad_query[:, ch] = low(scale * grad_query)

    part_width = width // 2

    def pair_product(targets_two, which):
        for kind, target in enumerate(targets_two):
            cols = lanes_at(kind * width + which * part_width, part_width)
            right = r.grad_pairs[:, cols]
            for tile in range(width // TILE):
                rows = slice(tile * TILE, (tile + 1) * TILE)
                target[rows, :] = low(dot_tn(r.in_low[:, rows], right))

    base_across.wait_recv()
    other_base = r.base.at[rows_at(opt_x * up_rows, up_rows)]
    base_last = courier.send(other_base, other_base, targets[CORE])
    base_beside.wait_recv()
    pair_product((r.pair_other.at[0], r.pair_other.at[1]), 1 - core)
    pair_copy = courier.send(r.pair_other, r.pair_in, targets[CORE])
    for which in (UP, OUT, DOWN):
        halving.take(which, 2)
        halving.give(which, 3)
    pair_product((r.grad_key, r.grad_value), core)
    r.in_sums[...] = jnp.zeros_like(r.in_sums)

    def norm_in_back(step, carry):
        at = rows_at(step * 64, 64)
        grad_in = dot_nt(r.grad_pairs[at, :], r.pair_full[...])
        hat = r.in_hat[at, :]
        r.in_sums[0:1, :] = r.in_sums[0:1, :] + jnp.sum(grad_in * hat, axis=0, keepdims=True)
        r.in_sums[1:2, :] = r.in_sums[1:2, :] + jnp.sum(grad_in, axis=0, keepdims=True)
        scaled = grad_in * r.in_vectors[0:1, :]
        r.input_grad[at, :] = r.in_inv[at, :] * (
            scaled
            - jnp.mean(scaled, axis=-1, keepdims=True)
            - hat * jnp.mean(scaled * hat, axis=-1, keepdims=True)
        )
        return carry

    lax.fori_loop(0, r.in_low.shape[0] // 64, norm_in_back, 0)
    r.vectors[4:6, :width] = r.in_sums[0:2, :]
    base_last.wait_recv()
    pair_copy.wait_recv()
    add_into(r.grad_key, r.pair_in.at[0])
    add_into(r.grad_value, r.pair_in.at[1])
    for which in (UP, OUT, DOWN):
        halving.take(which, 3)
    courier.finish()


def run_pass(tokens, usable, cotangent, latents, lat_vectors, in_vectors, weights, moments):
    f32, bf16 = jnp.float32, jnp.bfloat16
    w_query, w_key, w_value, w_out, w_up, w_down = weights
    operands = dict(
        tokens=tokens,
        usable=usable,
        cotangent=cotangent,
        latents=latents,
        lat_vectors=lat_vectors,
        in_vectors=in_vectors,
        w_query=w_query,
        w_key=w_key,
        w_value=w_value,
        w_out=w_out,
        w_up=w_up,
        w_down=w_down,
        mom_query=moments[0],
        mom_key=moments[1],
        mom_value=moments[2],
        mom_out=moments[3],
        mom_up=moments[4],
        mom_down=moments[5],
    )
    count, width = tokens.shape
    micro, _, span = usable.shape
    lat_count, width_lat = latents.shape
    own = lat_count // 8
    rows = micro * own
    outputs = dict(
        block_out=((rows, width_lat), bf16),
        input_grad=((count, width), f32),
        grad_key=((width, width // 2), bf16),
        grad_value=((width, width // 2), bf16),
        grad_query=((lat_count, width), bf16),
        vectors=((8, width_lat), f32),
        rest=((own, width_lat), bf16),
        lat_low=((lat_count, width_lat), bf16),
        lat_block=((lat_count, width_lat // 4), bf16),
        query_full=((width_lat, width), bf16),
        base=((width_lat, width_lat), bf16),
    )
    scratch = dict(
        grad_up=((2, width_lat // 2, width_lat // 2), bf16),
        grad_down=((2, width_lat // 2, width_lat // 2), bf16),
        grad_out=((2, width // 2, width_lat // 2), bf16),
        f_query=(w_query.shape, f32),
        f_key=(w_key.shape, f32),
        f_value=(w_value.shape, f32),
        f_out=(w_out.shape, f32),
        f_up=(w_up.shape, f32),
        f_down=(w_down.shape, f32),
        pair_full=((width, 2 * width), bf16),
        out_full=((width, width_lat), bf16),
        up_full=((width_lat, width_lat), bf16),
        down_full=((width_lat, width_lat), bf16),
        in_low=((count, width), bf16),
        in_hat=((count, width), f32),
        in_inv=((count, 1), f32),
        in_sums=((8, width), f32),
        pairs=((count, 2 * width), bf16),
        queries=((lat_count, width), bf16),
        weights=((micro * HEADS, lat_count, span), f32),
        top=((lat_count, 128), f32),
        lse=((lat_count, 128), f32),
        part=((micro, lat_count, width), bf16),
        part_in=((8, micro, own, width), bf16),
        lse_in=((8, own, 128), f32),
        attended=((rows, width), f32),
        hidden=((rows, width_lat), f32),
        mlp_hat=((rows, width_lat), f32),
        slope=((rows, width_lat), f32),
        x_att=((2 * rows, width), bf16),
        x_branch=((2 * rows, width_lat), bf16),
        x_mlp=((2 * rows, width_lat), bf16),
        x_pre=((2 * rows, width_lat), bf16),
        x_act=((2 * rows, width_lat), bf16),
        x_cot=((2 * rows, width_lat), bf16),
        grad_att=((micro, lat_count, width), bf16),
        back=((lat_count, 128), f32),
        grad_pairs=((count, 2 * width), bf16),
        pair_other=((2, width, width // 2), bf16),
        pair_in=((2, width, width // 2), bf16),
    )
    for which, name in ((UP, "up"), (DOWN, "down"), (OUT, "out")):
        chain = chain_of(which, scratch["grad_" + name][0])
        for stage, shape in enumerate(chain[:-1]):
            scratch[f"{name}_{stage}"] = (shape, bf16)
        outputs["piece_" + name] = (chain[-1], bf16)
    copies = 5 * 5 + 7 * micro + 7 + 14 + 6 + 1 + 3 + 12
    sems = dict(
        send=pltpu.SemaphoreType.DMA((copies,)),
        recv=pltpu.SemaphoreType.DMA((copies,)),
        local=pltpu.SemaphoreType.DMA((6,)),
        moment_sem=pltpu.SemaphoreType.DMA,
    )
    keys = (*operands, *outputs, *scratch, *sems)
    vmem, anywhere = pl.BlockSpec(memory_space=pltpu.VMEM), pl.BlockSpec(memory_space=pl.ANY)
    results = pl.pallas_call(
        functools.partial(pass_body, keys),
        out_shape=[jax.ShapeDtypeStruct(*spec) for spec in outputs.values()],
        in_specs=[vmem] * 6 + [anywhere] * 12,
        out_specs=[vmem] * len(outputs),
        scratch_shapes=[*(pltpu.VMEM(*spec) for spec in scratch.values()), *sems.values()],
        compiler_params=pltpu.CompilerParams(
            collective_id=2, has_side_effects=True, vmem_limit_bytes=VMEM_LIMIT
        ),
        name="pass",
    )(*operands.values())
    return named(outputs, results)


def tail_body(keys, *refs):
    r = named(keys, refs)
    seq, opt = lax.axis_index("seq"), lax.axis_index("opt")
    bits, targets = partners(seq, opt)
    core, z0, z1, y, x = bits[CORE], bits[Z0], bits[Z1], bits[Y], bits[X]
    ring = [((seq + step) % 8, opt) for step in range(1, 8)]
    height = r.lat_block.shape[1]
    clear(r.g_full.at[0])
    clear(r.g_full.at[1])
    beyond = [((seq + step) % 8, targets[X][1]) for step in range(8)]
    greet([targets[CORE], *ring, *beyond])
    courier = Courier(r.send, r.recv)
    sums = {UP: r.up, DOWN: r.down, OUT: r.out, KEY: r.key, VALUE: r.value, QUERY: r.query}
    halving = Halving(
        courier,
        bits,
        targets,
        sums,
        {
            KEY: (r.key_0, r.key_1, r.key_2, r.key_3),
            VALUE: (r.value_0, r.value_1, r.value_2, r.value_3),
            QUERY: (r.query_0, r.query_1, r.query_2, r.query_3, r.query_4),
        },
    )
    for which in (QUERY, KEY, VALUE):
        halving.give(which, 0)
    def piece_place(which, seq_from, x_from):
        bit_y, bit_z0, bit_z1 = seq_from % 2, (seq_from // 2) % 2, seq_from // 4
        high, mid = (bit_y, bit_z0) if which in Y_FIRST else (bit_z0, bit_y)
        rows = sums[which].shape[0]
        return rows_at(x_from * (2 * height) + high * height + (mid * 2 + bit_z1) * rows, rows)

    def piece_copy(index, which, seq_from, x_from, same):
        cols = sums[which].shape[1]
        place = piece_place(which, seq_from, x_from)
        return pltpu.make_async_remote_copy(
            src_ref=sums[which],
            dst_ref=r.g_full.at[core, place, pl.ds(0, cols)],
            send_sem=r.piece_send.at[index, 0 if same else 1],
            recv_sem=r.piece_recv.at[0 if same else 1, seq_from],
            device_id=(SLOTS[index], opt if same else targets[X][1]),
            device_id_type=MESH,
        )

    def offer(index, which):
        piece_copy(index, which, seq, x, False).start()

        @pl.when(seq != SLOTS[index])
        def _():
            piece_copy(index, which, seq, x, True).start()

        @pl.when(seq == SLOTS[index])
        def _():
            cols = sums[which].shape[1]
            r.g_full[core, piece_place(which, seq, x), :cols] = sums[which][...]

    owned = ((1, KEY), (2, VALUE), (3, OUT), (4, UP), (5, DOWN))
    for index, which in owned[2:]:
        offer(index, which)
    r.vectors_sum[...] = r.vectors[...]
    vector_copy = courier.send(r.vectors, r.vectors_in.at[0], targets[CORE])
    rest_width = r.rest.shape[1] // 2
    column = lanes_at(core * rest_width, rest_width)
    rest_copy = courier.send(
        r.rest.at[:, lanes_at((1 - core) * rest_width, rest_width)], r.rest_in.at[0], targets[CORE]
    )
    halving.take(QUERY, 0)
    halving.give(QUERY, 1)
    vector_copy.wait_recv()
    r.vectors_sum[...] = r.vectors_sum[...] + r.vectors_in[0]
    rest_copy.wait_recv()
    r.rest_sum[...] = low(wide(r.rest[:, column]) + wide(r.rest_in[0]))
    rest_copy = courier.send(r.rest_sum, r.rest_in.at[1], targets[X])
    for stage in range(4):
        axis = (X, Y, Z0, Z1)[stage]
        r.vectors_out[stage] = r.vectors_sum[...]
        vector_copy = courier.send(
            r.vectors_out.at[stage], r.vectors_in.at[stage + 1], targets[axis]
        )
        if stage > 0:
            rest_copy.wait_recv()
            if stage == 1:
                r.rest_all[z1, z0, y, :, column] = low(wide(r.rest_sum[...]) + wide(r.rest_in[1]))
            every = slice(None)
            lead = ((z1, z0, y), (every, z0, y), (every, every, y))[stage - 1]
            view = r.rest_all.at[(*lead, every, column)]
            rest_copy = courier.send(view, view, targets[(Z1, Z0, Y)[stage - 1]])
        for which in (QUERY, KEY, VALUE):
            own_stage = stage + 1 if which == QUERY else stage
            halving.take(which, own_stage)
            if stage < 3:
                halving.give(which, own_stage + 1)
        vector_copy.wait_recv()
        r.vectors_sum[...] = r.vectors_sum[...] + r.vectors_in[stage + 1]
    rest_copy.wait_recv()
    view = r.rest_all.at[:, :, :, :, column]
    rest_copy = courier.send(view, view, targets[CORE])

    for index, which in owned[:2]:
        offer(index, which)
    rows, width = sums[QUERY].shape
    query_column = lanes_at(core * width, width)
    start = (x * 8 + y * 4 + z0 * 2 + z1) * rows
    r.query_all[rows_at(start, rows), query_column] = sums[QUERY][...]
    view = r.query_all.at[rows_at(start, rows), query_column]
    query_copies = [courier.send(view, view, target) for target in ring]

    gathered = (r.g_up, r.g_down, r.g_key, r.g_value, r.g_out)
    full = (r.n_up, r.n_down, r.n_key, r.n_value, r.n_out)
    for which in range(5):
        high, mid = (y, z0) if which in Y_FIRST else (z0, y)
        rows = sums[which].shape[0]
        gathered[which][rows_at((high * 4 + mid * 2 + z1) * rows, rows), :] = sums[which][...]

    def gather(which, step):
        first_axis, last_axis = (Y, Z0) if which in Y_FIRST else (Z0, Y)
        high, mid = bits[first_axis], bits[last_axis]
        rows = sums[which].shape[0]
        if step < 3:
            base, count = ((high * 4 + mid * 2 + z1, 1), (high * 4 + mid * 2, 2), (high * 4, 4))[
                step
            ]
            source = target = gathered[which].at[rows_at(base * rows, count * rows)]
        else:
            cols = sums[which].shape[1]
            source = gathered[which].at[rows_at((1 - core) * (4 * rows), 4 * rows)]
            target = full[which].at[:, lanes_at(core * cols, cols)]
        return pltpu.make_async_remote_copy(
            src_ref=source,
            dst_ref=target,
            send_sem=r.gather_send.at[which, step],
            recv_sem=r.gather_recv.at[which, step],
            device_id=targets[(Z1, last_axis, first_axis, CORE)[step]],
            device_id_type=MESH,
        )

    for which in range(5):
        gather(which, 0).start()
    for copy in query_copies:
        copy.wait_recv()
    view = r.query_all.at[rows_at(x * (8 * sums[QUERY].shape[0]), 8 * sums[QUERY].shape[0]), query_column]
    courier.send(view, view, targets[X]).wait_recv()
    view = r.query_all.at[:, query_column]
    courier.send(view, view, targets[CORE]).wait_recv()
    rest_copy.wait_recv()

    for index, which in owned:

        @pl.when(seq == SLOTS[index])
        def _(index=index, which=which):
            for seq_from in range(8):
                if seq_from != SLOTS[index]:
                    piece_copy(index, which, seq_from, x, True).wait_recv()
                piece_copy(index, which, seq_from, 1 - x, False).wait_recv()

    beside = courier.send(r.g_full.at[core], r.g_full.at[core], targets[CORE])
    beside.wait_recv()
    side = r.whole.shape[1]
    tiles = side // TILE
    narrow = (seq == SLOTS[1]) | (seq == SLOTS[2])
    r.total[0] = 0.0

    def join(tile, carry):
        at = rows_at(tile * TILE, TILE)
        r.wide[at, :] = wide(r.base[at, :])

        @pl.when(jnp.logical_not(narrow))
        def _():
            for index in range(2):
                lanes = slice(index * (side // 2), (index + 1) * (side // 2))
                r.wide[at, lanes] = r.wide[at, lanes] + wide(r.g_full[index, at, :])

        @pl.when(narrow)
        def _():
            part = width
            for index in range(2):
                lanes = slice(index * part, (index + 1) * part)
                r.wide[at, lanes] = r.wide[at, lanes] + wide(r.g_full[index, at, :part])

        @pl.when(seq == SLOTS[0])
        def _():
            lanes = slice(0, 2 * width)
            r.wide[at, lanes] = r.wide[at, lanes] + dot_tn(
                r.lat_low[:, lanes_at(tile * TILE, TILE)], r.query_all[...]
            )

        block = r.wide[at, :]
        r.total[0] = r.total[0] + jnp.sum(block * block)
        return carry

    lax.fori_loop(0, tiles, join, 0)
    scale = 1.0 / (jnp.sqrt(jnp.full((1, 1), r.total[0], jnp.float32)) + 1e-07)

    def normalise(tile, carry):
        at = rows_at(tile * TILE, TILE)
        block = r.wide[at, :] * scale
        r.wide[at, :] = block
        r.whole[at, :] = low(block)
        return carry

    lax.fori_loop(0, tiles, normalise, 0)

    def update(at):
        block = coef_one * r.wide[at, :] + dot_nn(r.whole[at, :], r.poly[...])
        r.wide[at, :] = block
        r.whole[at, :] = low(block)

    def sweep(index, carry):
        for step, turn in enumerate((0, 1, 3, 4)):

            @pl.when(index == turn)
            def _(step=step):
                if step < 4:
                    for which in range(5):
                        gather(which, step).wait_recv()
                if step < 3:
                    for which in range(5):
                        gather(which, step + 1).start()
                if step == 3:
                    for which in range(5):
                        rows, cols = gathered[which].shape
                        full[which][:, lanes_at(core * cols, cols)] = gathered[which][
                            rows_at(core * (rows // 2), rows // 2), :
                        ]

        polynomial(r.whole, r.gram, r.poly)

        @pl.when(index < 4)
        def _():
            def step_rows(tile, inner):
                update(rows_at(tile * TILE, TILE))
                return inner

            lax.fori_loop(0, tiles, step_rows, 0)

        return carry

    lax.fori_loop(0, 5, sweep, 0)
    own_first = opt * height
    update(rows_at(own_first, height))

    outs = (r.o_query, r.o_key, r.o_value, r.o_out, r.o_up, r.o_down)
    z, depth = seq // 2, 4

    def copy(which, part, way, mine):
        out = outs[which]
        rows = out.shape[0] // PARTS
        view = out.at[pl.ds(part * rows, rows)]
        source = view
        if mine:
            source = r.whole.at[rows_at(own_first + part * rows, rows), pl.ds(0, out.shape[1])]
        return pltpu.make_async_remote_copy(
            src_ref=source,
            dst_ref=view,
            send_sem=r.spread_send.at[way, which * PARTS + part],
            recv_sem=r.spread_recv.at[which * PARTS + part],
            device_id=((seq + 2, opt), (seq - 2, opt), targets[Y])[way],
            device_id_type=MESH,
        )

    def ways(which, mine):
        slot_y, slot_z = SLOTS[which] % 2, SLOTS[which] // 2
        turn = (y == slot_y) & ((z == slot_z) if mine else (z != slot_z))
        return (
            turn & (z >= slot_z) & (z < depth - 1),
            turn & (z <= slot_z) & (z > 0),
            turn,
        )

    def for_ways(which, mine, action):
        for way, on in enumerate(ways(which, mine)):

            @pl.when(on)
            def _(way=way):
                action(way)

    def latent_gradients():
        r.lat_grads[...] = jnp.zeros_like(r.lat_grads)
        r.lat_grads[2:6, :] = r.vectors_sum[0:4, :]

        def latent_rows(step, carry):
            at = rows_at(step * 32, 32)
            hat, inverse = norm(r.latents[at, :])
            grad = dot_nt(r.query_all[at, :], r.query_full[...])
            r.lat_grads[0:1, :] = r.lat_grads[0:1, :] + jnp.sum(grad * hat, axis=0, keepdims=True)
            r.lat_grads[1:2, :] = r.lat_grads[1:2, :] + jnp.sum(grad, axis=0, keepdims=True)
            scaled = grad * r.lat_vectors[0:1, :]
            r.latent_grad[at, :] = wide(r.rest_all[step // 4, (step // 2) % 2, step % 2]) + inverse * (
                scaled
                - jnp.mean(scaled, axis=-1, keepdims=True)
                - hat * jnp.mean(scaled * hat, axis=-1, keepdims=True)
            )
            return carry

        lax.fori_loop(0, r.latents.shape[0] // 32, latent_rows, 0)
        r.query_grad[...] = dot_tn(r.lat_block[...], r.query_all[...])

    for step in range(PARTS + 1):
        if step == 1:
            latent_gradients()
        for which in ORDER if step < PARTS else ():
            if step >= AHEAD:
                for_ways(
                    which, True, lambda way: copy(which, step - AHEAD, way, True).wait_send()
                )
            for_ways(which, True, lambda way: copy(which, step, way, True).start())
        for which in ORDER if step > 0 else ():

            @pl.when(ways(which, False)[2])
            def _(which=which, step=step):
                copy(which, step - 1, 2, False).wait_recv()

            for_ways(which, False, lambda way: copy(which, step - 1, way, False).start())
    for which in ORDER:

        @pl.when(seq == SLOTS[which])
        def _(which=which):
            rows, cols = outs[which].shape
            outs[which][...] = r.whole[rows_at(own_first, rows), :cols]

    for part in range(PARTS):
        for which in ORDER:

            @pl.when(y != SLOTS[which] % 2)
            def _(which=which, part=part):
                copy(which, part, 2, False).wait_recv()

    for part in range(PARTS):
        for which in ORDER:
            for_ways(which, False, lambda way: copy(which, part, way, False).wait_send())
            if part >= PARTS - AHEAD:
                for_ways(which, True, lambda way: copy(which, part, way, True).wait_send())
    for index, which in owned:
        piece_copy(index, which, seq, x, False).wait_send()

        @pl.when(seq != SLOTS[index])
        def _(index=index, which=which):
            piece_copy(index, which, seq, x, True).wait_send()

    for which in range(5):
        for step in range(4):
            gather(which, step).wait_send()
    courier.finish()


def run_tail(done, latents, lat_vectors, moments):
    f32, bf16 = jnp.float32, jnp.bfloat16
    mom_query, mom_key, mom_value, mom_out, mom_up, mom_down = moments
    width_lat = latents.shape[1]
    key, value = (
        grad.reshape(2, grad.shape[0] // 2, grad.shape[1])
        for grad in (done.grad_key, done.grad_value)
    )
    operands = dict(
        vectors=done.vectors,
        rest=done.rest,
        lat_low=done.lat_low,
        lat_block=done.lat_block,
        query_full=done.query_full,
        base=done.base,
        latents=latents,
        lat_vectors=lat_vectors,
        up=done.piece_up,
        down=done.piece_down,
        out=done.piece_out,
        key=key,
        value=value,
        query=done.grad_query,
    )
    outputs = dict(
        vectors_sum=(done.vectors.shape, f32),
        lat_grads=((8, width_lat), f32),
        latent_grad=(latents.shape, f32),
        query_grad=(mom_query.shape, f32),
        n_up=(mom_up.shape, bf16),
        n_down=(mom_down.shape, bf16),
        n_key=(mom_key.shape, bf16),
        n_value=(mom_value.shape, bf16),
        n_out=(mom_out.shape, bf16),
        o_query=(mom_query.shape, bf16),
        o_key=(mom_key.shape, bf16),
        o_value=(mom_value.shape, bf16),
        o_out=(mom_out.shape, bf16),
        o_up=(mom_up.shape, bf16),
        o_down=(mom_down.shape, bf16),
    )
    half_rest = (done.rest.shape[0], done.rest.shape[1] // 2)
    scratch = dict(
        vectors_in=((5, *done.vectors.shape), f32),
        vectors_out=((4, *done.vectors.shape), f32),
        rest_in=((2, *half_rest), bf16),
        rest_sum=(half_rest, bf16),
        rest_all=((2, 2, 2, *done.rest.shape), bf16),
        query_all=(done.grad_query.shape, bf16),
        g_full=((2, width_lat, width_lat // 2), bf16),
        g_up=((width_lat // 2, width_lat // 2), bf16),
        g_down=((width_lat // 2, width_lat // 2), bf16),
        g_key=(key.shape[1:], bf16),
        g_value=(value.shape[1:], bf16),
        g_out=((2 * mom_out.shape[0], width_lat // 2), bf16),
        wide=((width_lat, width_lat), f32),
        whole=((width_lat, width_lat), bf16),
        gram=((width_lat, width_lat), bf16),
        poly=((width_lat, width_lat), bf16),
    )
    for which, name, array in (
        (KEY, "key", key),
        (VALUE, "value", value),
        (QUERY, "query", done.grad_query),
    ):
        for stage, shape in enumerate(chain_of(which, array.shape)):
            scratch[f"{name}_{stage}"] = (shape, bf16)
    copies = 48
    count = len(SLOTS) * PARTS
    dma = pltpu.SemaphoreType.DMA
    sems = dict(
        send=dma((copies,)),
        recv=dma((copies,)),
        piece_send=dma((6, 2)),
        piece_recv=dma((2, 8)),
        gather_send=dma((5, 4)),
        gather_recv=dma((5, 4)),
        spread_send=dma((3, count)),
        spread_recv=dma((count,)),
        total=pltpu.SMEM((1,), f32),
    )
    keys = (*operands, *outputs, *scratch, *sems)
    vmem = pl.BlockSpec(memory_space=pltpu.VMEM)
    results = pl.pallas_call(
        functools.partial(tail_body, keys),
        out_shape=[jax.ShapeDtypeStruct(*spec) for spec in outputs.values()],
        in_specs=[vmem] * len(operands),
        out_specs=[vmem] * len(outputs),
        scratch_shapes=[*(pltpu.VMEM(*spec) for spec in scratch.values()), *sems.values()],
        compiler_params=pltpu.CompilerParams(
            collective_id=0, has_side_effects=True, vmem_limit_bytes=VMEM_LIMIT
        ),
        name="tail",
    )(*operands.values())
    return named(outputs, results)


def adam_update(param, gradient, first, second, step_rate, decay):
    first_new = 0.9 * first + 0.1 * gradient
    second_new = 0.95 * second + 0.05 * gradient * gradient
    ratio = first_new / (1.0 - 0.9**STEP) / (jnp.sqrt(second_new / (1.0 - 0.95**STEP)) + 1e-08)
    return (first_new, second_new, param - step_rate * (ratio + decay * param))


def local_small(
    inputs,
    key_mask,
    lengths,
    cotangent,
    latents,
    lat_vectors,
    in_vectors,
    w_query,
    w_key,
    w_value,
    w_out,
    w_up,
    w_down,
    mom_query,
    mom_key,
    mom_value,
    mom_out,
    mom_up,
    mom_down,
    lat_first,
    lat_second,
    in_first,
    in_second,
    latent_first,
    latent_second,
):
    seq_index = lax.axis_index("seq")
    micro_count, _, span, width_in = inputs.shape
    lat_count, width_lat = latents.shape
    positions = seq_index * span + jnp.arange(span, dtype=jnp.int32)
    usable = (positions < lengths[:, :, None]) & ((key_mask == 1) | (positions == 0))
    masters = (w_query, w_key, w_value, w_out, w_up, w_down)
    moments = (mom_query, mom_key, mom_value, mom_out, mom_up, mom_down)
    done = run_pass(
        inputs.reshape(-1, width_in),
        usable.astype(jnp.float32),
        cotangent.reshape(-1, width_lat),
        latents,
        lat_vectors,
        in_vectors,
        masters,
        moments,
    )
    summed = run_tail(done, latents, lat_vectors, moments)
    gradients = (
        summed.query_grad,
        summed.n_key,
        summed.n_value,
        summed.n_out,
        summed.n_up,
        summed.n_down,
    )
    moments_new = [
        0.95 * moment + gradient.astype(jnp.float32)
        for moment, gradient in zip(moments, gradients)
    ]
    currents = (
        summed.o_query,
        summed.o_key,
        summed.o_value,
        summed.o_out,
        summed.o_up,
        summed.o_down,
    )
    new_masters = update_masters(masters, currents)
    lat_vec_sum = summed.lat_grads[:6]
    in_vec_sum = summed.vectors_sum[4:6, :width_in]
    latent_sum = summed.latent_grad
    return (
        done.block_out.reshape(cotangent.shape),
        done.input_grad.reshape(inputs.shape),
        *moments_new,
        *new_masters,
        *adam_update(lat_vectors, lat_vec_sum, lat_first, lat_second, 0.6, 0.0),
        *adam_update(in_vectors, in_vec_sum, in_first, in_second, 0.6, 0.0),
        *adam_update(latents, latent_sum, latent_first, latent_second, 1.0, 0.1),
    )


def update_masters(masters, currents):
    fans = (D_LAT, E_IN, E_IN, OUT_FAN, D_LAT, D_LAT)
    sides = (D_LAT, E_IN, E_IN, D_LAT, D_LAT, D_LAT)
    new_masters = []
    for master, current, fan_in, long_side in zip(masters, currents, fans, sides):
        step_rate = fan_in ** (-0.5)
        new_masters.append(
            (1.0 - 0.1 * step_rate) * master
            - step_rate * long_side**0.5 * current.astype(jnp.float32)
        )
    return new_masters


def local(
    inputs,
    key_mask,
    lengths,
    cotangent,
    latents,
    lat_vectors,
    in_vectors,
    w_query,
    w_key,
    w_value,
    w_out,
    w_up,
    w_down,
    mom_query,
    mom_key,
    mom_value,
    mom_out,
    mom_up,
    mom_down,
    lat_first,
    lat_second,
    in_first,
    in_second,
    latent_first,
    latent_second,
):
    query_low, key_low, value_low, out_low, up_low, down_low = (
        lax.all_gather(w_query.astype(jnp.bfloat16), "opt", axis=0, tiled=True),
        lax.all_gather(w_key.astype(jnp.bfloat16), "opt", axis=0, tiled=True),
        lax.all_gather(w_value.astype(jnp.bfloat16), "opt", axis=0, tiled=True),
        lax.all_gather(w_out.astype(jnp.bfloat16), "opt", axis=0, tiled=True),
        lax.all_gather(w_up.astype(jnp.bfloat16), "opt", axis=0, tiled=True),
        lax.all_gather(w_down.astype(jnp.bfloat16), "opt", axis=0, tiled=True),
    )
    pair_low = jnp.concatenate([key_low, value_low], axis=1)
    seq_index = lax.axis_index("seq")
    seq_size = lax.axis_size("seq")
    opt_index = lax.axis_index("opt")
    opt_size = lax.axis_size("opt")
    micro_count, doc_local, span, width_in = inputs.shape
    lat_count, width_lat = latents.shape
    own_rows = lat_count // seq_size
    row_start = seq_index * own_rows
    score_scale = HEAD_DIM ** (-0.5)
    lat_normed, lat_hat, lat_inv = layer_norm(latents, lat_vectors[0], lat_vectors[1])
    lat_low = lat_normed.astype(jnp.bfloat16)
    query_rows = jnp.dot(lat_low, query_low, preferred_element_type=jnp.float32).astype(
        jnp.bfloat16
    )
    query_heads = query_rows.reshape(lat_count, HEADS, HEAD_DIM)
    own_latents = lax.dynamic_slice_in_dim(latents, row_start, own_rows, 0)
    positions = seq_index * span + jnp.arange(span, dtype=jnp.int32)
    grad_query_rows = jnp.zeros((lat_count, width_in), jnp.float32)
    grad_pair = jnp.zeros((width_in, 2 * width_in), jnp.float32)
    grad_out_w = jnp.zeros((width_in, width_lat), jnp.float32)
    grad_up_w = jnp.zeros((width_lat, width_lat), jnp.float32)
    grad_down_w = jnp.zeros((width_lat, width_lat), jnp.float32)
    mlp_gain = jnp.zeros((width_lat,), jnp.float32)
    mlp_shift = jnp.zeros((width_lat,), jnp.float32)
    bias_up = jnp.zeros((width_lat,), jnp.float32)
    bias_down = jnp.zeros((width_lat,), jnp.float32)
    in_gain = jnp.zeros((width_in,), jnp.float32)
    in_shift = jnp.zeros((width_in,), jnp.float32)
    latent_rest = jnp.zeros((own_rows, width_lat), jnp.float32)
    block_parts = []
    input_parts = []
    for micro_step in range(micro_count):
        tokens = inputs[micro_step]
        usable = (positions[None, :] < lengths[micro_step][:, None]) & (
            (key_mask[micro_step] == 1) | (positions[None, :] == 0)
        )
        in_normed, in_hat, in_inv = layer_norm(
            tokens.astype(jnp.float32), in_vectors[0], in_vectors[1]
        )
        in_low = in_normed.astype(jnp.bfloat16)
        pair_rows = jnp.einsum(
            "bse,ef->bsf", in_low, pair_low, preferred_element_type=jnp.float32
        ).astype(jnp.bfloat16)
        key_heads = pair_rows[:, :, :width_in].reshape(doc_local, span, HEADS, HEAD_DIM)
        value_heads = pair_rows[:, :, width_in:].reshape(doc_local, span, HEADS, HEAD_DIM)
        masked = masked_scores(query_heads, key_heads, usable, score_scale)
        row_max = lax.pmax(jnp.max(masked, axis=-1), "seq")
        weights = jnp.exp(masked - row_max[..., None])
        weights_low = weights.astype(jnp.bfloat16)
        summed, row_sum = (
            lax.psum(
                jnp.einsum(
                    "bhns,bshd->bnhd", weights_low, value_heads, preferred_element_type=jnp.float32
                ).astype(jnp.bfloat16),
                "seq",
            ).astype(jnp.float32),
            lax.psum(jnp.sum(weights, axis=-1).astype(jnp.bfloat16), "seq").astype(jnp.float32),
        )
        sum_heads = jnp.transpose(row_sum, (0, 2, 1))[..., None]
        attended = summed / sum_heads
        own_att = (
            lax.dynamic_slice_in_dim(attended, row_start, own_rows, 1)
            .reshape(doc_local, own_rows, width_in)
            .astype(jnp.bfloat16)
        )
        hidden = own_latents[None] + jnp.einsum(
            "bne,ef->bnf", own_att, out_low, preferred_element_type=jnp.float32
        )
        mlp_normed, mlp_hat, mlp_inv = layer_norm(hidden, lat_vectors[2], lat_vectors[3])
        mlp_low = mlp_normed.astype(jnp.bfloat16)
        pre_act = (
            jnp.einsum("bnf,fg->bng", mlp_low, up_low, preferred_element_type=jnp.float32)
            + lat_vectors[4]
        )
        activated, gelu_pull = jax.vjp(exact_gelu, pre_act)
        act_low = activated.astype(jnp.bfloat16)
        block_parts.append(
            (
                hidden
                + jnp.einsum("bng,gk->bnk", act_low, down_low, preferred_element_type=jnp.float32)
                + lat_vectors[5]
            ).astype(jnp.bfloat16)
        )
        back_rows = cotangent[micro_step]
        grad_down_w = grad_down_w + jnp.einsum(
            "bng,bnk->gk", act_low, back_rows, preferred_element_type=jnp.float32
        )
        bias_down = bias_down + jnp.sum(back_rows.astype(jnp.float32), axis=(0, 1))
        grad_act = jnp.einsum(
            "bnk,gk->bng", back_rows, down_low, preferred_element_type=jnp.float32
        )
        grad_pre = gelu_pull(grad_act)[0].astype(jnp.bfloat16)
        grad_up_w = grad_up_w + jnp.einsum(
            "bnf,bng->fg", mlp_low, grad_pre, preferred_element_type=jnp.float32
        )
        bias_up = bias_up + jnp.sum(grad_pre.astype(jnp.float32), axis=(0, 1))
        grad_mlp = jnp.einsum("bng,fg->bnf", grad_pre, up_low, preferred_element_type=jnp.float32)
        mlp_gain = mlp_gain + jnp.sum(grad_mlp * mlp_hat, axis=(0, 1))
        mlp_shift = mlp_shift + jnp.sum(grad_mlp, axis=(0, 1))
        grad_hidden = back_rows.astype(jnp.float32) + norm_back(
            grad_mlp, mlp_hat, mlp_inv, lat_vectors[2]
        )
        latent_rest = latent_rest + jnp.sum(grad_hidden, axis=0)
        grad_branch = grad_hidden.astype(jnp.bfloat16)
        grad_out_w = grad_out_w + jnp.einsum(
            "bne,bnf->ef", own_att, grad_branch, preferred_element_type=jnp.float32
        )
        grad_own = jnp.einsum(
            "bnf,ef->bne", grad_branch, out_low, preferred_element_type=jnp.float32
        ).astype(jnp.bfloat16)
        grad_att = (
            lax.all_gather(grad_own, "seq", axis=1, tiled=True)
            .astype(jnp.float32)
            .reshape(doc_local, lat_count, HEADS, HEAD_DIM)
        )
        grad_summed = (grad_att / sum_heads).astype(jnp.bfloat16)
        inner = jnp.transpose(jnp.sum(grad_att * attended, axis=-1) / sum_heads[..., 0], (0, 2, 1))
        grad_prob = jnp.einsum(
            "bnhd,bshd->bhns", grad_summed, value_heads, preferred_element_type=jnp.float32
        )
        grad_scores = (weights * (grad_prob - inner[..., None])).astype(jnp.bfloat16)
        grad_query_rows = grad_query_rows + score_scale * jnp.einsum(
            "bhns,bshd->nhd", grad_scores, key_heads, preferred_element_type=jnp.float32
        ).reshape(lat_count, width_in)
        grad_keys = (
            score_scale
            * jnp.einsum(
                "bhns,nhd->bshd", grad_scores, query_heads, preferred_element_type=jnp.float32
            )
        ).astype(jnp.bfloat16)
        grad_values = jnp.einsum(
            "bhns,bnhd->bshd", weights_low, grad_summed, preferred_element_type=jnp.float32
        ).astype(jnp.bfloat16)
        grad_pairs = jnp.concatenate(
            [
                grad_keys.reshape(doc_local, span, width_in),
                grad_values.reshape(doc_local, span, width_in),
            ],
            axis=-1,
        )
        grad_pair = grad_pair + jnp.einsum(
            "bse,bsf->ef", in_low, grad_pairs, preferred_element_type=jnp.float32
        )
        grad_in = jnp.einsum(
            "bsf,ef->bse", grad_pairs, pair_low, preferred_element_type=jnp.float32
        )
        in_gain = in_gain + jnp.sum(grad_in * in_hat, axis=(0, 1))
        in_shift = in_shift + jnp.sum(grad_in, axis=(0, 1))
        input_parts.append(norm_back(grad_in, in_hat, in_inv, in_vectors[0]))
    grad_query_w = jnp.matmul(lat_low.astype(jnp.float32).T, grad_query_rows, precision=highest)
    grad_lat = jnp.matmul(grad_query_rows, query_low.astype(jnp.float32).T, precision=highest)
    zero_index = jnp.zeros((), jnp.int32)
    latent_grad = norm_back(grad_lat, lat_hat, lat_inv, lat_vectors[0]) + lax.dynamic_update_slice(
        jnp.zeros_like(latents), latent_rest, (row_start, zero_index)
    )
    lat_vec_grad = jnp.stack(
        [
            jnp.sum(grad_lat * lat_hat, axis=0),
            jnp.sum(grad_lat, axis=0),
            mlp_gain,
            mlp_shift,
            bias_up,
            bias_down,
        ]
    )
    in_vec_grad = jnp.stack([in_gain, in_shift])
    weight_grads = (
        grad_query_w,
        grad_pair[:, :width_in],
        grad_pair[:, width_in:],
        grad_out_w,
        grad_up_w,
        grad_down_w,
    )
    masters = (w_query, w_key, w_value, w_out, w_up, w_down)
    moments = (mom_query, mom_key, mom_value, mom_out, mom_up, mom_down)
    first_here = jnp.where(seq_index == 0, 0.95, 0.0)
    with_moment = []
    for gradient, moment in zip(weight_grads, moments):
        start = opt_index * moment.shape[0]
        rows = lax.dynamic_slice_in_dim(gradient, start, moment.shape[0], 0) + first_here * moment
        with_moment.append(
            lax.dynamic_update_slice(gradient, rows, (start, zero_index)).astype(jnp.bfloat16)
        )
    summed_low = lax.psum(tuple(with_moment), ("seq", "opt"))
    lat_vec_sum, in_vec_sum, latent_sum = lax.psum(
        (lat_vec_grad, in_vec_grad, latent_grad), ("seq", "opt")
    )
    moments_new = [
        lax.dynamic_slice_in_dim(summed, opt_index * moment.shape[0], moment.shape[0], 0).astype(
            jnp.float32
        )
        for summed, moment in zip(summed_low, moments)
    ]

    def padded(index):
        def pick():
            matrix = summed_low[index].T if index == 3 else summed_low[index]
            return jnp.pad(
                matrix, ((0, width_lat - matrix.shape[0]), (0, width_lat - matrix.shape[1]))
            )

        return pick

    slot = seq_index % 8
    own_matrix = lax.switch(jnp.minimum(slot, 5), [padded(index) for index in range(6)])
    own_result = newton(own_matrix)
    own_result = lax.cond(slot == 3, lambda: own_result.T, lambda: own_result)
    mine = jnp.stack(
        [
            lax.dynamic_slice_in_dim(own_result, opt_index * height, width_lat // opt_size, 0)
            for height in (width_in // opt_size, width_lat // opt_size)
        ]
    )
    is_wide = (slot == 0) | (slot >= 4)
    mine = jnp.where(is_wide, mine[1], mine[0])
    spread = lax.all_gather(mine, "seq", axis=0, tiled=False)
    currents = [
        spread[index, : moment.shape[0], : moment.shape[1]].astype(jnp.float32)
        for index, moment in enumerate(moments)
    ]
    new_masters = update_masters(masters, currents)
    lat_m, lat_v, lat_p = adam_update(lat_vectors, lat_vec_sum, lat_first, lat_second, 0.6, 0.0)
    in_m, in_v, in_p = adam_update(in_vectors, in_vec_sum, in_first, in_second, 0.6, 0.0)
    latent_m, latent_v, latent_p = adam_update(
        latents, latent_sum, latent_first, latent_second, 1.0, 0.1
    )
    block_out = jnp.stack(block_parts)
    input_grad = jnp.stack(input_parts)
    return (
        block_out,
        input_grad,
        moments_new[0],
        moments_new[1],
        moments_new[2],
        moments_new[3],
        moments_new[4],
        moments_new[5],
        new_masters[0],
        new_masters[1],
        new_masters[2],
        new_masters[3],
        new_masters[4],
        new_masters[5],
        lat_m,
        lat_v,
        lat_p,
        in_m,
        in_v,
        in_p,
        latent_m,
        latent_v,
        latent_p,
    )


def solution(mesh):
    small = (mesh.shape["seq"], mesh.shape["opt"]) == (8, 4)
    return jax.shard_map(
        local_small if small else local,
        mesh=mesh,
        in_specs=(
            P(None, "opt", "seq", None),
            P(None, "opt", "seq"),
            P(None, "opt"),
            P(None, "opt", "seq", None),
            P(),
            P(),
            P(),
            P("opt", None),
            P("opt", None),
            P("opt", None),
            P("opt", None),
            P("opt", None),
            P("opt", None),
            P("opt", None),
            P("opt", None),
            P("opt", None),
            P("opt", None),
            P("opt", None),
            P("opt", None),
            P(),
            P(),
            P(),
            P(),
            P(),
            P(),
        ),
        out_specs=(
            P(None, "opt", "seq", None),
            P(None, "opt", "seq", None),
            P("opt", None),
            P("opt", None),
            P("opt", None),
            P("opt", None),
            P("opt", None),
            P("opt", None),
            P("opt", None),
            P("opt", None),
            P("opt", None),
            P("opt", None),
            P("opt", None),
            P("opt", None),
            P(),
            P(),
            P(),
            P(),
            P(),
            P(),
            P(),
            P(),
            P(),
        ),
        check_vma=False,
    )
```

```python
import functools
import types

import jax
import jax.numpy as jnp
from jax import lax
from jax.experimental import pallas as pl
from jax.experimental.pallas import tpu as pltpu
from jax.sharding import PartitionSpec as P

D_LAT = 1280
HEADS = 8
HEAD_DIM = 96
E_IN = 768
STEP = 10
OUT_FAN = 4
TILE = 256
PARTS = (4, 4, 4, 4, 8, 8)
AHEAD = 2
POINTS = {0: (0, 0), 1: (4, 0), 2: (1, 0), 4: (0, 1), 5: (4, 1), 6: (1, 1)}
VMEM_LIMIT = 60 * 2**20
MESH = pl.DeviceIdType.MESH


highest = lax.Precision.HIGHEST
coef_one = 3.4445
coef_two = -4.775
coef_three = 2.0315


def layer_norm(values, scale_vec, offset):
    center = jnp.mean(values, axis=-1, keepdims=True)
    shifted = values - center
    inverse = lax.rsqrt(jnp.mean(shifted * shifted, axis=-1, keepdims=True) + 1e-05)
    normal_hat = shifted * inverse
    return (normal_hat * scale_vec + offset, normal_hat, inverse)


def norm_back(grad_out, normal_hat, inverse, scale_vec):
    scaled = grad_out * scale_vec
    return inverse * (
        scaled
        - jnp.mean(scaled, axis=-1, keepdims=True)
        - normal_hat * jnp.mean(scaled * normal_hat, axis=-1, keepdims=True)
    )


def exact_gelu(values):
    return jax.nn.gelu(values, approximate=False)


def masked_scores(query_heads, key_heads, usable, score_scale):
    scores = (
        jnp.einsum("nhd,bshd->bhns", query_heads, key_heads, preferred_element_type=jnp.float32)
        * score_scale
    )
    return jnp.where(usable[:, None, None, :], scores, -1e30)


def polynomial(low, gram, poly):
    side_tiles = gram.shape[0] // TILE

    def mirror(target, block, i):
        own = slice(i * TILE, (i + 1) * TILE)
        target[own, i * TILE :] = block
        for j in range(i + 1, side_tiles):
            part = block[:, (j - i) * TILE : (j - i + 1) * TILE]
            target[j * TILE : (j + 1) * TILE, own] = part.T

    for i in range(side_tiles):
        own = slice(i * TILE, (i + 1) * TILE)
        block = lax.dot_general(
            low[:, own],
            low[:, i * TILE :],
            (((0,), (0,)), ((), ())),
            preferred_element_type=jnp.float32,
        )
        mirror(gram, block.astype(jnp.bfloat16), i)
    for i in range(side_tiles):
        own = slice(i * TILE, (i + 1) * TILE)
        block = coef_three * jnp.dot(
            gram[own, :], gram[:, i * TILE :], preferred_element_type=jnp.float32
        ) + coef_two * gram[own, i * TILE :].astype(jnp.float32)
        mirror(poly, block.astype(jnp.bfloat16), i)


def newton_body(rows_ref, out_ref, wide, low, gram, poly, total):
    count, side = rows_ref.shape
    row_tiles = count // TILE
    total[0] = 0.0

    def add_squares(tile, carry):
        block = rows_ref[pl.ds(tile * TILE, TILE), :].astype(jnp.float32)
        total[0] = total[0] + jnp.sum(block * block)
        return carry

    lax.fori_loop(0, row_tiles, add_squares, 0)
    scale = 1.0 / (jnp.sqrt(jnp.full((1, 1), total[0], jnp.float32)) + 1e-07)

    def normalise(tile, carry):
        block = rows_ref[pl.ds(tile * TILE, TILE), :].astype(jnp.float32) * scale
        wide[pl.ds(tile * TILE, TILE), :] = block
        low[pl.ds(tile * TILE, TILE), :] = block.astype(jnp.bfloat16)
        return carry

    lax.fori_loop(0, row_tiles, normalise, 0)

    def sweep(index, carry):
        polynomial(low, gram, poly)

        def update(tile, inner):
            rows = pl.ds(tile * TILE, TILE)
            block = coef_one * wide[rows, :] + jnp.dot(
                low[rows, :], poly[...], preferred_element_type=jnp.float32
            )
            wide[rows, :] = block
            low[rows, :] = block.astype(jnp.bfloat16)
            return inner

        lax.fori_loop(0, row_tiles, update, 0)
        return carry

    lax.fori_loop(0, 5, sweep, 0)
    out_ref[...] = low[...]


def newton(rows):
    shape = rows.shape
    return pl.pallas_call(
        newton_body,
        out_shape=jax.ShapeDtypeStruct(shape, jnp.bfloat16),
        in_specs=[pl.BlockSpec(memory_space=pltpu.VMEM)],
        out_specs=pl.BlockSpec(memory_space=pltpu.VMEM),
        scratch_shapes=[
            pltpu.VMEM(shape, jnp.float32),
            pltpu.VMEM(shape, jnp.bfloat16),
            pltpu.VMEM((shape[1], shape[1]), jnp.bfloat16),
            pltpu.VMEM((shape[1], shape[1]), jnp.bfloat16),
            pltpu.SMEM((1,), jnp.float32),
        ],
        compiler_params=pltpu.CompilerParams(vmem_limit_bytes=60 * 2**20),
        name="newton",
    )(rows)


CORE, X, Y, Z0, Z1 = range(5)
LEAD, ROWS, COLS = range(3)
UP, DOWN, KEY, VALUE, OUT, QUERY = range(6)
ROUTES = (
    ((X, LEAD), (Y, ROWS), (Z0, ROWS), (Z1, ROWS)),
    ((Y, ROWS), (X, LEAD), (Z0, ROWS), (Z1, ROWS)),
    ((X, LEAD), (Y, ROWS), (Z0, ROWS), (Z1, ROWS)),
    ((Z0, ROWS), (X, LEAD), (Y, ROWS), (Z1, ROWS)),
    ((Z0, ROWS), (Y, ROWS), (X, LEAD), (Z1, ROWS)),
    ((CORE, COLS), (X, ROWS), (Y, ROWS), (Z0, ROWS), (Z1, ROWS)),
)
Y_FIRST = (UP, DOWN, KEY)
SLOTS = (3, 0, 7, 4, 2, 5)


def partners(seq, opt):
    bits = (opt % 2, opt // 2, seq % 2, (seq // 2) % 2, seq // 4)
    steps = ((0, 1), (0, 2), (1, 0), (2, 0), (4, 0))
    targets = [
        (seq + (1 - 2 * bit) * along_seq, opt + (1 - 2 * bit) * along_opt)
        for bit, (along_seq, along_opt) in zip(bits, steps)
    ]
    return bits, targets


def greet(targets):
    barrier = pltpu.get_barrier_semaphore()
    for target in targets:
        pl.semaphore_signal(barrier, inc=1, device_id=target, device_id_type=MESH)
    pl.semaphore_wait(barrier, len(targets))


class Courier:
    def __init__(self, send_sem, recv_sem):
        self.send_sem, self.recv_sem, self.started = send_sem, recv_sem, []

    def send(self, source, target_ref, device):
        index = len(self.started)
        copy = pltpu.make_async_remote_copy(
            src_ref=source,
            dst_ref=target_ref,
            send_sem=self.send_sem.at[index],
            recv_sem=self.recv_sem.at[index],
            device_id=device,
            device_id_type=MESH,
        )
        copy.start()
        self.started.append(copy)
        return copy

    def finish(self):
        for copy in self.started:
            copy.wait_send()


class Loader:
    def __init__(self, sem):
        self.sem, self.count = sem, 0

    def start(self, source, target):
        copy = pltpu.make_async_copy(source, target, self.sem.at[self.count])
        self.count += 1
        copy.start()
        return copy


def rows_at(start, count, unit=16):
    return pl.ds(pl.multiple_of(start, unit), count)


def lanes_at(start, count):
    return pl.ds(pl.multiple_of(start, 128), count)


def clear(ref):
    def body(step, carry):
        ref[rows_at(step * 32, 32), :] = jnp.zeros((32, ref.shape[1]), ref.dtype)
        return carry

    lax.fori_loop(0, ref.shape[0] // 32, body, 0)


def dot_nn(left, right):
    return jnp.dot(left, right, preferred_element_type=jnp.float32)


def dot_nt(left, right):
    return lax.dot_general(
        left, right, (((1,), (1,)), ((), ())), preferred_element_type=jnp.float32
    )


def dot_tn(left, right):
    return lax.dot_general(
        left, right, (((0,), (0,)), ((), ())), preferred_element_type=jnp.float32
    )


def named(keys, refs):
    return types.SimpleNamespace(**dict(zip(keys, refs)))


def low(values):
    return values.astype(jnp.bfloat16)


def wide(values):
    return values.astype(jnp.float32)


def norm(values):
    shifted = values - jnp.mean(values, axis=-1, keepdims=True)
    inverse = lax.rsqrt(jnp.mean(shifted * shifted, axis=-1, keepdims=True) + 1e-05)
    return shifted * inverse, inverse


def cut(ref, kind, bit):
    if kind == LEAD:
        return ref.at[bit]
    rows, cols = ref.shape[-2:]
    lead = (slice(None),) * (len(ref.shape) - 2)
    if kind == ROWS:
        return ref.at[(*lead, rows_at(bit * (rows // 2), rows // 2), slice(None))]
    return ref.at[(*lead, slice(None), lanes_at(bit * (cols // 2), cols // 2))]


def half_shape(shape, kind):
    if kind == LEAD:
        return shape[1:]
    if kind == ROWS:
        return (*shape[:-2], shape[-2] // 2, shape[-1])
    return (*shape[:-1], shape[-1] // 2)


def add_into(total, term):
    def body(step, carry):
        at = rows_at(step * 16, 16)
        for lead in range(total.shape[0]) if len(total.shape) == 3 else (None,):
            where = (at, slice(None)) if lead is None else (lead, at, slice(None))
            total[where] = low(wide(total[where]) + wide(term[where]))
        return carry

    lax.fori_loop(0, total.shape[-2] // 16, body, 0)


class Halving:
    def __init__(self, courier, bits, targets, sums, stages):
        self.courier, self.bits, self.targets = courier, bits, targets
        self.sums, self.stages, self.pending = sums, stages, {}

    def give(self, which, stage):
        axis, kind = ROUTES[which][stage]
        self.pending[which] = self.courier.send(
            cut(self.sums[which], kind, 1 - self.bits[axis]),
            self.stages[which][stage],
            self.targets[axis],
        )

    def take(self, which, stage):
        axis, kind = ROUTES[which][stage]
        self.pending[which].wait_recv()
        add_into(self.stages[which][stage], cut(self.sums[which], kind, self.bits[axis]))
        self.sums[which] = self.stages[which][stage]


def chain_of(which, shape):
    chain = []
    for _, kind in ROUTES[which]:
        shape = half_shape(shape, kind)
        chain.append(shape)
    return chain


def head_lanes(first, shape):
    row = lax.broadcasted_iota(jnp.int32, shape, 0) - first
    column = lax.broadcasted_iota(jnp.int32, shape, 1)
    inside = (row >= 0) & (row < HEADS)
    inside &= (column >= row * HEAD_DIM) & (column < (row + 1) * HEAD_DIM)
    return inside.astype(jnp.float32)


def pass_body(keys, *refs):
    r = named(keys, refs)
    seq, opt = lax.axis_index("seq"), lax.axis_index("opt")
    bits, targets = partners(seq, opt)
    core, y = bits[CORE], bits[Y]
    opt_x = targets[X][1]
    ring = [((seq + step) % 8, opt) for step in range(1, 8)]
    micro, span = r.usable.shape[0], r.usable.shape[2]
    width = r.in_low.shape[1]
    lat_count, width_lat = r.latents.shape
    own = lat_count // 8
    scale = HEAD_DIM ** (-0.5)
    load = Loader(r.local)
    loads = [
        load.start(source, target)
        for source, target in (
            (r.w_key, r.f_key),
            (r.w_value, r.f_value),
            (r.w_query, r.f_query),
            (r.w_out, r.f_out),
            (r.w_up, r.f_up),
            (r.w_down, r.f_down),
        )
    ]
    clear(r.base)
    greet([targets[CORE], targets[X], *ring])
    courier = Courier(r.send, r.recv)

    def begin(full, rows):
        block = full.at[rows_at(opt * rows, rows)]
        half = full.at[rows_at(opt * rows + y * (rows // 2), rows // 2)]
        return [
            courier.send(half, half, targets[X]),
            courier.send(block, block, targets[CORE]),
        ]

    def relay(full, rows, state):
        state[0].wait_recv()
        half = full.at[rows_at(opt_x * rows + y * (rows // 2), rows // 2)]
        state.append(courier.send(half, half, targets[Y]))
        state.append(courier.send(half, half, targets[CORE]))

    def relay_more(full, rows, state):
        state[2].wait_recv()
        half = full.at[rows_at(opt_x * rows + (1 - y) * (rows // 2), rows // 2)]
        state.append(courier.send(half, half, targets[CORE]))

    def complete(state):
        for index in (1, 3, 4):
            state[index].wait_recv()

    def place(full, source):
        rows = source.shape[0]

        def body(step, carry):
            at = rows_at(step * 32, 32)
            full[rows_at(opt * rows + step * 32, 32), :] = low(source[at, :])
            return carry

        lax.fori_loop(0, rows // 32, body, 0)

    key_rows = r.f_key.shape[0]
    loads[0].wait()
    loads[1].wait()

    def place_pair(step, carry):
        at = rows_at(opt * key_rows + step * 32, 32)
        source = rows_at(step * 32, 32)
        r.pair_full[at, :width] = low(r.f_key[source, :])
        r.pair_full[at, width:] = low(r.f_value[source, :])
        return carry

    lax.fori_loop(0, key_rows // 32, place_pair, 0)
    pair_state = begin(r.pair_full, key_rows)

    def norm_in(step, carry):
        at = rows_at(step * 64, 64)
        hat, inverse = norm(wide(r.tokens[at, :]))
        r.in_hat[at, :] = hat
        r.in_inv[at, :] = inverse
        r.in_low[at, :] = low(hat * r.in_vectors[0:1, :] + r.in_vectors[1:2, :])
        return carry

    lax.fori_loop(0, r.in_low.shape[0] // 64, norm_in, 0)
    def norm_lat(step, carry):
        at = rows_at(step * 32, 32)
        hat, _ = norm(r.latents[at, :])
        r.lat_low[at, :] = low(hat * r.lat_vectors[0:1, :] + r.lat_vectors[1:2, :])
        return carry

    lax.fori_loop(0, lat_count // 32, norm_lat, 0)
    query_rows, out_rows, up_rows = (
        r.f_query.shape[0],
        r.f_out.shape[0],
        r.f_up.shape[0],
    )
    for index in range(4):

        @pl.when(opt == index)
        def _(index=index):
            r.lat_block[...] = r.lat_low[:, index * up_rows : (index + 1) * up_rows]

    for index, (full, staged) in enumerate(
        (
            (r.query_full, r.f_query),
            (r.out_full, r.f_out),
            (r.up_full, r.f_up),
            (r.down_full, r.f_down),
        )
    ):
        loads[2 + index].wait()
        place(full, staged)
    relay(r.pair_full, key_rows, pair_state)
    query_state = begin(r.query_full, query_rows)
    relay_more(r.pair_full, key_rows, pair_state)
    complete(pair_state)

    def project(step, carry):
        at = rows_at(step * 128, 128)
        r.pairs[at, :] = low(dot_nn(r.in_low[at, :], r.pair_full[...]))
        return carry

    lax.fori_loop(0, r.in_low.shape[0] // 128, project, 0)
    relay(r.query_full, query_rows, query_state)
    out_state = begin(r.out_full, out_rows)
    relay_more(r.query_full, query_rows, query_state)
    complete(query_state)

    def project_query(step, carry):
        at = rows_at(step * 128, 128)
        r.queries[at, :] = low(dot_nn(r.lat_low[at, :], r.query_full[...]))
        return carry

    lax.fori_loop(0, lat_count // 128, project_query, 0)

    relay(r.out_full, out_rows, out_state)
    up_state = begin(r.up_full, up_rows)
    to_owner = []
    for m in range(micro):
        at = slice(m * span, (m + 1) * span)
        usable = r.usable[m] > 0.5
        for h in range(HEADS):
            ch = slice(h * HEAD_DIM, (h + 1) * HEAD_DIM)
            ch_v = slice(width + h * HEAD_DIM, width + (h + 1) * HEAD_DIM)
            masked = jnp.where(
                usable, dot_nt(r.queries[:, ch], r.pairs[at, ch]) * scale, -1e30
            )
            top = jnp.max(masked, axis=1, keepdims=True)
            weights = jnp.exp(masked - top)
            sums = jnp.sum(weights, axis=1, keepdims=True)
            r.weights[m * HEADS + h] = weights
            lane = m * HEADS + h
            r.top[:, lane : lane + 1] = top
            r.lse[:, lane : lane + 1] = top + jnp.log(sums)
            r.part[m, :, ch] = low(dot_nn(low(weights), r.pairs[at, ch_v]) / sums)
        for target in ring:
            rows = rows_at(target[0] * own, own)
            to_owner.append(
                courier.send(r.part.at[m, rows], r.part_in.at[seq, m], target)
            )
        if m == 0:
            relay_more(r.out_full, out_rows, out_state)
            relay(r.up_full, up_rows, up_state)
            down_state = begin(r.down_full, up_rows)
    for target in ring:
        rows = rows_at(target[0] * own, own)
        to_owner.append(courier.send(r.lse.at[rows], r.lse_in.at[seq], target))
    mine = rows_at(seq * own, own)
    r.part_in[seq] = r.part[:, mine, :]
    r.lse_in[seq] = r.lse[mine, :]
    relay_more(r.up_full, up_rows, up_state)
    relay(r.down_full, up_rows, down_state)
    for moment, staged, slot in zip(
        (r.mom_query, r.mom_key, r.mom_value, r.mom_out, r.mom_up, r.mom_down),
        (r.f_query, r.f_key, r.f_value, r.f_out, r.f_up, r.f_down),
        SLOTS,
    ):

        @pl.when(seq == slot)
        def _(moment=moment, staged=staged):
            copy = pltpu.make_async_copy(moment, staged, r.moment_sem)
            copy.start()
            copy.wait()
            r.base[rows_at(opt * up_rows, staged.shape[0]), : staged.shape[1]] = low(
                0.95 * staged[...]
            )

    own_base = r.base.at[rows_at(opt * up_rows, up_rows)]
    base_across = courier.send(own_base, own_base, targets[X])
    base_beside = courier.send(own_base, own_base, targets[CORE])
    relay_more(r.down_full, up_rows, down_state)
    for copy in to_owner:
        copy.wait_recv()

    peak = r.lse_in[0]
    for peer in range(1, 8):
        peak = jnp.maximum(peak, r.lse_in[peer])
    total = jnp.exp(r.lse_in[0] - peak)
    for peer in range(1, 8):
        total = total + jnp.exp(r.lse_in[peer] - peak)
    lse_all = peak + jnp.log(total)
    spread_heads = [head_lanes(m * HEADS, (128, width)) for m in range(micro)]
    collect_heads = [head_lanes((micro + m) * HEADS, (128, width)) for m in range(micro)]
    for m in range(micro):
        rows = slice(m * own, (m + 1) * own)
        for peer in range(8):
            share = jnp.dot(
                jnp.exp(r.lse_in[peer] - lse_all),
                spread_heads[m],
                precision=highest,
                preferred_element_type=jnp.float32,
            ) * wide(r.part_in[peer, m])
            r.attended[rows, :] = share if peer == 0 else r.attended[rows, :] + share
    local_rows = rows_at(core * (micro * own), micro * own)
    att_low = low(r.attended[...])
    r.x_att[local_rows, :] = att_low
    back_rows = r.cotangent[...]
    r.x_cot[local_rows, :] = back_rows
    complete(out_state)
    own_latents = jnp.concatenate([r.latents[mine, :]] * micro, axis=0)
    r.hidden[...] = own_latents + dot_nn(att_low, r.out_full[...])
    mlp_hat, mlp_inv = norm(r.hidden[...])
    r.mlp_hat[...] = mlp_hat
    mlp_low = low(mlp_hat * r.lat_vectors[2:3, :] + r.lat_vectors[3:4, :])
    r.x_mlp[local_rows, :] = mlp_low
    complete(up_state)
    pre_act = dot_nn(mlp_low, r.up_full[...]) + r.lat_vectors[4:5, :]
    cdf = 0.5 * (1.0 + lax.erf(pre_act * 0.7071067811865476))
    act_low = low(pre_act * cdf)
    r.slope[...] = cdf + pre_act * jnp.exp(-0.5 * pre_act * pre_act) * 0.3989422804014327
    r.x_act[local_rows, :] = act_low
    complete(down_state)
    grad_pre = low(dot_nt(back_rows, r.down_full[...]) * r.slope[...])
    r.x_pre[local_rows, :] = grad_pre
    grad_mlp = dot_nt(grad_pre, r.up_full[...])
    mlp_hat = r.mlp_hat[...]
    r.vectors[...] = jnp.zeros_like(r.vectors)
    r.vectors[0:1, :] = jnp.sum(grad_mlp * mlp_hat, axis=0, keepdims=True)
    r.vectors[1:2, :] = jnp.sum(grad_mlp, axis=0, keepdims=True)
    r.vectors[2:3, :] = jnp.sum(wide(grad_pre), axis=0, keepdims=True)
    r.vectors[3:4, :] = jnp.sum(wide(back_rows), axis=0, keepdims=True)
    scaled = grad_mlp * r.lat_vectors[2:3, :]
    grad_hidden = wide(back_rows) + mlp_inv * (
        scaled
        - jnp.mean(scaled, axis=-1, keepdims=True)
        - mlp_hat * jnp.mean(scaled * mlp_hat, axis=-1, keepdims=True)
    )
    rest = grad_hidden[:own]
    for m in range(1, micro):
        rest = rest + grad_hidden[m * own : (m + 1) * own]
    r.rest[...] = low(rest)
    grad_branch = low(grad_hidden)
    r.x_branch[local_rows, :] = grad_branch
    grad_own = low(dot_nt(grad_branch, r.out_full[...]))
    products = wide(grad_own) * r.attended[...]
    back = jnp.where(
        lax.broadcasted_iota(jnp.int32, lse_all.shape, 1) < micro * HEADS, lse_all, 0.0
    )
    for m in range(micro):
        rows = slice(m * own, (m + 1) * own)
        r.grad_att[m, mine, :] = grad_own[rows]
        back = back + lax.dot_general(
            products[rows],
            collect_heads[m],
            (((1,), (1,)), ((), ())),
            precision=highest,
            preferred_element_type=jnp.float32,
        )
    r.back[mine, :] = back
    returns = []
    for target in ring:
        for view in (r.grad_att.at[:, mine], r.back.at[mine]):
            returns.append(courier.send(view, view, target))
    chip = []
    for array in (r.x_act, r.x_cot, r.x_mlp, r.x_pre, r.x_att, r.x_branch):
        view = array.at[local_rows]
        chip.append(courier.send(view, view, targets[CORE]))
    r.block_out[...] = low(
        r.hidden[...] + dot_nn(act_low, r.down_full[...]) + r.lat_vectors[5:6, :]
    )
    for copy in chip:
        copy.wait_recv()
    half = lanes_at(core * (width_lat // 2), width_lat // 2)
    for target, left, right in (
        (r.grad_down, r.x_act, r.x_cot),
        (r.grad_up, r.x_mlp, r.x_pre),
        (r.grad_out, r.x_att, r.x_branch),
    ):
        for tile in range(left.shape[1] // 128):
            cols = slice(tile * 128, (tile + 1) * 128)
            x_half, first = divmod(tile * 128, target.shape[1])
            target[x_half, first : first + 128, :] = low(dot_tn(left[:, cols], right[:, half]))
    halving = Halving(
        courier,
        bits,
        targets,
        {UP: r.grad_up, DOWN: r.grad_down, OUT: r.grad_out},
        {
            UP: (r.up_0, r.up_1, r.up_2, r.piece_up),
            DOWN: (r.down_0, r.down_1, r.down_2, r.piece_down),
            OUT: (r.out_0, r.out_1, r.out_2, r.piece_out),
        },
    )
    for which in (UP, DOWN, OUT):
        halving.give(which, 0)
    for copy in returns:
        copy.wait_recv()

    for h in range(HEADS):
        if h in POINTS:
            which, stage = POINTS[h]
            halving.take(which, stage)
            halving.give(which, stage + 1)
        ch = slice(h * HEAD_DIM, (h + 1) * HEAD_DIM)
        ch_v = slice(width + h * HEAD_DIM, width + (h + 1) * HEAD_DIM)
        grad_query = None
        for m in range(micro):
            at = slice(m * span, (m + 1) * span)
            lane = m * HEADS + h
            lane_in = (micro + m) * HEADS + h
            prob = r.weights[lane] * jnp.exp(
                r.top[:, lane : lane + 1] - r.back[:, lane : lane + 1]
            )
            grad_att = r.grad_att[m, :, ch]
            grad_prob = dot_nt(grad_att, r.pairs[at, ch_v])
            grad_scores = low(prob * (grad_prob - r.back[:, lane_in : lane_in + 1]))
            part = dot_nn(grad_scores, r.pairs[at, ch])
            grad_query = part if grad_query is None else grad_query + part
            r.grad_pairs[at, ch] = low(scale * dot_tn(grad_scores, r.queries[:, ch]))
            r.grad_pairs[at, ch_v] = low(dot_tn(low(prob), grad_att))
        r.grad_query[:, ch] = low(scale * grad_query)

    part_width = width // 2

    def pair_product(targets_two, which):
        for kind, target in enumerate(targets_two):
            cols = lanes_at(kind * width + which * part_width, part_width)
            right = r.grad_pairs[:, cols]
            for tile in range(width // TILE):
                rows = slice(tile * TILE, (tile + 1) * TILE)
                target[rows, :] = low(dot_tn(r.in_low[:, rows], right))

    base_across.wait_recv()
    other_base = r.base.at[rows_at(opt_x * up_rows, up_rows)]
    base_last = courier.send(other_base, other_base, targets[CORE])
    base_beside.wait_recv()
    pair_product((r.pair_other.at[0], r.pair_other.at[1]), 1 - core)
    pair_copy = courier.send(r.pair_other, r.pair_in, targets[CORE])
    for which in (UP, OUT, DOWN):
        halving.take(which, 2)
        halving.give(which, 3)
    pair_product((r.grad_key, r.grad_value), core)
    r.in_sums[...] = jnp.zeros_like(r.in_sums)

    def norm_in_back(step, carry):
        at = rows_at(step * 64, 64)
        grad_in = dot_nt(r.grad_pairs[at, :], r.pair_full[...])
        hat = r.in_hat[at, :]
        r.in_sums[0:1, :] = r.in_sums[0:1, :] + jnp.sum(grad_in * hat, axis=0, keepdims=True)
        r.in_sums[1:2, :] = r.in_sums[1:2, :] + jnp.sum(grad_in, axis=0, keepdims=True)
        scaled = grad_in * r.in_vectors[0:1, :]
        r.input_grad[at, :] = r.in_inv[at, :] * (
            scaled
            - jnp.mean(scaled, axis=-1, keepdims=True)
            - hat * jnp.mean(scaled * hat, axis=-1, keepdims=True)
        )
        return carry

    lax.fori_loop(0, r.in_low.shape[0] // 64, norm_in_back, 0)
    r.vectors[4:6, :width] = r.in_sums[0:2, :]
    base_last.wait_recv()
    pair_copy.wait_recv()
    add_into(r.grad_key, r.pair_in.at[0])
    add_into(r.grad_value, r.pair_in.at[1])
    for which in (UP, OUT, DOWN):
        halving.take(which, 3)
    courier.finish()


def run_pass(tokens, usable, cotangent, latents, lat_vectors, in_vectors, weights, moments):
    f32, bf16 = jnp.float32, jnp.bfloat16
    w_query, w_key, w_value, w_out, w_up, w_down = weights
    operands = dict(
        tokens=tokens,
        usable=usable,
        cotangent=cotangent,
        latents=latents,
        lat_vectors=lat_vectors,
        in_vectors=in_vectors,
        w_query=w_query,
        w_key=w_key,
        w_value=w_value,
        w_out=w_out,
        w_up=w_up,
        w_down=w_down,
        mom_query=moments[0],
        mom_key=moments[1],
        mom_value=moments[2],
        mom_out=moments[3],
        mom_up=moments[4],
        mom_down=moments[5],
    )
    count, width = tokens.shape
    micro, _, span = usable.shape
    lat_count, width_lat = latents.shape
    own = lat_count // 8
    rows = micro * own
    outputs = dict(
        block_out=((rows, width_lat), bf16),
        input_grad=((count, width), f32),
        grad_key=((width, width // 2), bf16),
        grad_value=((width, width // 2), bf16),
        grad_query=((lat_count, width), bf16),
        vectors=((8, width_lat), f32),
        rest=((own, width_lat), bf16),
        lat_low=((lat_count, width_lat), bf16),
        lat_block=((lat_count, width_lat // 4), bf16),
        query_full=((width_lat, width), bf16),
        base=((width_lat, width_lat), bf16),
    )
    scratch = dict(
        grad_up=((2, width_lat // 2, width_lat // 2), bf16),
        grad_down=((2, width_lat // 2, width_lat // 2), bf16),
        grad_out=((2, width // 2, width_lat // 2), bf16),
        f_query=(w_query.shape, f32),
        f_key=(w_key.shape, f32),
        f_value=(w_value.shape, f32),
        f_out=(w_out.shape, f32),
        f_up=(w_up.shape, f32),
        f_down=(w_down.shape, f32),
        pair_full=((width, 2 * width), bf16),
        out_full=((width, width_lat), bf16),
        up_full=((width_lat, width_lat), bf16),
        down_full=((width_lat, width_lat), bf16),
        in_low=((count, width), bf16),
        in_hat=((count, width), f32),
        in_inv=((count, 1), f32),
        in_sums=((8, width), f32),
        pairs=((count, 2 * width), bf16),
        queries=((lat_count, width), bf16),
        weights=((micro * HEADS, lat_count, span), f32),
        top=((lat_count, 128), f32),
        lse=((lat_count, 128), f32),
        part=((micro, lat_count, width), bf16),
        part_in=((8, micro, own, width), bf16),
        lse_in=((8, own, 128), f32),
        attended=((rows, width), f32),
        hidden=((rows, width_lat), f32),
        mlp_hat=((rows, width_lat), f32),
        slope=((rows, width_lat), f32),
        x_att=((2 * rows, width), bf16),
        x_branch=((2 * rows, width_lat), bf16),
        x_mlp=((2 * rows, width_lat), bf16),
        x_pre=((2 * rows, width_lat), bf16),
        x_act=((2 * rows, width_lat), bf16),
        x_cot=((2 * rows, width_lat), bf16),
        grad_att=((micro, lat_count, width), bf16),
        back=((lat_count, 128), f32),
        grad_pairs=((count, 2 * width), bf16),
        pair_other=((2, width, width // 2), bf16),
        pair_in=((2, width, width // 2), bf16),
    )
    for which, name in ((UP, "up"), (DOWN, "down"), (OUT, "out")):
        chain = chain_of(which, scratch["grad_" + name][0])
        for stage, shape in enumerate(chain[:-1]):
            scratch[f"{name}_{stage}"] = (shape, bf16)
        outputs["piece_" + name] = (chain[-1], bf16)
    copies = 5 * 5 + 7 * micro + 7 + 14 + 6 + 1 + 3 + 12
    sems = dict(
        send=pltpu.SemaphoreType.DMA((copies,)),
        recv=pltpu.SemaphoreType.DMA((copies,)),
        local=pltpu.SemaphoreType.DMA((6,)),
        moment_sem=pltpu.SemaphoreType.DMA,
    )
    keys = (*operands, *outputs, *scratch, *sems)
    vmem, anywhere = pl.BlockSpec(memory_space=pltpu.VMEM), pl.BlockSpec(memory_space=pl.ANY)
    results = pl.pallas_call(
        functools.partial(pass_body, keys),
        out_shape=[jax.ShapeDtypeStruct(*spec) for spec in outputs.values()],
        in_specs=[vmem] * 6 + [anywhere] * 12,
        out_specs=[vmem] * len(outputs),
        scratch_shapes=[*(pltpu.VMEM(*spec) for spec in scratch.values()), *sems.values()],
        compiler_params=pltpu.CompilerParams(
            collective_id=2, has_side_effects=True, vmem_limit_bytes=VMEM_LIMIT
        ),
        name="pass",
    )(*operands.values())
    return named(outputs, results)


def tail_body(keys, *refs):
    r = named(keys, refs)
    seq, opt = lax.axis_index("seq"), lax.axis_index("opt")
    bits, targets = partners(seq, opt)
    core, z0, z1, y, x = bits[CORE], bits[Z0], bits[Z1], bits[Y], bits[X]
    ring = [((seq + step) % 8, opt) for step in range(1, 8)]
    height = r.lat_block.shape[1]
    load = Loader(r.local)
    loads = [
        load.start(source, target)
        for source, target in (
            (r.base, r.h_base),
            (r.lat_low, r.h_lat_low),
            (r.query_full, r.h_query_full),
            (r.latents, r.h_latents),
        )
    ]
    clear(r.g_full.at[0])
    clear(r.g_full.at[1])
    beyond = [((seq + step) % 8, targets[X][1]) for step in range(8)]
    greet([targets[CORE], *ring, *beyond])
    courier = Courier(r.send, r.recv)
    sums = {UP: r.up, DOWN: r.down, OUT: r.out, KEY: r.key, VALUE: r.value, QUERY: r.query}
    halving = Halving(
        courier,
        bits,
        targets,
        sums,
        {
            KEY: (r.key_0, r.key_1, r.key_2, r.key_3),
            VALUE: (r.value_0, r.value_1, r.value_2, r.value_3),
            QUERY: (r.query_0, r.query_1, r.query_2, r.query_3, r.query_4),
        },
    )
    for which in (QUERY, KEY, VALUE):
        halving.give(which, 0)
    def piece_place(which, seq_from, x_from):
        bit_y, bit_z0, bit_z1 = seq_from % 2, (seq_from // 2) % 2, seq_from // 4
        high, mid = (bit_y, bit_z0) if which in Y_FIRST else (bit_z0, bit_y)
        rows = sums[which].shape[0]
        return rows_at(x_from * (2 * height) + high * height + (mid * 2 + bit_z1) * rows, rows)

    def piece_copy(index, which, seq_from, x_from, same):
        cols = sums[which].shape[1]
        place = piece_place(which, seq_from, x_from)
        return pltpu.make_async_remote_copy(
            src_ref=sums[which],
            dst_ref=r.g_full.at[core, place, pl.ds(0, cols)],
            send_sem=r.piece_send.at[index, 0 if same else 1],
            recv_sem=r.piece_recv.at[0 if same else 1, seq_from],
            device_id=(SLOTS[index], opt if same else targets[X][1]),
            device_id_type=MESH,
        )

    def offer(index, which):
        piece_copy(index, which, seq, x, False).start()

        @pl.when(seq != SLOTS[index])
        def _():
            piece_copy(index, which, seq, x, True).start()

        @pl.when(seq == SLOTS[index])
        def _():
            cols = sums[which].shape[1]
            r.g_full[core, piece_place(which, seq, x), :cols] = sums[which][...]

    owned = ((1, KEY), (2, VALUE), (3, OUT), (4, UP), (5, DOWN))
    for index, which in owned[2:]:
        offer(index, which)
    r.vectors_sum[...] = r.vectors[...]
    vector_copy = courier.send(r.vectors, r.vectors_in.at[0], targets[CORE])
    rest_width = r.rest.shape[1] // 2
    column = lanes_at(core * rest_width, rest_width)
    rest_copy = courier.send(
        r.rest.at[:, lanes_at((1 - core) * rest_width, rest_width)], r.rest_in.at[0], targets[CORE]
    )
    halving.take(QUERY, 0)
    halving.give(QUERY, 1)
    vector_copy.wait_recv()
    r.vectors_sum[...] = r.vectors_sum[...] + r.vectors_in[0]
    rest_copy.wait_recv()
    r.rest_sum[...] = low(wide(r.rest[:, column]) + wide(r.rest_in[0]))
    rest_copy = courier.send(r.rest_sum, r.rest_in.at[1], targets[X])
    for stage in range(4):
        axis = (X, Y, Z0, Z1)[stage]
        r.vectors_out[stage] = r.vectors_sum[...]
        vector_copy = courier.send(
            r.vectors_out.at[stage], r.vectors_in.at[stage + 1], targets[axis]
        )
        if stage > 0:
            rest_copy.wait_recv()
            if stage == 1:
                r.rest_all[z1, z0, y, :, column] = low(wide(r.rest_sum[...]) + wide(r.rest_in[1]))
            every = slice(None)
            lead = ((z1, z0, y), (every, z0, y), (every, every, y))[stage - 1]
            view = r.rest_all.at[(*lead, every, column)]
            rest_copy = courier.send(view, view, targets[(Z1, Z0, Y)[stage - 1]])
        for which in (QUERY, KEY, VALUE):
            own_stage = stage + 1 if which == QUERY else stage
            halving.take(which, own_stage)
            if stage < 3:
                halving.give(which, own_stage + 1)
        vector_copy.wait_recv()
        r.vectors_sum[...] = r.vectors_sum[...] + r.vectors_in[stage + 1]
    rest_copy.wait_recv()
    view = r.rest_all.at[:, :, :, :, column]
    rest_copy = courier.send(view, view, targets[CORE])

    for index, which in owned[:2]:
        offer(index, which)
    rows, width = sums[QUERY].shape
    query_column = lanes_at(core * width, width)
    start = (x * 8 + y * 4 + z0 * 2 + z1) * rows
    r.query_all[rows_at(start, rows), query_column] = sums[QUERY][...]
    view = r.query_all.at[rows_at(start, rows), query_column]
    query_copies = [courier.send(view, view, target) for target in ring]

    gathered = (r.g_up, r.g_down, r.g_key, r.g_value, r.g_out)
    full = (r.n_up, r.n_down, r.n_key, r.n_value, r.n_out)
    for which in range(5):
        high, mid = (y, z0) if which in Y_FIRST else (z0, y)
        rows = sums[which].shape[0]
        gathered[which][rows_at((high * 4 + mid * 2 + z1) * rows, rows), :] = sums[which][...]

    def gather(which, step):
        first_axis, last_axis = (Y, Z0) if which in Y_FIRST else (Z0, Y)
        high, mid = bits[first_axis], bits[last_axis]
        rows = sums[which].shape[0]
        if step < 3:
            base, count = ((high * 4 + mid * 2 + z1, 1), (high * 4 + mid * 2, 2), (high * 4, 4))[
                step
            ]
            source = target = gathered[which].at[rows_at(base * rows, count * rows)]
        else:
            cols = sums[which].shape[1]
            source = gathered[which].at[rows_at((1 - core) * (4 * rows), 4 * rows)]
            target = full[which].at[:, lanes_at(core * cols, cols)]
        return pltpu.make_async_remote_copy(
            src_ref=source,
            dst_ref=target,
            send_sem=r.gather_send.at[which, step],
            recv_sem=r.gather_recv.at[which, step],
            device_id=targets[(Z1, last_axis, first_axis, CORE)[step]],
            device_id_type=MESH,
        )

    for which in range(5):
        gather(which, 0).start()
    for copy in query_copies:
        copy.wait_recv()
    view = r.query_all.at[rows_at(x * (8 * sums[QUERY].shape[0]), 8 * sums[QUERY].shape[0]), query_column]
    courier.send(view, view, targets[X]).wait_recv()
    view = r.query_all.at[:, query_column]
    courier.send(view, view, targets[CORE]).wait_recv()
    rest_copy.wait_recv()

    for index, which in owned:

        @pl.when(seq == SLOTS[index])
        def _(index=index, which=which):
            for seq_from in range(8):
                if seq_from != SLOTS[index]:
                    piece_copy(index, which, seq_from, x, True).wait_recv()
                piece_copy(index, which, seq_from, 1 - x, False).wait_recv()

    beside = courier.send(r.g_full.at[core], r.g_full.at[core], targets[CORE])
    beside.wait_recv()
    for copy in loads:
        copy.wait()
    side = r.whole.shape[1]
    tiles = side // TILE
    big = (seq == SLOTS[4]) | (seq == SLOTS[5])
    small = (seq == SLOTS[0]) | (seq == SLOTS[1]) | (seq == SLOTS[2]) | (seq == SLOTS[3])
    both = 2 * width
    turned = r.out.shape[0] * 4
    r.total[0] = 0.0

    def joined(at, lanes, block):
        r.wide[at, lanes] = block
        r.total[0] = r.total[0] + jnp.sum(block * block)

    def over_tiles(body):
        def step(tile, carry):
            body(rows_at(tile * TILE, TILE), tile)
            return carry

        lax.fori_loop(0, tiles, step, 0)

    @pl.when(big)
    def _():
        def body(at, tile):
            for index in range(2):
                lanes = slice(index * (side // 2), (index + 1) * (side // 2))
                joined(at, lanes, wide(r.h_base[at, lanes]) + wide(r.g_full[index, at, :]))

        over_tiles(body)

    @pl.when((seq == SLOTS[1]) | (seq == SLOTS[2]))
    def _():
        def body(at, tile):
            for index in range(2):
                lanes = slice(index * width, (index + 1) * width)
                joined(at, lanes, wide(r.h_base[at, lanes]) + wide(r.g_full[index, at, :width]))

        over_tiles(body)

    @pl.when(seq == SLOTS[0])
    def _():
        def body(at, tile):
            lanes = slice(0, both)
            joined(
                at,
                lanes,
                wide(r.h_base[at, lanes])
                + dot_tn(r.h_lat_low[:, lanes_at(tile * TILE, TILE)], r.query_all[...]),
            )

        over_tiles(body)

    @pl.when(seq == SLOTS[3])
    def _():
        for block in range(4):
            at = slice(block * height, block * height + turned)
            for index in range(2):
                lanes = slice(index * (side // 2), (index + 1) * (side // 2))
                part = wide(r.h_base[at, lanes]) + wide(r.g_full[index, at, :])
                joined(lanes, slice(block * turned, (block + 1) * turned), part.T)

    scale = 1.0 / (jnp.sqrt(jnp.full((1, 1), r.total[0], jnp.float32)) + 1e-07)

    def normalise(cols):
        def body(at, tile):
            block = r.wide[at, :cols] * scale
            r.wide[at, :cols] = block
            r.whole[at, :cols] = low(block)

        over_tiles(body)

    def update(at, cols):
        block = coef_one * r.wide[at, :cols] + dot_nn(r.whole[at, :cols], r.poly[:cols, :cols])
        r.wide[at, :cols] = block
        r.whole[at, :cols] = low(block)

    def gathers(step, action):
        for which in range(5):
            action(gather(which, step))

    def gather_take(step):
        gathers(step, lambda copy: copy.wait_recv())

    def gather_give(step):
        gathers(step, lambda copy: copy.start())
        if step == 3:
            for which in range(5):
                rows, cols = gathered[which].shape
                full[which][:, lanes_at(core * cols, cols)] = gathered[which][
                    rows_at(core * (rows // 2), rows // 2), :
                ]

    outs = (r.o_query, r.o_key, r.o_value, r.o_out, r.o_up, r.o_down)
    z, depth = seq // 2, 4

    def copy(which, part, way):
        out = outs[which]
        cols = out.shape[1] * 4 // PARTS[which]
        rows = out.shape[0] // 4
        across = out.shape[1] // cols
        view = out.at[pl.ds(part // across * rows, rows), pl.ds(part % across * cols, cols)]
        return pltpu.make_async_remote_copy(
            src_ref=view,
            dst_ref=view,
            send_sem=r.spread_send.at[way, which * max(PARTS) + part],
            recv_sem=r.spread_recv.at[which * max(PARTS) + part],
            device_id=((seq + 2, opt), (seq - 2, opt), targets[Y])[way],
            device_id_type=MESH,
        )

    def for_ways(which, mine, action):
        slot_y, slot_z = SLOTS[which] % 2, SLOTS[which] // 2
        turn = (y == slot_y) & ((z == slot_z) if mine else (z != slot_z))
        on = (
            turn & (z >= slot_z) & (z < depth - 1),
            turn & (z <= slot_z) & (z > 0),
            turn,
        )
        for way in range(3):

            @pl.when(on[way])
            def _(way=way):
                action(way)

    def send_own(which):
        for part in range(PARTS[which]):
            if part >= AHEAD:
                for_ways(which, True, lambda way: copy(which, part - AHEAD, way).wait_send())
            for_ways(which, True, lambda way: copy(which, part, way).start())

    def pass_on(group, first, last):
        for part in range(first, last):
            for which in group:

                @pl.when((y == SLOTS[which] % 2) & (z != SLOTS[which] // 2))
                def _(which=which, part=part):
                    copy(which, part, 2).wait_recv()

                for_ways(which, False, lambda way: copy(which, part, way).start())

    def latent_gradients():
        r.lat_grads[...] = jnp.zeros_like(r.lat_grads)
        r.lat_grads[2:6, :] = r.vectors_sum[0:4, :]

        def latent_rows(step, carry):
            at = rows_at(step * 32, 32)
            hat, inverse = norm(r.h_latents[at, :])
            grad = dot_nt(r.query_all[at, :], r.h_query_full[...])
            r.lat_grads[0:1, :] = r.lat_grads[0:1, :] + jnp.sum(grad * hat, axis=0, keepdims=True)
            r.lat_grads[1:2, :] = r.lat_grads[1:2, :] + jnp.sum(grad, axis=0, keepdims=True)
            scaled = grad * r.lat_vectors[0:1, :]
            r.latent_grad[at, :] = wide(r.rest_all[step // 4, (step // 2) % 2, step % 2]) + inverse * (
                scaled
                - jnp.mean(scaled, axis=-1, keepdims=True)
                - hat * jnp.mean(scaled * hat, axis=-1, keepdims=True)
            )
            return carry

        lax.fori_loop(0, r.latents.shape[0] // 32, latent_rows, 0)
        r.query_grad[...] = dot_tn(r.lat_block[...], r.query_all[...])

    few, many = (0, 1, 2, 3), (4, 5)
    own_first = opt * height
    gather_take(0)
    gather_give(1)

    @pl.when(big)
    def _():
        normalise(side)

        def sweep(index, carry):
            @pl.when(index == 1)
            def _():
                gather_take(1)
                gather_give(2)

            @pl.when(index == 3)
            def _():
                pass_on(few, 0, 2)

            @pl.when(index == 4)
            def _():
                gather_take(2)
                gather_give(3)
                pass_on(few, 2, 4)

            polynomial(r.whole, r.gram, r.poly)

            @pl.when(index < 4)
            def _():
                update(slice(0, side), side)

            return carry

        lax.fori_loop(0, 5, sweep, 0)
        update(rows_at(own_first, height), side)

    @pl.when(small)
    def _():
        normalise(both)

        def sweep(index, carry):
            polynomial(r.whole.at[:, :both], r.gram.at[:both, :both], r.poly.at[:both, :both])
            update(slice(0, side), both)
            return carry

        lax.fori_loop(0, 5, sweep, 0)

    for which in few + many:

        @pl.when(seq == SLOTS[which])
        def _(which=which):
            rows, cols = outs[which].shape
            if which == 3:
                for block in range(4):

                    @pl.when(opt == block)
                    def _(block=block):
                        lanes = slice(block * rows, (block + 1) * rows)
                        outs[which][...] = low(wide(r.whole[:, lanes]).T)
            else:
                outs[which][...] = r.whole[rows_at(own_first, rows), :cols]

    @pl.when(jnp.logical_not(big))
    def _():
        gather_take(1)
        gather_give(2)
        for which in few:
            send_own(which)
        pass_on(few, 0, 4)
        gather_take(2)
        gather_give(3)

    for which in many:
        send_own(which)
    gather_take(3)
    latent_gradients()
    pass_on(many, 0, 8)
    for which in few + many:
        for part in range(PARTS[which]):

            @pl.when(y != SLOTS[which] % 2)
            def _(which=which, part=part):
                copy(which, part, 2).wait_recv()

    for which in few + many:
        for part in range(PARTS[which]):
            for_ways(which, False, lambda way: copy(which, part, way).wait_send())
            if part >= PARTS[which] - AHEAD:
                for_ways(which, True, lambda way: copy(which, part, way).wait_send())
    for index, which in owned:
        piece_copy(index, which, seq, x, False).wait_send()

        @pl.when(seq != SLOTS[index])
        def _(index=index, which=which):
            piece_copy(index, which, seq, x, True).wait_send()

    for step in range(4):
        gathers(step, lambda copy: copy.wait_send())
    courier.finish()


def run_tail(done, latents, lat_vectors, moments):
    f32, bf16 = jnp.float32, jnp.bfloat16
    mom_query, mom_key, mom_value, mom_out, mom_up, mom_down = moments
    width_lat = latents.shape[1]
    key, value = (
        grad.reshape(2, grad.shape[0] // 2, grad.shape[1])
        for grad in (done.grad_key, done.grad_value)
    )
    operands = dict(
        base=done.base,
        lat_low=done.lat_low,
        query_full=done.query_full,
        latents=latents,
        vectors=done.vectors,
        rest=done.rest,
        lat_block=done.lat_block,
        lat_vectors=lat_vectors,
        up=done.piece_up,
        down=done.piece_down,
        out=done.piece_out,
        key=key,
        value=value,
        query=done.grad_query,
    )
    outputs = dict(
        vectors_sum=(done.vectors.shape, f32),
        lat_grads=((8, width_lat), f32),
        latent_grad=(latents.shape, f32),
        query_grad=(mom_query.shape, f32),
        n_up=(mom_up.shape, bf16),
        n_down=(mom_down.shape, bf16),
        n_key=(mom_key.shape, bf16),
        n_value=(mom_value.shape, bf16),
        n_out=(mom_out.shape, bf16),
        o_query=(mom_query.shape, bf16),
        o_key=(mom_key.shape, bf16),
        o_value=(mom_value.shape, bf16),
        o_out=(mom_out.shape, bf16),
        o_up=(mom_up.shape, bf16),
        o_down=(mom_down.shape, bf16),
    )
    half_rest = (done.rest.shape[0], done.rest.shape[1] // 2)
    scratch = dict(
        h_base=(done.base.shape, bf16),
        h_lat_low=(done.lat_low.shape, bf16),
        h_query_full=(done.query_full.shape, bf16),
        h_latents=(latents.shape, f32),
        vectors_in=((5, *done.vectors.shape), f32),
        vectors_out=((4, *done.vectors.shape), f32),
        rest_in=((2, *half_rest), bf16),
        rest_sum=(half_rest, bf16),
        rest_all=((2, 2, 2, *done.rest.shape), bf16),
        query_all=(done.grad_query.shape, bf16),
        g_full=((2, width_lat, width_lat // 2), bf16),
        g_up=((width_lat // 2, width_lat // 2), bf16),
        g_down=((width_lat // 2, width_lat // 2), bf16),
        g_key=(key.shape[1:], bf16),
        g_value=(value.shape[1:], bf16),
        g_out=((2 * mom_out.shape[0], width_lat // 2), bf16),
        wide=((width_lat, width_lat), f32),
        whole=((width_lat, width_lat), bf16),
        gram=((width_lat, width_lat), bf16),
        poly=((width_lat, width_lat), bf16),
    )
    for which, name, array in (
        (KEY, "key", key),
        (VALUE, "value", value),
        (QUERY, "query", done.grad_query),
    ):
        for stage, shape in enumerate(chain_of(which, array.shape)):
            scratch[f"{name}_{stage}"] = (shape, bf16)
    copies = 48
    count = len(SLOTS) * max(PARTS)
    dma = pltpu.SemaphoreType.DMA
    sems = dict(
        send=dma((copies,)),
        recv=dma((copies,)),
        piece_send=dma((6, 2)),
        piece_recv=dma((2, 8)),
        gather_send=dma((5, 4)),
        gather_recv=dma((5, 4)),
        spread_send=dma((3, count)),
        spread_recv=dma((count,)),
        total=pltpu.SMEM((1,), f32),
        local=dma((4,)),
    )
    keys = (*operands, *outputs, *scratch, *sems)
    vmem, anywhere = pl.BlockSpec(memory_space=pltpu.VMEM), pl.BlockSpec(memory_space=pl.ANY)
    results = pl.pallas_call(
        functools.partial(tail_body, keys),
        out_shape=[jax.ShapeDtypeStruct(*spec) for spec in outputs.values()],
        in_specs=[anywhere] * 4 + [vmem] * (len(operands) - 4),
        out_specs=[vmem] * len(outputs),
        scratch_shapes=[*(pltpu.VMEM(*spec) for spec in scratch.values()), *sems.values()],
        compiler_params=pltpu.CompilerParams(
            collective_id=0, has_side_effects=True, vmem_limit_bytes=VMEM_LIMIT
        ),
        name="tail",
    )(*operands.values())
    return named(outputs, results)


def finish_body(keys, rates, *refs):
    r = named(keys, refs)
    count = len(rates)
    load = Loader(r.load_sem)
    into = lambda name, index: getattr(r, f"{name}{index}")
    loads = []
    for index in range(count):
        loads.append(
            [
                load.start(into(name, index), into("v" + name, index))
                for name in ("m", "g", "w", "o")
            ]
        )
    states = [
        load.start(source, target)
        for source, target in (
            (r.latents, r.vlatents),
            (r.first, r.vfirst),
            (r.second, r.vsecond),
            (r.grad, r.vgrad),
        )
    ]
    store = Loader(r.store_sem)
    stores = []

    def over_rows(ref, body):
        def step(index, carry):
            body(rows_at(index * 32, 32))
            return carry

        lax.fori_loop(0, ref.shape[0] // 32, step, 0)

    for index, (keep, rate) in enumerate(rates):
        moment, grad, weight, turn = (into("v" + name, index) for name in ("m", "g", "w", "o"))
        loads[index][0].wait()
        loads[index][1].wait()

        def new_moment(at, moment=moment, grad=grad):
            moment[at, :] = 0.95 * moment[at, :] + wide(grad[at, :])

        over_rows(moment, new_moment)
        stores.append(store.start(moment, into("nm", index)))
        loads[index][2].wait()
        loads[index][3].wait()

        def new_weight(at, weight=weight, turn=turn, keep=keep, rate=rate):
            weight[at, :] = keep * weight[at, :] - rate * wide(turn[at, :])

        over_rows(weight, new_weight)
        stores.append(store.start(weight, into("nw", index)))
    for copy in states:
        copy.wait()

    def new_latents(at):
        first, second, new = adam_update(
            r.vlatents[at, :], r.vgrad[at, :], r.vfirst[at, :], r.vsecond[at, :], 1.0, 0.1
        )
        r.vfirst[at, :], r.vsecond[at, :], r.vlatents[at, :] = first, second, new

    over_rows(r.vlatents, new_latents)
    for source, target in (
        (r.vfirst, r.nfirst),
        (r.vsecond, r.nsecond),
        (r.vlatents, r.nlatents),
    ):
        stores.append(store.start(source, target))
    r.lat_first_new[...], r.lat_second_new[...], r.lat_new[...] = adam_update(
        r.lat_vectors[...], r.lat_grads[:6, :], r.lat_first[...], r.lat_second[...], 0.6, 0.0
    )
    width = r.in_vectors.shape[1]
    r.in_first_new[...], r.in_second_new[...], r.in_new[...] = adam_update(
        r.in_vectors[...], r.vectors[4:6, :width], r.in_first[...], r.in_second[...], 0.6, 0.0
    )
    for copy in stores:
        copy.wait()


def run_finish(moments, gradients, masters, turns, latent_state, vector_state):
    f32 = jnp.float32
    fans = (D_LAT, E_IN, E_IN, OUT_FAN, D_LAT, D_LAT)
    sides = (D_LAT, E_IN, E_IN, D_LAT, D_LAT, D_LAT)
    rates = [
        (1.0 - 0.1 * fan ** (-0.5), fan ** (-0.5) * side**0.5) for fan, side in zip(fans, sides)
    ]
    large = {}
    for index, arrays in enumerate(zip(moments, gradients, masters, turns)):
        for name, array in zip(("m", "g", "w", "o"), arrays):
            large[f"{name}{index}"] = array
    large.update(latent_state)
    operands = {**large, **vector_state}
    outputs, scratch = {}, {}
    for index, moment in enumerate(moments):
        outputs[f"nm{index}"] = outputs[f"nw{index}"] = (moment.shape, f32)
    latents = latent_state["latents"].shape
    outputs.update(nfirst=(latents, f32), nsecond=(latents, f32), nlatents=(latents, f32))
    in_place = len(outputs)
    lat, inner = vector_state["lat_first"].shape, vector_state["in_first"].shape
    outputs.update(lat_first_new=(lat, f32), lat_second_new=(lat, f32), lat_new=(lat, f32))
    outputs.update(in_first_new=(inner, f32), in_second_new=(inner, f32), in_new=(inner, f32))
    for name, array in large.items():
        scratch["v" + name] = pltpu.VMEM(array.shape, array.dtype)
    scratch["load_sem"] = pltpu.SemaphoreType.DMA((len(large),))
    scratch["store_sem"] = pltpu.SemaphoreType.DMA((in_place,))
    vmem, anywhere = pl.BlockSpec(memory_space=pltpu.VMEM), pl.BlockSpec(memory_space=pl.ANY)
    results = pl.pallas_call(
        functools.partial(finish_body, (*operands, *outputs, *scratch), rates),
        out_shape=[jax.ShapeDtypeStruct(*spec) for spec in outputs.values()],
        in_specs=[anywhere] * len(large) + [vmem] * len(vector_state),
        out_specs=[anywhere] * in_place + [vmem] * 6,
        scratch_shapes=list(scratch.values()),
        compiler_params=pltpu.CompilerParams(vmem_limit_bytes=VMEM_LIMIT),
        name="finish",
    )(*operands.values())
    return named(outputs, results)


def adam_update(param, gradient, first, second, step_rate, decay):
    first_new = 0.9 * first + 0.1 * gradient
    second_new = 0.95 * second + 0.05 * gradient * gradient
    ratio = first_new / (1.0 - 0.9**STEP) / (jnp.sqrt(second_new / (1.0 - 0.95**STEP)) + 1e-08)
    return (first_new, second_new, param - step_rate * (ratio + decay * param))


def local_small(
    inputs,
    key_mask,
    lengths,
    cotangent,
    latents,
    lat_vectors,
    in_vectors,
    w_query,
    w_key,
    w_value,
    w_out,
    w_up,
    w_down,
    mom_query,
    mom_key,
    mom_value,
    mom_out,
    mom_up,
    mom_down,
    lat_first,
    lat_second,
    in_first,
    in_second,
    latent_first,
    latent_second,
):
    seq_index = lax.axis_index("seq")
    micro_count, _, span, width_in = inputs.shape
    lat_count, width_lat = latents.shape
    positions = seq_index * span + jnp.arange(span, dtype=jnp.int32)
    usable = (positions < lengths[:, :, None]) & ((key_mask == 1) | (positions == 0))
    masters = (w_query, w_key, w_value, w_out, w_up, w_down)
    moments = (mom_query, mom_key, mom_value, mom_out, mom_up, mom_down)
    done = run_pass(
        inputs.reshape(-1, width_in),
        usable.astype(jnp.float32),
        cotangent.reshape(-1, width_lat),
        latents,
        lat_vectors,
        in_vectors,
        masters,
        moments,
    )
    summed = run_tail(done, latents, lat_vectors, moments)
    gradients = (
        summed.query_grad,
        summed.n_key,
        summed.n_value,
        summed.n_out,
        summed.n_up,
        summed.n_down,
    )
    currents = (
        summed.o_query,
        summed.o_key,
        summed.o_value,
        summed.o_out,
        summed.o_up,
        summed.o_down,
    )
    new = run_finish(
        moments,
        gradients,
        masters,
        currents,
        dict(latents=latents, first=latent_first, second=latent_second, grad=summed.latent_grad),
        dict(
            lat_vectors=lat_vectors,
            lat_grads=summed.lat_grads,
            lat_first=lat_first,
            lat_second=lat_second,
            in_vectors=in_vectors,
            vectors=summed.vectors_sum,
            in_first=in_first,
            in_second=in_second,
        ),
    )
    return (
        done.block_out.reshape(cotangent.shape),
        done.input_grad.reshape(inputs.shape),
        new.nm0,
        new.nm1,
        new.nm2,
        new.nm3,
        new.nm4,
        new.nm5,
        new.nw0,
        new.nw1,
        new.nw2,
        new.nw3,
        new.nw4,
        new.nw5,
        new.lat_first_new,
        new.lat_second_new,
        new.lat_new,
        new.in_first_new,
        new.in_second_new,
        new.in_new,
        new.nfirst,
        new.nsecond,
        new.nlatents,
    )


def update_masters(masters, currents):
    fans = (D_LAT, E_IN, E_IN, OUT_FAN, D_LAT, D_LAT)
    sides = (D_LAT, E_IN, E_IN, D_LAT, D_LAT, D_LAT)
    new_masters = []
    for master, current, fan_in, long_side in zip(masters, currents, fans, sides):
        step_rate = fan_in ** (-0.5)
        new_masters.append(
            (1.0 - 0.1 * step_rate) * master
            - step_rate * long_side**0.5 * current.astype(jnp.float32)
        )
    return new_masters


def local(
    inputs,
    key_mask,
    lengths,
    cotangent,
    latents,
    lat_vectors,
    in_vectors,
    w_query,
    w_key,
    w_value,
    w_out,
    w_up,
    w_down,
    mom_query,
    mom_key,
    mom_value,
    mom_out,
    mom_up,
    mom_down,
    lat_first,
    lat_second,
    in_first,
    in_second,
    latent_first,
    latent_second,
):
    query_low, key_low, value_low, out_low, up_low, down_low = (
        lax.all_gather(w_query.astype(jnp.bfloat16), "opt", axis=0, tiled=True),
        lax.all_gather(w_key.astype(jnp.bfloat16), "opt", axis=0, tiled=True),
        lax.all_gather(w_value.astype(jnp.bfloat16), "opt", axis=0, tiled=True),
        lax.all_gather(w_out.astype(jnp.bfloat16), "opt", axis=0, tiled=True),
        lax.all_gather(w_up.astype(jnp.bfloat16), "opt", axis=0, tiled=True),
        lax.all_gather(w_down.astype(jnp.bfloat16), "opt", axis=0, tiled=True),
    )
    pair_low = jnp.concatenate([key_low, value_low], axis=1)
    seq_index = lax.axis_index("seq")
    seq_size = lax.axis_size("seq")
    opt_index = lax.axis_index("opt")
    opt_size = lax.axis_size("opt")
    micro_count, doc_local, span, width_in = inputs.shape
    lat_count, width_lat = latents.shape
    own_rows = lat_count // seq_size
    row_start = seq_index * own_rows
    score_scale = HEAD_DIM ** (-0.5)
    lat_normed, lat_hat, lat_inv = layer_norm(latents, lat_vectors[0], lat_vectors[1])
    lat_low = lat_normed.astype(jnp.bfloat16)
    query_rows = jnp.dot(lat_low, query_low, preferred_element_type=jnp.float32).astype(
        jnp.bfloat16
    )
    query_heads = query_rows.reshape(lat_count, HEADS, HEAD_DIM)
    own_latents = lax.dynamic_slice_in_dim(latents, row_start, own_rows, 0)
    positions = seq_index * span + jnp.arange(span, dtype=jnp.int32)
    grad_query_rows = jnp.zeros((lat_count, width_in), jnp.float32)
    grad_pair = jnp.zeros((width_in, 2 * width_in), jnp.float32)
    grad_out_w = jnp.zeros((width_in, width_lat), jnp.float32)
    grad_up_w = jnp.zeros((width_lat, width_lat), jnp.float32)
    grad_down_w = jnp.zeros((width_lat, width_lat), jnp.float32)
    mlp_gain = jnp.zeros((width_lat,), jnp.float32)
    mlp_shift = jnp.zeros((width_lat,), jnp.float32)
    bias_up = jnp.zeros((width_lat,), jnp.float32)
    bias_down = jnp.zeros((width_lat,), jnp.float32)
    in_gain = jnp.zeros((width_in,), jnp.float32)
    in_shift = jnp.zeros((width_in,), jnp.float32)
    latent_rest = jnp.zeros((own_rows, width_lat), jnp.float32)
    block_parts = []
    input_parts = []
    for micro_step in range(micro_count):
        tokens = inputs[micro_step]
        usable = (positions[None, :] < lengths[micro_step][:, None]) & (
            (key_mask[micro_step] == 1) | (positions[None, :] == 0)
        )
        in_normed, in_hat, in_inv = layer_norm(
            tokens.astype(jnp.float32), in_vectors[0], in_vectors[1]
        )
        in_low = in_normed.astype(jnp.bfloat16)
        pair_rows = jnp.einsum(
            "bse,ef->bsf", in_low, pair_low, preferred_element_type=jnp.float32
        ).astype(jnp.bfloat16)
        key_heads = pair_rows[:, :, :width_in].reshape(doc_local, span, HEADS, HEAD_DIM)
        value_heads = pair_rows[:, :, width_in:].reshape(doc_local, span, HEADS, HEAD_DIM)
        masked = masked_scores(query_heads, key_heads, usable, score_scale)
        row_max = lax.pmax(jnp.max(masked, axis=-1), "seq")
        weights = jnp.exp(masked - row_max[..., None])
        weights_low = weights.astype(jnp.bfloat16)
        summed, row_sum = (
            lax.psum(
                jnp.einsum(
                    "bhns,bshd->bnhd", weights_low, value_heads, preferred_element_type=jnp.float32
                ).astype(jnp.bfloat16),
                "seq",
            ).astype(jnp.float32),
            lax.psum(jnp.sum(weights, axis=-1).astype(jnp.bfloat16), "seq").astype(jnp.float32),
        )
        sum_heads = jnp.transpose(row_sum, (0, 2, 1))[..., None]
        attended = summed / sum_heads
        own_att = (
            lax.dynamic_slice_in_dim(attended, row_start, own_rows, 1)
            .reshape(doc_local, own_rows, width_in)
            .astype(jnp.bfloat16)
        )
        hidden = own_latents[None] + jnp.einsum(
            "bne,ef->bnf", own_att, out_low, preferred_element_type=jnp.float32
        )
        mlp_normed, mlp_hat, mlp_inv = layer_norm(hidden, lat_vectors[2], lat_vectors[3])
        mlp_low = mlp_normed.astype(jnp.bfloat16)
        pre_act = (
            jnp.einsum("bnf,fg->bng", mlp_low, up_low, preferred_element_type=jnp.float32)
            + lat_vectors[4]
        )
        activated, gelu_pull = jax.vjp(exact_gelu, pre_act)
        act_low = activated.astype(jnp.bfloat16)
        block_parts.append(
            (
                hidden
                + jnp.einsum("bng,gk->bnk", act_low, down_low, preferred_element_type=jnp.float32)
                + lat_vectors[5]
            ).astype(jnp.bfloat16)
        )
        back_rows = cotangent[micro_step]
        grad_down_w = grad_down_w + jnp.einsum(
            "bng,bnk->gk", act_low, back_rows, preferred_element_type=jnp.float32
        )
        bias_down = bias_down + jnp.sum(back_rows.astype(jnp.float32), axis=(0, 1))
        grad_act = jnp.einsum(
            "bnk,gk->bng", back_rows, down_low, preferred_element_type=jnp.float32
        )
        grad_pre = gelu_pull(grad_act)[0].astype(jnp.bfloat16)
        grad_up_w = grad_up_w + jnp.einsum(
            "bnf,bng->fg", mlp_low, grad_pre, preferred_element_type=jnp.float32
        )
        bias_up = bias_up + jnp.sum(grad_pre.astype(jnp.float32), axis=(0, 1))
        grad_mlp = jnp.einsum("bng,fg->bnf", grad_pre, up_low, preferred_element_type=jnp.float32)
        mlp_gain = mlp_gain + jnp.sum(grad_mlp * mlp_hat, axis=(0, 1))
        mlp_shift = mlp_shift + jnp.sum(grad_mlp, axis=(0, 1))
        grad_hidden = back_rows.astype(jnp.float32) + norm_back(
            grad_mlp, mlp_hat, mlp_inv, lat_vectors[2]
        )
        latent_rest = latent_rest + jnp.sum(grad_hidden, axis=0)
        grad_branch = grad_hidden.astype(jnp.bfloat16)
        grad_out_w = grad_out_w + jnp.einsum(
            "bne,bnf->ef", own_att, grad_branch, preferred_element_type=jnp.float32
        )
        grad_own = jnp.einsum(
            "bnf,ef->bne", grad_branch, out_low, preferred_element_type=jnp.float32
        ).astype(jnp.bfloat16)
        grad_att = (
            lax.all_gather(grad_own, "seq", axis=1, tiled=True)
            .astype(jnp.float32)
            .reshape(doc_local, lat_count, HEADS, HEAD_DIM)
        )
        grad_summed = (grad_att / sum_heads).astype(jnp.bfloat16)
        inner = jnp.transpose(jnp.sum(grad_att * attended, axis=-1) / sum_heads[..., 0], (0, 2, 1))
        grad_prob = jnp.einsum(
            "bnhd,bshd->bhns", grad_summed, value_heads, preferred_element_type=jnp.float32
        )
        grad_scores = (weights * (grad_prob - inner[..., None])).astype(jnp.bfloat16)
        grad_query_rows = grad_query_rows + score_scale * jnp.einsum(
            "bhns,bshd->nhd", grad_scores, key_heads, preferred_element_type=jnp.float32
        ).reshape(lat_count, width_in)
        grad_keys = (
            score_scale
            * jnp.einsum(
                "bhns,nhd->bshd", grad_scores, query_heads, preferred_element_type=jnp.float32
            )
        ).astype(jnp.bfloat16)
        grad_values = jnp.einsum(
            "bhns,bnhd->bshd", weights_low, grad_summed, preferred_element_type=jnp.float32
        ).astype(jnp.bfloat16)
        grad_pairs = jnp.concatenate(
            [
                grad_keys.reshape(doc_local, span, width_in),
                grad_values.reshape(doc_local, span, width_in),
            ],
            axis=-1,
        )
        grad_pair = grad_pair + jnp.einsum(
            "bse,bsf->ef", in_low, grad_pairs, preferred_element_type=jnp.float32
        )
        grad_in = jnp.einsum(
            "bsf,ef->bse", grad_pairs, pair_low, preferred_element_type=jnp.float32
        )
        in_gain = in_gain + jnp.sum(grad_in * in_hat, axis=(0, 1))
        in_shift = in_shift + jnp.sum(grad_in, axis=(0, 1))
        input_parts.append(norm_back(grad_in, in_hat, in_inv, in_vectors[0]))
    grad_query_w = jnp.matmul(lat_low.astype(jnp.float32).T, grad_query_rows, precision=highest)
    grad_lat = jnp.matmul(grad_query_rows, query_low.astype(jnp.float32).T, precision=highest)
    zero_index = jnp.zeros((), jnp.int32)
    latent_grad = norm_back(grad_lat, lat_hat, lat_inv, lat_vectors[0]) + lax.dynamic_update_slice(
        jnp.zeros_like(latents), latent_rest, (row_start, zero_index)
    )
    lat_vec_grad = jnp.stack(
        [
            jnp.sum(grad_lat * lat_hat, axis=0),
            jnp.sum(grad_lat, axis=0),
            mlp_gain,
            mlp_shift,
            bias_up,
            bias_down,
        ]
    )
    in_vec_grad = jnp.stack([in_gain, in_shift])
    weight_grads = (
        grad_query_w,
        grad_pair[:, :width_in],
        grad_pair[:, width_in:],
        grad_out_w,
        grad_up_w,
        grad_down_w,
    )
    masters = (w_query, w_key, w_value, w_out, w_up, w_down)
    moments = (mom_query, mom_key, mom_value, mom_out, mom_up, mom_down)
    first_here = jnp.where(seq_index == 0, 0.95, 0.0)
    with_moment = []
    for gradient, moment in zip(weight_grads, moments):
        start = opt_index * moment.shape[0]
        rows = lax.dynamic_slice_in_dim(gradient, start, moment.shape[0], 0) + first_here * moment
        with_moment.append(
            lax.dynamic_update_slice(gradient, rows, (start, zero_index)).astype(jnp.bfloat16)
        )
    summed_low = lax.psum(tuple(with_moment), ("seq", "opt"))
    lat_vec_sum, in_vec_sum, latent_sum = lax.psum(
        (lat_vec_grad, in_vec_grad, latent_grad), ("seq", "opt")
    )
    moments_new = [
        lax.dynamic_slice_in_dim(summed, opt_index * moment.shape[0], moment.shape[0], 0).astype(
            jnp.float32
        )
        for summed, moment in zip(summed_low, moments)
    ]

    def padded(index):
        def pick():
            matrix = summed_low[index].T if index == 3 else summed_low[index]
            return jnp.pad(
                matrix, ((0, width_lat - matrix.shape[0]), (0, width_lat - matrix.shape[1]))
            )

        return pick

    slot = seq_index % 8
    own_matrix = lax.switch(jnp.minimum(slot, 5), [padded(index) for index in range(6)])
    own_result = newton(own_matrix)
    own_result = lax.cond(slot == 3, lambda: own_result.T, lambda: own_result)
    mine = jnp.stack(
        [
            lax.dynamic_slice_in_dim(own_result, opt_index * height, width_lat // opt_size, 0)
            for height in (width_in // opt_size, width_lat // opt_size)
        ]
    )
    is_wide = (slot == 0) | (slot >= 4)
    mine = jnp.where(is_wide, mine[1], mine[0])
    spread = lax.all_gather(mine, "seq", axis=0, tiled=False)
    currents = [
        spread[index, : moment.shape[0], : moment.shape[1]].astype(jnp.float32)
        for index, moment in enumerate(moments)
    ]
    new_masters = update_masters(masters, currents)
    lat_m, lat_v, lat_p = adam_update(lat_vectors, lat_vec_sum, lat_first, lat_second, 0.6, 0.0)
    in_m, in_v, in_p = adam_update(in_vectors, in_vec_sum, in_first, in_second, 0.6, 0.0)
    latent_m, latent_v, latent_p = adam_update(
        latents, latent_sum, latent_first, latent_second, 1.0, 0.1
    )
    block_out = jnp.stack(block_parts)
    input_grad = jnp.stack(input_parts)
    return (
        block_out,
        input_grad,
        moments_new[0],
        moments_new[1],
        moments_new[2],
        moments_new[3],
        moments_new[4],
        moments_new[5],
        new_masters[0],
        new_masters[1],
        new_masters[2],
        new_masters[3],
        new_masters[4],
        new_masters[5],
        lat_m,
        lat_v,
        lat_p,
        in_m,
        in_v,
        in_p,
        latent_m,
        latent_v,
        latent_p,
    )


def solution(mesh):
    small = (mesh.shape["seq"], mesh.shape["opt"]) == (8, 4)
    return jax.shard_map(
        local_small if small else local,
        mesh=mesh,
        in_specs=(
            P(None, "opt", "seq", None),
            P(None, "opt", "seq"),
            P(None, "opt"),
            P(None, "opt", "seq", None),
            P(),
            P(),
            P(),
            P("opt", None),
            P("opt", None),
            P("opt", None),
            P("opt", None),
            P("opt", None),
            P("opt", None),
            P("opt", None),
            P("opt", None),
            P("opt", None),
            P("opt", None),
            P("opt", None),
            P("opt", None),
            P(),
            P(),
            P(),
            P(),
            P(),
            P(),
        ),
        out_specs=(
            P(None, "opt", "seq", None),
            P(None, "opt", "seq", None),
            P("opt", None),
            P("opt", None),
            P("opt", None),
            P("opt", None),
            P("opt", None),
            P("opt", None),
            P("opt", None),
            P("opt", None),
            P("opt", None),
            P("opt", None),
            P("opt", None),
            P("opt", None),
            P(),
            P(),
            P(),
            P(),
            P(),
            P(),
            P(),
            P(),
            P(),
        ),
        check_vma=False,
    )
```

```python
import functools
import types

import jax
import jax.numpy as jnp
from jax import lax
from jax.experimental import pallas as pl
from jax.experimental.pallas import tpu as pltpu
from jax.sharding import PartitionSpec as P

D_LAT = 1280
HEADS = 8
HEAD_DIM = 96
E_IN = 768
STEP = 10
OUT_FAN = 4
TILE = 256
PARTS = (4, 4, 4, 4, 8, 8)
AHEAD = 2
POINTS = {1: (0, 0), 2: (4, 0), 3: (1, 0), 5: (0, 1), 6: (4, 1), 7: (1, 1)}
VMEM_LIMIT = 60 * 2**20
MESH = pl.DeviceIdType.MESH


highest = lax.Precision.HIGHEST
coef_one = 3.4445
coef_two = -4.775
coef_three = 2.0315


def layer_norm(values, scale_vec, offset):
    center = jnp.mean(values, axis=-1, keepdims=True)
    shifted = values - center
    inverse = lax.rsqrt(jnp.mean(shifted * shifted, axis=-1, keepdims=True) + 1e-05)
    normal_hat = shifted * inverse
    return (normal_hat * scale_vec + offset, normal_hat, inverse)


def norm_back(grad_out, normal_hat, inverse, scale_vec):
    scaled = grad_out * scale_vec
    return inverse * (
        scaled
        - jnp.mean(scaled, axis=-1, keepdims=True)
        - normal_hat * jnp.mean(scaled * normal_hat, axis=-1, keepdims=True)
    )


def exact_gelu(values):
    return jax.nn.gelu(values, approximate=False)


def masked_scores(query_heads, key_heads, usable, score_scale):
    scores = (
        jnp.einsum("nhd,bshd->bhns", query_heads, key_heads, preferred_element_type=jnp.float32)
        * score_scale
    )
    return jnp.where(usable[:, None, None, :], scores, -1e30)


def polynomial(low, gram, poly):
    side_tiles = gram.shape[0] // TILE

    def mirror(target, block, i):
        own = slice(i * TILE, (i + 1) * TILE)
        target[own, i * TILE :] = block
        for j in range(i + 1, side_tiles):
            part = block[:, (j - i) * TILE : (j - i + 1) * TILE]
            target[j * TILE : (j + 1) * TILE, own] = part.T

    for i in range(side_tiles):
        own = slice(i * TILE, (i + 1) * TILE)
        block = lax.dot_general(
            low[:, own],
            low[:, i * TILE :],
            (((0,), (0,)), ((), ())),
            preferred_element_type=jnp.float32,
        )
        mirror(gram, block.astype(jnp.bfloat16), i)
    for i in range(side_tiles):
        own = slice(i * TILE, (i + 1) * TILE)
        block = coef_three * jnp.dot(
            gram[own, :], gram[:, i * TILE :], preferred_element_type=jnp.float32
        ) + coef_two * gram[own, i * TILE :].astype(jnp.float32)
        mirror(poly, block.astype(jnp.bfloat16), i)


def newton_body(rows_ref, out_ref, wide, low, gram, poly, total):
    count, side = rows_ref.shape
    row_tiles = count // TILE
    total[0] = 0.0

    def add_squares(tile, carry):
        block = rows_ref[pl.ds(tile * TILE, TILE), :].astype(jnp.float32)
        total[0] = total[0] + jnp.sum(block * block)
        return carry

    lax.fori_loop(0, row_tiles, add_squares, 0)
    scale = 1.0 / (jnp.sqrt(jnp.full((1, 1), total[0], jnp.float32)) + 1e-07)

    def normalise(tile, carry):
        block = rows_ref[pl.ds(tile * TILE, TILE), :].astype(jnp.float32) * scale
        wide[pl.ds(tile * TILE, TILE), :] = block
        low[pl.ds(tile * TILE, TILE), :] = block.astype(jnp.bfloat16)
        return carry

    lax.fori_loop(0, row_tiles, normalise, 0)

    def sweep(index, carry):
        polynomial(low, gram, poly)

        def update(tile, inner):
            rows = pl.ds(tile * TILE, TILE)
            block = coef_one * wide[rows, :] + jnp.dot(
                low[rows, :], poly[...], preferred_element_type=jnp.float32
            )
            wide[rows, :] = block
            low[rows, :] = block.astype(jnp.bfloat16)
            return inner

        lax.fori_loop(0, row_tiles, update, 0)
        return carry

    lax.fori_loop(0, 5, sweep, 0)
    out_ref[...] = low[...]


def newton(rows):
    shape = rows.shape
    return pl.pallas_call(
        newton_body,
        out_shape=jax.ShapeDtypeStruct(shape, jnp.bfloat16),
        in_specs=[pl.BlockSpec(memory_space=pltpu.VMEM)],
        out_specs=pl.BlockSpec(memory_space=pltpu.VMEM),
        scratch_shapes=[
            pltpu.VMEM(shape, jnp.float32),
            pltpu.VMEM(shape, jnp.bfloat16),
            pltpu.VMEM((shape[1], shape[1]), jnp.bfloat16),
            pltpu.VMEM((shape[1], shape[1]), jnp.bfloat16),
            pltpu.SMEM((1,), jnp.float32),
        ],
        compiler_params=pltpu.CompilerParams(vmem_limit_bytes=60 * 2**20),
        name="newton",
    )(rows)


CORE, X, Y, Z0, Z1 = range(5)
LEAD, ROWS, COLS = range(3)
UP, DOWN, KEY, VALUE, OUT, QUERY = range(6)
ROUTES = (
    ((Y, ROWS), (Z0, ROWS), (Z1, ROWS)),
    ((Z0, ROWS), (Y, ROWS), (Z1, ROWS)),
    ((X, LEAD), (Y, ROWS), (Z0, ROWS), (Z1, ROWS)),
    ((Z0, ROWS), (X, LEAD), (Y, ROWS), (Z1, ROWS)),
    ((Y, ROWS), (Z0, ROWS), (Z1, ROWS)),
    ((CORE, COLS), (X, ROWS), (Y, ROWS), (Z0, ROWS), (Z1, ROWS)),
)
Y_FIRST = (UP, KEY, OUT)
SLOTS = (3, 0, 7, 4, 2, 5)


def partners(seq, opt):
    bits = (opt % 2, opt // 2, seq % 2, (seq // 2) % 2, seq // 4)
    steps = ((0, 1), (0, 2), (1, 0), (2, 0), (4, 0))
    targets = [
        (seq + (1 - 2 * bit) * along_seq, opt + (1 - 2 * bit) * along_opt)
        for bit, (along_seq, along_opt) in zip(bits, steps)
    ]
    return bits, targets


def greet(targets):
    barrier = pltpu.get_barrier_semaphore()
    for target in targets:
        pl.semaphore_signal(barrier, inc=1, device_id=target, device_id_type=MESH)
    pl.semaphore_wait(barrier, len(targets))


class Courier:
    def __init__(self, send_sem, recv_sem):
        self.send_sem, self.recv_sem, self.started = send_sem, recv_sem, []

    def send(self, source, target_ref, device):
        index = len(self.started)
        copy = pltpu.make_async_remote_copy(
            src_ref=source,
            dst_ref=target_ref,
            send_sem=self.send_sem.at[index],
            recv_sem=self.recv_sem.at[index],
            device_id=device,
            device_id_type=MESH,
        )
        copy.start()
        self.started.append(copy)
        return copy

    def finish(self):
        for copy in self.started:
            copy.wait_send()


class Loader:
    def __init__(self, sem):
        self.sem, self.count = sem, 0

    def start(self, source, target):
        copy = pltpu.make_async_copy(source, target, self.sem.at[self.count])
        self.count += 1
        copy.start()
        return copy


def rows_at(start, count, unit=16):
    return pl.ds(pl.multiple_of(start, unit), count)


def lanes_at(start, count):
    return pl.ds(pl.multiple_of(start, 128), count)


def clear(ref):
    def body(step, carry):
        ref[rows_at(step * 32, 32), :] = jnp.zeros((32, ref.shape[1]), ref.dtype)
        return carry

    lax.fori_loop(0, ref.shape[0] // 32, body, 0)


def dot_nn(left, right):
    return jnp.dot(left, right, preferred_element_type=jnp.float32)


def dot_nt(left, right):
    return lax.dot_general(
        left, right, (((1,), (1,)), ((), ())), preferred_element_type=jnp.float32
    )


def dot_tn(left, right):
    return lax.dot_general(
        left, right, (((0,), (0,)), ((), ())), preferred_element_type=jnp.float32
    )


def named(keys, refs):
    return types.SimpleNamespace(**dict(zip(keys, refs)))


def low(values):
    return values.astype(jnp.bfloat16)


def wide(values):
    return values.astype(jnp.float32)


def norm(values):
    shifted = values - jnp.mean(values, axis=-1, keepdims=True)
    inverse = lax.rsqrt(jnp.mean(shifted * shifted, axis=-1, keepdims=True) + 1e-05)
    return shifted * inverse, inverse


def cut(ref, kind, bit):
    if kind == LEAD:
        return ref.at[bit]
    rows, cols = ref.shape[-2:]
    lead = (slice(None),) * (len(ref.shape) - 2)
    if kind == ROWS:
        return ref.at[(*lead, rows_at(bit * (rows // 2), rows // 2), slice(None))]
    return ref.at[(*lead, slice(None), lanes_at(bit * (cols // 2), cols // 2))]


def half_shape(shape, kind):
    if kind == LEAD:
        return shape[1:]
    if kind == ROWS:
        return (*shape[:-2], shape[-2] // 2, shape[-1])
    return (*shape[:-1], shape[-1] // 2)


def add_into(total, term):
    def body(step, carry):
        at = rows_at(step * 16, 16)
        for lead in range(total.shape[0]) if len(total.shape) == 3 else (None,):
            where = (at, slice(None)) if lead is None else (lead, at, slice(None))
            total[where] = low(wide(total[where]) + wide(term[where]))
        return carry

    lax.fori_loop(0, total.shape[-2] // 16, body, 0)


class Halving:
    def __init__(self, courier, bits, targets, sums, stages):
        self.courier, self.bits, self.targets = courier, bits, targets
        self.sums, self.stages, self.pending = sums, stages, {}

    def give(self, which, stage):
        axis, kind = ROUTES[which][stage]
        self.pending[which] = self.courier.send(
            cut(self.sums[which], kind, 1 - self.bits[axis]),
            self.stages[which][stage],
            self.targets[axis],
        )

    def take(self, which, stage):
        axis, kind = ROUTES[which][stage]
        self.pending[which].wait_recv()
        add_into(self.stages[which][stage], cut(self.sums[which], kind, self.bits[axis]))
        self.sums[which] = self.stages[which][stage]


def chain_of(which, shape):
    chain = []
    for _, kind in ROUTES[which]:
        shape = half_shape(shape, kind)
        chain.append(shape)
    return chain


def head_lanes(first, shape):
    row = lax.broadcasted_iota(jnp.int32, shape, 0) - first
    column = lax.broadcasted_iota(jnp.int32, shape, 1)
    inside = (row >= 0) & (row < HEADS)
    inside &= (column >= row * HEAD_DIM) & (column < (row + 1) * HEAD_DIM)
    return inside.astype(jnp.float32)


def pass_body(keys, *refs):
    r = named(keys, refs)
    seq, opt = lax.axis_index("seq"), lax.axis_index("opt")
    bits, targets = partners(seq, opt)
    core, y = bits[CORE], bits[Y]
    opt_x = targets[X][1]
    ring = [((seq + step) % 8, opt) for step in range(1, 8)]
    micro, span = r.usable.shape[0], r.usable.shape[2]
    width = r.in_low.shape[1]
    lat_count, width_lat = r.latents.shape
    own = lat_count // 8
    scale = HEAD_DIM ** (-0.5)
    load = Loader(r.local)
    loads = [
        load.start(source, target)
        for source, target in (
            (r.w_key, r.f_key),
            (r.w_value, r.f_value),
            (r.w_query, r.f_query),
            (r.w_out, r.f_out),
            (r.w_up, r.f_up),
            (r.w_down, r.f_down),
        )
    ]
    clear(r.base)
    greet([targets[CORE], targets[X], *ring])
    courier = Courier(r.send, r.recv)

    def begin(full, rows, axis):
        block = full.at[rows_at(opt * rows, rows)]
        half = full.at[rows_at(opt * rows + bits[axis] * (rows // 2), rows // 2)]
        return [
            courier.send(half, half, targets[X]),
            courier.send(block, block, targets[CORE]),
        ]

    def relay(full, rows, axis, state):
        state[0].wait_recv()
        half = full.at[rows_at(opt_x * rows + bits[axis] * (rows // 2), rows // 2)]
        state.append(courier.send(half, half, targets[axis]))
        state.append(courier.send(half, half, targets[CORE]))

    def relay_more(full, rows, axis, state):
        state[2].wait_recv()
        half = full.at[rows_at(opt_x * rows + (1 - bits[axis]) * (rows // 2), rows // 2)]
        state.append(courier.send(half, half, targets[CORE]))

    def complete(state):
        for index in (1, 3, 4):
            state[index].wait_recv()

    def place(full, source):
        rows = source.shape[0]

        def body(step, carry):
            at = rows_at(step * 32, 32)
            full[rows_at(opt * rows + step * 32, 32), :] = low(source[at, :])
            return carry

        lax.fori_loop(0, rows // 32, body, 0)

    key_rows = r.f_key.shape[0]
    loads[0].wait()
    loads[1].wait()

    def place_pair(step, carry):
        at = rows_at(opt * key_rows + step * 32, 32)
        source = rows_at(step * 32, 32)
        r.pair_full[at, :width] = low(r.f_key[source, :])
        r.pair_full[at, width:] = low(r.f_value[source, :])
        return carry

    lax.fori_loop(0, key_rows // 32, place_pair, 0)
    pair_state = begin(r.pair_full, key_rows, Y)

    def norm_in(step, carry):
        at = rows_at(step * 64, 64)
        hat, inverse = norm(wide(r.tokens[at, :]))
        r.in_hat[at, :] = hat
        r.in_inv[at, :] = inverse
        r.in_low[at, :] = low(hat * r.in_vectors[0:1, :] + r.in_vectors[1:2, :])
        return carry

    lax.fori_loop(0, r.in_low.shape[0] // 64, norm_in, 0)
    def norm_lat(step, carry):
        at = rows_at(step * 32, 32)
        hat, _ = norm(r.latents[at, :])
        r.lat_low[at, :] = low(hat * r.lat_vectors[0:1, :] + r.lat_vectors[1:2, :])
        return carry

    lax.fori_loop(0, lat_count // 32, norm_lat, 0)
    query_rows, out_rows, up_rows = (
        r.f_query.shape[0],
        r.f_out.shape[0],
        r.f_up.shape[0],
    )
    for index in range(4):

        @pl.when(opt == index)
        def _(index=index):
            r.lat_block[...] = r.lat_low[:, index * up_rows : (index + 1) * up_rows]

    for index, (full, staged) in enumerate(
        (
            (r.query_full, r.f_query),
            (r.out_full, r.f_out),
            (r.up_full, r.f_up),
            (r.down_full, r.f_down),
        )
    ):
        loads[2 + index].wait()
        place(full, staged)
    relay(r.pair_full, key_rows, Y, pair_state)
    query_state = begin(r.query_full, query_rows, Z0)
    relay(r.query_full, query_rows, Z0, query_state)
    out_state = begin(r.out_full, out_rows, Y)
    relay_more(r.pair_full, key_rows, Y, pair_state)
    complete(pair_state)

    def project(step, carry):
        at = rows_at(step * 256, 256)
        r.pairs[at, :] = low(dot_nn(r.in_low[at, :], r.pair_full[...]))
        return carry

    lax.fori_loop(0, r.in_low.shape[0] // 256, project, 0)
    relay(r.out_full, out_rows, Y, out_state)
    up_state = begin(r.up_full, up_rows, Z0)
    relay_more(r.query_full, query_rows, Z0, query_state)
    complete(query_state)

    def project_query(step, carry):
        at = rows_at(step * 128, 128)
        r.queries[at, :] = low(dot_nn(r.lat_low[at, :], r.query_full[...]))
        return carry

    lax.fori_loop(0, lat_count // 128, project_query, 0)

    local_rows = rows_at(opt * (micro * own), micro * own)
    shared = []

    def hand_over(array):
        view = array.at[local_rows]
        shared.append(
            (array, courier.send(view, view, targets[X]), courier.send(view, view, targets[CORE]))
        )

    back_rows = r.cotangent[...]
    r.x_cot[local_rows, :] = back_rows

    to_owner = []
    for m in range(micro):
        at = slice(m * span, (m + 1) * span)
        usable = r.usable[m] > 0.5
        for h in range(HEADS):
            ch = slice(h * HEAD_DIM, (h + 1) * HEAD_DIM)
            ch_v = slice(width + h * HEAD_DIM, width + (h + 1) * HEAD_DIM)
            masked = jnp.where(
                usable, dot_nt(r.queries[:, ch], r.pairs[at, ch]) * scale, -1e30
            )
            top = jnp.max(masked, axis=1, keepdims=True)
            weights = jnp.exp(masked - top)
            sums = jnp.sum(weights, axis=1, keepdims=True)
            r.weights[m * HEADS + h] = weights
            lane = m * HEADS + h
            r.top[:, lane : lane + 1] = top
            r.lse[:, lane : lane + 1] = top + jnp.log(sums)
            r.part[m, :, ch] = low(dot_nn(low(weights), r.pairs[at, ch_v]) / sums)
        for target in ring:
            rows = rows_at(target[0] * own, own)
            to_owner.append(
                courier.send(r.part.at[m, rows], r.part_in.at[seq, m], target)
            )
        if m == 0:
            relay(r.up_full, up_rows, Z0, up_state)
            down_state = begin(r.down_full, up_rows, Y)
            relay_more(r.out_full, out_rows, Y, out_state)
    for target in ring:
        rows = rows_at(target[0] * own, own)
        to_owner.append(courier.send(r.lse.at[rows], r.lse_in.at[seq], target))
    mine = rows_at(seq * own, own)
    r.part_in[seq] = r.part[:, mine, :]
    r.lse_in[seq] = r.lse[mine, :]
    relay(r.down_full, up_rows, Y, down_state)
    hand_over(r.x_cot)
    relay_more(r.up_full, up_rows, Z0, up_state)
    relay_more(r.down_full, up_rows, Y, down_state)
    for copy in to_owner:
        copy.wait_recv()

    peak = r.lse_in[0]
    for peer in range(1, 8):
        peak = jnp.maximum(peak, r.lse_in[peer])
    total = jnp.exp(r.lse_in[0] - peak)
    for peer in range(1, 8):
        total = total + jnp.exp(r.lse_in[peer] - peak)
    lse_all = peak + jnp.log(total)
    spread_heads = [head_lanes(m * HEADS, (128, width)) for m in range(micro)]
    collect_heads = [head_lanes((micro + m) * HEADS, (128, width)) for m in range(micro)]
    for m in range(micro):
        rows = slice(m * own, (m + 1) * own)
        for peer in range(8):
            share = jnp.dot(
                jnp.exp(r.lse_in[peer] - lse_all),
                spread_heads[m],
                precision=highest,
                preferred_element_type=jnp.float32,
            ) * wide(r.part_in[peer, m])
            r.attended[rows, :] = share if peer == 0 else r.attended[rows, :] + share
    att_low = low(r.attended[...])
    r.x_att[local_rows, :] = att_low
    hand_over(r.x_att)
    back_rows = r.cotangent[...]
    complete(out_state)
    own_latents = jnp.concatenate([r.latents[mine, :]] * micro, axis=0)
    r.hidden[...] = own_latents + dot_nn(att_low, r.out_full[...])
    mlp_hat, mlp_inv = norm(r.hidden[...])
    r.mlp_hat[...] = mlp_hat
    mlp_low = low(mlp_hat * r.lat_vectors[2:3, :] + r.lat_vectors[3:4, :])
    r.x_mlp[local_rows, :] = mlp_low
    hand_over(r.x_mlp)
    complete(up_state)
    pre_act = dot_nn(mlp_low, r.up_full[...]) + r.lat_vectors[4:5, :]
    cdf = 0.5 * (1.0 + lax.erf(pre_act * 0.7071067811865476))
    act_low = low(pre_act * cdf)
    r.slope[...] = cdf + pre_act * jnp.exp(-0.5 * pre_act * pre_act) * 0.3989422804014327
    r.x_act[local_rows, :] = act_low
    hand_over(r.x_act)
    complete(down_state)
    grad_pre = low(dot_nt(back_rows, r.down_full[...]) * r.slope[...])
    r.x_pre[local_rows, :] = grad_pre
    hand_over(r.x_pre)
    grad_mlp = dot_nt(grad_pre, r.up_full[...])
    mlp_hat = r.mlp_hat[...]
    r.vectors[...] = jnp.zeros_like(r.vectors)
    r.vectors[0:1, :] = jnp.sum(grad_mlp * mlp_hat, axis=0, keepdims=True)
    r.vectors[1:2, :] = jnp.sum(grad_mlp, axis=0, keepdims=True)
    r.vectors[2:3, :] = jnp.sum(wide(grad_pre), axis=0, keepdims=True)
    r.vectors[3:4, :] = jnp.sum(wide(back_rows), axis=0, keepdims=True)
    scaled = grad_mlp * r.lat_vectors[2:3, :]
    grad_hidden = wide(back_rows) + mlp_inv * (
        scaled
        - jnp.mean(scaled, axis=-1, keepdims=True)
        - mlp_hat * jnp.mean(scaled * mlp_hat, axis=-1, keepdims=True)
    )
    rest = grad_hidden[:own]
    for m in range(1, micro):
        rest = rest + grad_hidden[m * own : (m + 1) * own]
    r.rest[...] = low(rest)
    grad_branch = low(grad_hidden)
    r.x_branch[local_rows, :] = grad_branch
    hand_over(r.x_branch)
    grad_own = low(dot_nt(grad_branch, r.out_full[...]))
    products = wide(grad_own) * r.attended[...]
    back = jnp.where(
        lax.broadcasted_iota(jnp.int32, lse_all.shape, 1) < micro * HEADS, lse_all, 0.0
    )
    for m in range(micro):
        rows = slice(m * own, (m + 1) * own)
        r.grad_att[m, mine, :] = grad_own[rows]
        back = back + lax.dot_general(
            products[rows],
            collect_heads[m],
            (((1,), (1,)), ((), ())),
            precision=highest,
            preferred_element_type=jnp.float32,
        )
    r.back[mine, :] = back
    returns = []
    for target in ring:
        for view in (r.grad_att.at[:, mine], r.back.at[mine]):
            returns.append(courier.send(view, view, target))
    r.block_out[...] = low(
        r.hidden[...] + dot_nn(act_low, r.down_full[...]) + r.lat_vectors[5:6, :]
    )
    passed = []
    for array, across, _ in shared:
        across.wait_recv()
        view = array.at[rows_at(opt_x * (micro * own), micro * own)]
        passed.append(courier.send(view, view, targets[CORE]))
    for _, _, beside in shared:
        beside.wait_recv()
    for copy in passed:
        copy.wait_recv()
    half = lanes_at(core * (width_lat // 2), width_lat // 2)
    for target, left, right in (
        (r.grad_up, r.x_mlp, r.x_pre),
        (r.grad_down, r.x_act, r.x_cot),
        (r.grad_out, r.x_att, r.x_branch),
    ):
        rows = target.shape[0]
        for tile in range(rows // 128):
            cols = lanes_at(bits[X] * rows + tile * 128, 128)
            target[tile * 128 : (tile + 1) * 128, :] = low(dot_tn(left[:, cols], right[:, half]))
    halving = Halving(
        courier,
        bits,
        targets,
        {UP: r.grad_up, DOWN: r.grad_down, OUT: r.grad_out},
        {
            UP: (r.up_0, r.up_1, r.piece_up),
            DOWN: (r.down_0, r.down_1, r.piece_down),
            OUT: (r.out_0, r.out_1, r.piece_out),
        },
    )
    for which in (UP, DOWN, OUT):
        halving.give(which, 0)
    for moment, staged, slot in zip(
        (r.mom_query, r.mom_key, r.mom_value, r.mom_out, r.mom_up, r.mom_down),
        (r.f_query, r.f_key, r.f_value, r.f_out, r.f_up, r.f_down),
        SLOTS,
    ):

        @pl.when(seq == slot)
        def _(moment=moment, staged=staged):
            copy = pltpu.make_async_copy(moment, staged, r.moment_sem)
            copy.start()
            copy.wait()
            r.base[rows_at(opt * up_rows, staged.shape[0]), : staged.shape[1]] = low(
                0.95 * staged[...]
            )

    own_base = r.base.at[rows_at(opt * up_rows, up_rows)]
    base_across = courier.send(own_base, own_base, targets[X])
    base_beside = courier.send(own_base, own_base, targets[CORE])
    for copy in returns:
        copy.wait_recv()

    for h in range(HEADS):
        if h in POINTS:
            which, stage = POINTS[h]
            halving.take(which, stage)
            halving.give(which, stage + 1)
        ch = slice(h * HEAD_DIM, (h + 1) * HEAD_DIM)
        ch_v = slice(width + h * HEAD_DIM, width + (h + 1) * HEAD_DIM)
        grad_query = None
        for m in range(micro):
            at = slice(m * span, (m + 1) * span)
            lane = m * HEADS + h
            lane_in = (micro + m) * HEADS + h
            prob = r.weights[lane] * jnp.exp(
                r.top[:, lane : lane + 1] - r.back[:, lane : lane + 1]
            )
            grad_att = r.grad_att[m, :, ch]
            grad_prob = dot_nt(grad_att, r.pairs[at, ch_v])
            grad_scores = low(prob * (grad_prob - r.back[:, lane_in : lane_in + 1]))
            part = dot_nn(grad_scores, r.pairs[at, ch])
            grad_query = part if grad_query is None else grad_query + part
            r.grad_pairs[at, ch] = low(scale * dot_tn(grad_scores, r.queries[:, ch]))
            r.grad_pairs[at, ch_v] = low(dot_tn(low(prob), grad_att))
        r.grad_query[:, ch] = low(scale * grad_query)

    part_width = width // 2

    def pair_product(targets_two, which):
        for kind, target in enumerate(targets_two):
            cols = lanes_at(kind * width + which * part_width, part_width)
            right = r.grad_pairs[:, cols]
            for tile in range(width // TILE):
                rows = slice(tile * TILE, (tile + 1) * TILE)
                target[rows, :] = low(dot_tn(r.in_low[:, rows], right))

    base_across.wait_recv()
    other_base = r.base.at[rows_at(opt_x * up_rows, up_rows)]
    base_last = courier.send(other_base, other_base, targets[CORE])
    base_beside.wait_recv()
    pair_product((r.pair_other.at[0], r.pair_other.at[1]), 1 - core)
    pair_copy = courier.send(r.pair_other, r.pair_in, targets[CORE])
    pair_product((r.grad_key, r.grad_value), core)
    r.in_sums[...] = jnp.zeros_like(r.in_sums)

    def norm_in_back(step, carry):
        at = rows_at(step * 128, 128)
        grad_in = dot_nt(r.grad_pairs[at, :], r.pair_full[...])
        hat = r.in_hat[at, :]
        r.in_sums[0:1, :] = r.in_sums[0:1, :] + jnp.sum(grad_in * hat, axis=0, keepdims=True)
        r.in_sums[1:2, :] = r.in_sums[1:2, :] + jnp.sum(grad_in, axis=0, keepdims=True)
        scaled = grad_in * r.in_vectors[0:1, :]
        r.input_grad[at, :] = r.in_inv[at, :] * (
            scaled
            - jnp.mean(scaled, axis=-1, keepdims=True)
            - hat * jnp.mean(scaled * hat, axis=-1, keepdims=True)
        )
        return carry

    lax.fori_loop(0, r.in_low.shape[0] // 128, norm_in_back, 0)
    r.vectors[4:6, :width] = r.in_sums[0:2, :]
    base_last.wait_recv()
    pair_copy.wait_recv()
    add_into(r.grad_key, r.pair_in.at[0])
    add_into(r.grad_value, r.pair_in.at[1])
    for which in (UP, OUT, DOWN):
        halving.take(which, 2)
    courier.finish()


def run_pass(tokens, usable, cotangent, latents, lat_vectors, in_vectors, weights, moments):
    f32, bf16 = jnp.float32, jnp.bfloat16
    w_query, w_key, w_value, w_out, w_up, w_down = weights
    operands = dict(
        tokens=tokens,
        usable=usable,
        cotangent=cotangent,
        latents=latents,
        lat_vectors=lat_vectors,
        in_vectors=in_vectors,
        w_query=w_query,
        w_key=w_key,
        w_value=w_value,
        w_out=w_out,
        w_up=w_up,
        w_down=w_down,
        mom_query=moments[0],
        mom_key=moments[1],
        mom_value=moments[2],
        mom_out=moments[3],
        mom_up=moments[4],
        mom_down=moments[5],
    )
    count, width = tokens.shape
    micro, _, span = usable.shape
    lat_count, width_lat = latents.shape
    own = lat_count // 8
    rows = micro * own
    outputs = dict(
        block_out=((rows, width_lat), bf16),
        input_grad=((count, width), f32),
        grad_key=((width, width // 2), bf16),
        grad_value=((width, width // 2), bf16),
        grad_query=((lat_count, width), bf16),
        vectors=((8, width_lat), f32),
        rest=((own, width_lat), bf16),
        lat_low=((lat_count, width_lat), bf16),
        lat_block=((lat_count, width_lat // 4), bf16),
        query_full=((width_lat, width), bf16),
        base=((width_lat, width_lat), bf16),
    )
    scratch = dict(
        grad_up=((width_lat // 2, width_lat // 2), bf16),
        grad_down=((width_lat // 2, width_lat // 2), bf16),
        grad_out=((width // 2, width_lat // 2), bf16),
        f_query=(w_query.shape, f32),
        f_key=(w_key.shape, f32),
        f_value=(w_value.shape, f32),
        f_out=(w_out.shape, f32),
        f_up=(w_up.shape, f32),
        f_down=(w_down.shape, f32),
        pair_full=((width, 2 * width), bf16),
        out_full=((width, width_lat), bf16),
        up_full=((width_lat, width_lat), bf16),
        down_full=((width_lat, width_lat), bf16),
        in_low=((count, width), bf16),
        in_hat=((count, width), f32),
        in_inv=((count, 1), f32),
        in_sums=((8, width), f32),
        pairs=((count, 2 * width), bf16),
        queries=((lat_count, width), bf16),
        weights=((micro * HEADS, lat_count, span), f32),
        top=((lat_count, 128), f32),
        lse=((lat_count, 128), f32),
        part=((micro, lat_count, width), bf16),
        part_in=((8, micro, own, width), bf16),
        lse_in=((8, own, 128), f32),
        attended=((rows, width), f32),
        hidden=((rows, width_lat), f32),
        mlp_hat=((rows, width_lat), f32),
        slope=((rows, width_lat), f32),
        x_att=((4 * rows, width), bf16),
        x_branch=((4 * rows, width_lat), bf16),
        x_mlp=((4 * rows, width_lat), bf16),
        x_pre=((4 * rows, width_lat), bf16),
        x_act=((4 * rows, width_lat), bf16),
        x_cot=((4 * rows, width_lat), bf16),
        grad_att=((micro, lat_count, width), bf16),
        back=((lat_count, 128), f32),
        grad_pairs=((count, 2 * width), bf16),
        pair_other=((2, width, width // 2), bf16),
        pair_in=((2, width, width // 2), bf16),
    )
    for which, name in ((UP, "up"), (DOWN, "down"), (OUT, "out")):
        chain = chain_of(which, scratch["grad_" + name][0])
        for stage, shape in enumerate(chain[:-1]):
            scratch[f"{name}_{stage}"] = (shape, bf16)
        outputs["piece_" + name] = (chain[-1], bf16)
    copies = 5 * 5 + 7 * micro + 7 + 14 + 18 + 1 + 3 + 9
    sems = dict(
        send=pltpu.SemaphoreType.DMA((copies,)),
        recv=pltpu.SemaphoreType.DMA((copies,)),
        local=pltpu.SemaphoreType.DMA((6,)),
        moment_sem=pltpu.SemaphoreType.DMA,
    )
    keys = (*operands, *outputs, *scratch, *sems)
    vmem, anywhere = pl.BlockSpec(memory_space=pltpu.VMEM), pl.BlockSpec(memory_space=pl.ANY)
    results = pl.pallas_call(
        functools.partial(pass_body, keys),
        out_shape=[jax.ShapeDtypeStruct(*spec) for spec in outputs.values()],
        in_specs=[vmem] * 6 + [anywhere] * 12,
        out_specs=[vmem] * len(outputs),
        scratch_shapes=[*(pltpu.VMEM(*spec) for spec in scratch.values()), *sems.values()],
        compiler_params=pltpu.CompilerParams(
            collective_id=2, has_side_effects=True, vmem_limit_bytes=VMEM_LIMIT
        ),
        name="pass",
    )(*operands.values())
    return named(outputs, results)


def tail_body(keys, *refs):
    r = named(keys, refs)
    seq, opt = lax.axis_index("seq"), lax.axis_index("opt")
    bits, targets = partners(seq, opt)
    core, z0, z1, y, x = bits[CORE], bits[Z0], bits[Z1], bits[Y], bits[X]
    ring = [((seq + step) % 8, opt) for step in range(1, 8)]
    height = r.lat_block.shape[1]
    load = Loader(r.local)
    loads = [
        load.start(source, target)
        for source, target in (
            (r.base, r.h_base),
            (r.lat_low, r.h_lat_low),
            (r.query_full, r.h_query_full),
            (r.latents, r.h_latents),
        )
    ]
    clear(r.g_full.at[0])
    clear(r.g_full.at[1])
    beyond = [((seq + step) % 8, targets[X][1]) for step in range(8)]
    greet([targets[CORE], *ring, *beyond])
    courier = Courier(r.send, r.recv)
    sums = {UP: r.up, DOWN: r.down, OUT: r.out, KEY: r.key, VALUE: r.value, QUERY: r.query}
    halving = Halving(
        courier,
        bits,
        targets,
        sums,
        {
            KEY: (r.key_0, r.key_1, r.key_2, r.key_3),
            VALUE: (r.value_0, r.value_1, r.value_2, r.value_3),
            QUERY: (r.query_0, r.query_1, r.query_2, r.query_3, r.query_4),
        },
    )
    for which in (QUERY, KEY, VALUE):
        halving.give(which, 0)
    def piece_place(which, seq_from, x_from):
        bit_y, bit_z0, bit_z1 = seq_from % 2, (seq_from // 2) % 2, seq_from // 4
        high, mid = (bit_y, bit_z0) if which in Y_FIRST else (bit_z0, bit_y)
        rows = sums[which].shape[0]
        return rows_at(x_from * (2 * height) + high * height + (mid * 2 + bit_z1) * rows, rows)

    def piece_copy(index, which, seq_from, x_from, same):
        cols = sums[which].shape[1]
        place = piece_place(which, seq_from, x_from)
        return pltpu.make_async_remote_copy(
            src_ref=sums[which],
            dst_ref=r.g_full.at[core, place, pl.ds(0, cols)],
            send_sem=r.piece_send.at[index, 0 if same else 1],
            recv_sem=r.piece_recv.at[0 if same else 1, seq_from],
            device_id=(SLOTS[index], opt if same else targets[X][1]),
            device_id_type=MESH,
        )

    def offer(index, which):
        piece_copy(index, which, seq, x, False).start()

        @pl.when(seq != SLOTS[index])
        def _():
            piece_copy(index, which, seq, x, True).start()

        @pl.when(seq == SLOTS[index])
        def _():
            cols = sums[which].shape[1]
            r.g_full[core, piece_place(which, seq, x), :cols] = sums[which][...]

    owned = ((1, KEY), (2, VALUE), (3, OUT), (4, UP), (5, DOWN))
    for index, which in owned[2:]:
        offer(index, which)
    r.vectors_sum[...] = r.vectors[...]
    vector_copy = courier.send(r.vectors, r.vectors_in.at[0], targets[CORE])
    rest_width = r.rest.shape[1] // 2
    column = lanes_at(core * rest_width, rest_width)
    rest_copy = courier.send(
        r.rest.at[:, lanes_at((1 - core) * rest_width, rest_width)], r.rest_in.at[0], targets[CORE]
    )
    halving.take(QUERY, 0)
    halving.give(QUERY, 1)
    vector_copy.wait_recv()
    r.vectors_sum[...] = r.vectors_sum[...] + r.vectors_in[0]
    rest_copy.wait_recv()
    r.rest_sum[...] = low(wide(r.rest[:, column]) + wide(r.rest_in[0]))
    rest_copy = courier.send(r.rest_sum, r.rest_in.at[1], targets[X])
    for stage in range(4):
        axis = (X, Y, Z0, Z1)[stage]
        r.vectors_out[stage] = r.vectors_sum[...]
        vector_copy = courier.send(
            r.vectors_out.at[stage], r.vectors_in.at[stage + 1], targets[axis]
        )
        if stage > 0:
            rest_copy.wait_recv()
            if stage == 1:
                r.rest_all[z1, z0, y, :, column] = low(wide(r.rest_sum[...]) + wide(r.rest_in[1]))
            every = slice(None)
            lead = ((z1, z0, y), (every, z0, y), (every, every, y))[stage - 1]
            view = r.rest_all.at[(*lead, every, column)]
            rest_copy = courier.send(view, view, targets[(Z1, Z0, Y)[stage - 1]])
        for which in (QUERY, KEY, VALUE):
            own_stage = stage + 1 if which == QUERY else stage
            halving.take(which, own_stage)
            if stage < 3:
                halving.give(which, own_stage + 1)
        vector_copy.wait_recv()
        r.vectors_sum[...] = r.vectors_sum[...] + r.vectors_in[stage + 1]
    rest_copy.wait_recv()
    view = r.rest_all.at[:, :, :, :, column]
    rest_copy = courier.send(view, view, targets[CORE])

    for index, which in owned[:2]:
        offer(index, which)
    rows, width = sums[QUERY].shape
    query_column = lanes_at(core * width, width)
    start = (x * 8 + y * 4 + z0 * 2 + z1) * rows
    r.query_all[rows_at(start, rows), query_column] = sums[QUERY][...]
    view = r.query_all.at[rows_at(start, rows), query_column]
    query_copies = [courier.send(view, view, target) for target in ring]

    gathered = (r.g_up, r.g_down, r.g_key, r.g_value, r.g_out)
    full = (r.n_up, r.n_down, r.n_key, r.n_value, r.n_out)
    for which in range(5):
        high, mid = (y, z0) if which in Y_FIRST else (z0, y)
        rows = sums[which].shape[0]
        gathered[which][rows_at((high * 4 + mid * 2 + z1) * rows, rows), :] = sums[which][...]

    def gather(which, step):
        first_axis, last_axis = (Y, Z0) if which in Y_FIRST else (Z0, Y)
        high, mid = bits[first_axis], bits[last_axis]
        rows = sums[which].shape[0]
        if step < 3:
            base, count = ((high * 4 + mid * 2 + z1, 1), (high * 4 + mid * 2, 2), (high * 4, 4))[
                step
            ]
            source = target = gathered[which].at[rows_at(base * rows, count * rows)]
        else:
            cols = sums[which].shape[1]
            source = gathered[which].at[rows_at((1 - core) * (4 * rows), 4 * rows)]
            target = full[which].at[:, lanes_at(core * cols, cols)]
        return pltpu.make_async_remote_copy(
            src_ref=source,
            dst_ref=target,
            send_sem=r.gather_send.at[which, step],
            recv_sem=r.gather_recv.at[which, step],
            device_id=targets[(Z1, last_axis, first_axis, CORE)[step]],
            device_id_type=MESH,
        )

    for which in range(5):
        gather(which, 0).start()
    for copy in query_copies:
        copy.wait_recv()
    view = r.query_all.at[rows_at(x * (8 * sums[QUERY].shape[0]), 8 * sums[QUERY].shape[0]), query_column]
    courier.send(view, view, targets[X]).wait_recv()
    view = r.query_all.at[:, query_column]
    courier.send(view, view, targets[CORE]).wait_recv()
    rest_copy.wait_recv()

    for index, which in owned:

        @pl.when(seq == SLOTS[index])
        def _(index=index, which=which):
            for seq_from in range(8):
                if seq_from != SLOTS[index]:
                    piece_copy(index, which, seq_from, x, True).wait_recv()
                piece_copy(index, which, seq_from, 1 - x, False).wait_recv()

    beside = courier.send(r.g_full.at[core], r.g_full.at[core], targets[CORE])
    beside.wait_recv()
    for copy in loads:
        copy.wait()
    side = r.whole.shape[1]
    tiles = side // TILE
    big = (seq == SLOTS[4]) | (seq == SLOTS[5])
    small = (seq == SLOTS[0]) | (seq == SLOTS[1]) | (seq == SLOTS[2]) | (seq == SLOTS[3])
    both = 2 * width
    turned = r.out.shape[0] * 4
    r.total[0] = 0.0

    def joined(at, lanes, block):
        r.wide[at, lanes] = block
        r.total[0] = r.total[0] + jnp.sum(block * block)

    def over_tiles(body):
        def step(tile, carry):
            body(rows_at(tile * TILE, TILE), tile)
            return carry

        lax.fori_loop(0, tiles, step, 0)

    @pl.when(big)
    def _():
        def body(at, tile):
            for index in range(2):
                lanes = slice(index * (side // 2), (index + 1) * (side // 2))
                joined(at, lanes, wide(r.h_base[at, lanes]) + wide(r.g_full[index, at, :]))

        over_tiles(body)

    @pl.when((seq == SLOTS[1]) | (seq == SLOTS[2]))
    def _():
        def body(at, tile):
            for index in range(2):
                lanes = slice(index * width, (index + 1) * width)
                joined(at, lanes, wide(r.h_base[at, lanes]) + wide(r.g_full[index, at, :width]))

        over_tiles(body)

    @pl.when(seq == SLOTS[0])
    def _():
        def body(at, tile):
            lanes = slice(0, both)
            joined(
                at,
                lanes,
                wide(r.h_base[at, lanes])
                + dot_tn(r.h_lat_low[:, lanes_at(tile * TILE, TILE)], r.query_all[...]),
            )

        over_tiles(body)

    @pl.when(seq == SLOTS[3])
    def _():
        for block in range(4):
            at = slice(block * height, block * height + turned)
            for index in range(2):
                lanes = slice(index * (side // 2), (index + 1) * (side // 2))
                part = wide(r.h_base[at, lanes]) + wide(r.g_full[index, at, :])
                joined(lanes, slice(block * turned, (block + 1) * turned), part.T)

    scale = 1.0 / (jnp.sqrt(jnp.full((1, 1), r.total[0], jnp.float32)) + 1e-07)

    def normalise(cols):
        def body(at, tile):
            block = r.wide[at, :cols] * scale
            r.wide[at, :cols] = block
            r.whole[at, :cols] = low(block)

        over_tiles(body)

    def update(at, cols):
        block = coef_one * r.wide[at, :cols] + dot_nn(r.whole[at, :cols], r.poly[:cols, :cols])
        r.wide[at, :cols] = block
        r.whole[at, :cols] = low(block)

    def gathers(step, action):
        for which in range(5):
            action(gather(which, step))

    def gather_take(step):
        gathers(step, lambda copy: copy.wait_recv())

    def gather_give(step):
        gathers(step, lambda copy: copy.start())
        if step == 3:
            for which in range(5):
                rows, cols = gathered[which].shape
                full[which][:, lanes_at(core * cols, cols)] = gathered[which][
                    rows_at(core * (rows // 2), rows // 2), :
                ]

    outs = (r.o_query, r.o_key, r.o_value, r.o_out, r.o_up, r.o_down)
    z, depth = seq // 2, 4

    def copy(which, part, way):
        out = outs[which]
        cols = out.shape[1] * 4 // PARTS[which]
        rows = out.shape[0] // 4
        across = out.shape[1] // cols
        view = out.at[pl.ds(part // across * rows, rows), pl.ds(part % across * cols, cols)]
        return pltpu.make_async_remote_copy(
            src_ref=view,
            dst_ref=view,
            send_sem=r.spread_send.at[way, which * max(PARTS) + part],
            recv_sem=r.spread_recv.at[which * max(PARTS) + part],
            device_id=((seq + 2, opt), (seq - 2, opt), targets[Y])[way],
            device_id_type=MESH,
        )

    def for_ways(which, mine, action):
        slot_y, slot_z = SLOTS[which] % 2, SLOTS[which] // 2
        turn = (y == slot_y) & ((z == slot_z) if mine else (z != slot_z))
        on = (
            turn & (z >= slot_z) & (z < depth - 1),
            turn & (z <= slot_z) & (z > 0),
            turn,
        )
        for way in range(3):

            @pl.when(on[way])
            def _(way=way):
                action(way)

    def send_own(which):
        for part in range(PARTS[which]):
            if part >= AHEAD:
                for_ways(which, True, lambda way: copy(which, part - AHEAD, way).wait_send())
            for_ways(which, True, lambda way: copy(which, part, way).start())

    def pass_on(group, first, last):
        for part in range(first, last):
            for which in group:

                @pl.when((y == SLOTS[which] % 2) & (z != SLOTS[which] // 2))
                def _(which=which, part=part):
                    copy(which, part, 2).wait_recv()

                for_ways(which, False, lambda way: copy(which, part, way).start())

    def latent_gradients():
        r.lat_grads[...] = jnp.zeros_like(r.lat_grads)
        r.lat_grads[2:6, :] = r.vectors_sum[0:4, :]

        def latent_rows(step, carry):
            at = rows_at(step * 32, 32)
            hat, inverse = norm(r.h_latents[at, :])
            grad = dot_nt(r.query_all[at, :], r.h_query_full[...])
            r.lat_grads[0:1, :] = r.lat_grads[0:1, :] + jnp.sum(grad * hat, axis=0, keepdims=True)
            r.lat_grads[1:2, :] = r.lat_grads[1:2, :] + jnp.sum(grad, axis=0, keepdims=True)
            scaled = grad * r.lat_vectors[0:1, :]
            r.latent_grad[at, :] = wide(r.rest_all[step // 4, (step // 2) % 2, step % 2]) + inverse * (
                scaled
                - jnp.mean(scaled, axis=-1, keepdims=True)
                - hat * jnp.mean(scaled * hat, axis=-1, keepdims=True)
            )
            return carry

        lax.fori_loop(0, r.latents.shape[0] // 32, latent_rows, 0)
        r.query_grad[...] = dot_tn(r.lat_block[...], r.query_all[...])

    few, many = (0, 1, 2, 3), (4, 5)
    own_first = opt * height
    gather_take(0)
    gather_give(1)

    @pl.when(big)
    def _():
        normalise(side)

        def sweep(index, carry):
            @pl.when(index == 1)
            def _():
                gather_take(1)
                gather_give(2)

            @pl.when(index == 3)
            def _():
                pass_on(few, 0, 2)

            @pl.when(index == 4)
            def _():
                gather_take(2)
                gather_give(3)
                pass_on(few, 2, 4)

            polynomial(r.whole, r.gram, r.poly)

            @pl.when(index < 4)
            def _():
                update(slice(0, side), side)

            return carry

        lax.fori_loop(0, 5, sweep, 0)
        update(rows_at(own_first, height), side)

    @pl.when(small)
    def _():
        normalise(both)

        def sweep(index, carry):
            polynomial(r.whole.at[:, :both], r.gram.at[:both, :both], r.poly.at[:both, :both])
            update(slice(0, side), both)
            return carry

        lax.fori_loop(0, 5, sweep, 0)

    for which in few + many:

        @pl.when(seq == SLOTS[which])
        def _(which=which):
            rows, cols = outs[which].shape
            if which == 3:
                for block in range(4):

                    @pl.when(opt == block)
                    def _(block=block):
                        lanes = slice(block * rows, (block + 1) * rows)
                        outs[which][...] = low(wide(r.whole[:, lanes]).T)
            else:
                outs[which][...] = r.whole[rows_at(own_first, rows), :cols]

    @pl.when(jnp.logical_not(big))
    def _():
        gather_take(1)
        gather_give(2)
        for which in few:
            send_own(which)
        pass_on(few, 0, 4)
        gather_take(2)
        gather_give(3)

    for which in many:
        send_own(which)
    gather_take(3)
    latent_gradients()
    pass_on(many, 0, 8)
    for which in few + many:
        for part in range(PARTS[which]):

            @pl.when(y != SLOTS[which] % 2)
            def _(which=which, part=part):
                copy(which, part, 2).wait_recv()

    for which in few + many:
        for part in range(PARTS[which]):
            for_ways(which, False, lambda way: copy(which, part, way).wait_send())
            if part >= PARTS[which] - AHEAD:
                for_ways(which, True, lambda way: copy(which, part, way).wait_send())
    for index, which in owned:
        piece_copy(index, which, seq, x, False).wait_send()

        @pl.when(seq != SLOTS[index])
        def _(index=index, which=which):
            piece_copy(index, which, seq, x, True).wait_send()

    for step in range(4):
        gathers(step, lambda copy: copy.wait_send())
    courier.finish()


def run_tail(done, latents, lat_vectors, moments):
    f32, bf16 = jnp.float32, jnp.bfloat16
    mom_query, mom_key, mom_value, mom_out, mom_up, mom_down = moments
    width_lat = latents.shape[1]
    key, value = (
        grad.reshape(2, grad.shape[0] // 2, grad.shape[1])
        for grad in (done.grad_key, done.grad_value)
    )
    operands = dict(
        base=done.base,
        lat_low=done.lat_low,
        query_full=done.query_full,
        latents=latents,
        vectors=done.vectors,
        rest=done.rest,
        lat_block=done.lat_block,
        lat_vectors=lat_vectors,
        up=done.piece_up,
        down=done.piece_down,
        out=done.piece_out,
        key=key,
        value=value,
        query=done.grad_query,
    )
    outputs = dict(
        vectors_sum=(done.vectors.shape, f32),
        lat_grads=((8, width_lat), f32),
        latent_grad=(latents.shape, f32),
        query_grad=(mom_query.shape, f32),
        n_up=(mom_up.shape, bf16),
        n_down=(mom_down.shape, bf16),
        n_key=(mom_key.shape, bf16),
        n_value=(mom_value.shape, bf16),
        n_out=(mom_out.shape, bf16),
        o_query=(mom_query.shape, bf16),
        o_key=(mom_key.shape, bf16),
        o_value=(mom_value.shape, bf16),
        o_out=(mom_out.shape, bf16),
        o_up=(mom_up.shape, bf16),
        o_down=(mom_down.shape, bf16),
    )
    half_rest = (done.rest.shape[0], done.rest.shape[1] // 2)
    scratch = dict(
        h_base=(done.base.shape, bf16),
        h_lat_low=(done.lat_low.shape, bf16),
        h_query_full=(done.query_full.shape, bf16),
        h_latents=(latents.shape, f32),
        vectors_in=((5, *done.vectors.shape), f32),
        vectors_out=((4, *done.vectors.shape), f32),
        rest_in=((2, *half_rest), bf16),
        rest_sum=(half_rest, bf16),
        rest_all=((2, 2, 2, *done.rest.shape), bf16),
        query_all=(done.grad_query.shape, bf16),
        g_full=((2, width_lat, width_lat // 2), bf16),
        g_up=((width_lat // 2, width_lat // 2), bf16),
        g_down=((width_lat // 2, width_lat // 2), bf16),
        g_key=(key.shape[1:], bf16),
        g_value=(value.shape[1:], bf16),
        g_out=((2 * mom_out.shape[0], width_lat // 2), bf16),
        wide=((width_lat, width_lat), f32),
        whole=((width_lat, width_lat), bf16),
        gram=((width_lat, width_lat), bf16),
        poly=((width_lat, width_lat), bf16),
    )
    for which, name, array in (
        (KEY, "key", key),
        (VALUE, "value", value),
        (QUERY, "query", done.grad_query),
    ):
        for stage, shape in enumerate(chain_of(which, array.shape)):
            scratch[f"{name}_{stage}"] = (shape, bf16)
    copies = 48
    count = len(SLOTS) * max(PARTS)
    dma = pltpu.SemaphoreType.DMA
    sems = dict(
        send=dma((copies,)),
        recv=dma((copies,)),
        piece_send=dma((6, 2)),
        piece_recv=dma((2, 8)),
        gather_send=dma((5, 4)),
        gather_recv=dma((5, 4)),
        spread_send=dma((3, count)),
        spread_recv=dma((count,)),
        total=pltpu.SMEM((1,), f32),
        local=dma((4,)),
    )
    keys = (*operands, *outputs, *scratch, *sems)
    vmem, anywhere = pl.BlockSpec(memory_space=pltpu.VMEM), pl.BlockSpec(memory_space=pl.ANY)
    results = pl.pallas_call(
        functools.partial(tail_body, keys),
        out_shape=[jax.ShapeDtypeStruct(*spec) for spec in outputs.values()],
        in_specs=[anywhere] * 4 + [vmem] * (len(operands) - 4),
        out_specs=[vmem] * len(outputs),
        scratch_shapes=[*(pltpu.VMEM(*spec) for spec in scratch.values()), *sems.values()],
        compiler_params=pltpu.CompilerParams(
            collective_id=0, has_side_effects=True, vmem_limit_bytes=VMEM_LIMIT
        ),
        name="tail",
    )(*operands.values())
    return named(outputs, results)


def finish_body(keys, rates, *refs):
    r = named(keys, refs)
    count = len(rates)
    load = Loader(r.load_sem)
    into = lambda name, index: getattr(r, f"{name}{index}")
    loads = []
    for index in range(count):
        loads.append(
            [
                load.start(into(name, index), into("v" + name, index))
                for name in ("m", "g", "w", "o")
            ]
        )
    states = [
        load.start(source, target)
        for source, target in (
            (r.latents, r.vlatents),
            (r.first, r.vfirst),
            (r.second, r.vsecond),
            (r.grad, r.vgrad),
        )
    ]
    store = Loader(r.store_sem)
    stores = []

    def over_rows(ref, body):
        def step(index, carry):
            body(rows_at(index * 32, 32))
            return carry

        lax.fori_loop(0, ref.shape[0] // 32, step, 0)

    for index, (keep, rate) in enumerate(rates):
        moment, grad, weight, turn = (into("v" + name, index) for name in ("m", "g", "w", "o"))
        loads[index][0].wait()
        loads[index][1].wait()

        def new_moment(at, moment=moment, grad=grad):
            moment[at, :] = 0.95 * moment[at, :] + wide(grad[at, :])

        over_rows(moment, new_moment)
        stores.append(store.start(moment, into("nm", index)))
        loads[index][2].wait()
        loads[index][3].wait()

        def new_weight(at, weight=weight, turn=turn, keep=keep, rate=rate):
            weight[at, :] = keep * weight[at, :] - rate * wide(turn[at, :])

        over_rows(weight, new_weight)
        stores.append(store.start(weight, into("nw", index)))
    for copy in states:
        copy.wait()

    def new_latents(at):
        first, second, new = adam_update(
            r.vlatents[at, :], r.vgrad[at, :], r.vfirst[at, :], r.vsecond[at, :], 1.0, 0.1
        )
        r.vfirst[at, :], r.vsecond[at, :], r.vlatents[at, :] = first, second, new

    over_rows(r.vlatents, new_latents)
    for source, target in (
        (r.vfirst, r.nfirst),
        (r.vsecond, r.nsecond),
        (r.vlatents, r.nlatents),
    ):
        stores.append(store.start(source, target))
    r.lat_first_new[...], r.lat_second_new[...], r.lat_new[...] = adam_update(
        r.lat_vectors[...], r.lat_grads[:6, :], r.lat_first[...], r.lat_second[...], 0.6, 0.0
    )
    width = r.in_vectors.shape[1]
    r.in_first_new[...], r.in_second_new[...], r.in_new[...] = adam_update(
        r.in_vectors[...], r.vectors[4:6, :width], r.in_first[...], r.in_second[...], 0.6, 0.0
    )
    for copy in stores:
        copy.wait()


def run_finish(moments, gradients, masters, turns, latent_state, vector_state):
    f32 = jnp.float32
    fans = (D_LAT, E_IN, E_IN, OUT_FAN, D_LAT, D_LAT)
    sides = (D_LAT, E_IN, E_IN, D_LAT, D_LAT, D_LAT)
    rates = [
        (1.0 - 0.1 * fan ** (-0.5), fan ** (-0.5) * side**0.5) for fan, side in zip(fans, sides)
    ]
    large = {}
    for index, arrays in enumerate(zip(moments, gradients, masters, turns)):
        for name, array in zip(("m", "g", "w", "o"), arrays):
            large[f"{name}{index}"] = array
    large.update(latent_state)
    operands = {**large, **vector_state}
    outputs, scratch = {}, {}
    for index, moment in enumerate(moments):
        outputs[f"nm{index}"] = outputs[f"nw{index}"] = (moment.shape, f32)
    latents = latent_state["latents"].shape
    outputs.update(nfirst=(latents, f32), nsecond=(latents, f32), nlatents=(latents, f32))
    in_place = len(outputs)
    lat, inner = vector_state["lat_first"].shape, vector_state["in_first"].shape
    outputs.update(lat_first_new=(lat, f32), lat_second_new=(lat, f32), lat_new=(lat, f32))
    outputs.update(in_first_new=(inner, f32), in_second_new=(inner, f32), in_new=(inner, f32))
    for name, array in large.items():
        scratch["v" + name] = pltpu.VMEM(array.shape, array.dtype)
    scratch["load_sem"] = pltpu.SemaphoreType.DMA((len(large),))
    scratch["store_sem"] = pltpu.SemaphoreType.DMA((in_place,))
    vmem, anywhere = pl.BlockSpec(memory_space=pltpu.VMEM), pl.BlockSpec(memory_space=pl.ANY)
    results = pl.pallas_call(
        functools.partial(finish_body, (*operands, *outputs, *scratch), rates),
        out_shape=[jax.ShapeDtypeStruct(*spec) for spec in outputs.values()],
        in_specs=[anywhere] * len(large) + [vmem] * len(vector_state),
        out_specs=[anywhere] * in_place + [vmem] * 6,
        scratch_shapes=list(scratch.values()),
        compiler_params=pltpu.CompilerParams(vmem_limit_bytes=VMEM_LIMIT),
        name="finish",
    )(*operands.values())
    return named(outputs, results)


def adam_update(param, gradient, first, second, step_rate, decay):
    first_new = 0.9 * first + 0.1 * gradient
    second_new = 0.95 * second + 0.05 * gradient * gradient
    ratio = first_new / (1.0 - 0.9**STEP) / (jnp.sqrt(second_new / (1.0 - 0.95**STEP)) + 1e-08)
    return (first_new, second_new, param - step_rate * (ratio + decay * param))


def local_small(
    inputs,
    key_mask,
    lengths,
    cotangent,
    latents,
    lat_vectors,
    in_vectors,
    w_query,
    w_key,
    w_value,
    w_out,
    w_up,
    w_down,
    mom_query,
    mom_key,
    mom_value,
    mom_out,
    mom_up,
    mom_down,
    lat_first,
    lat_second,
    in_first,
    in_second,
    latent_first,
    latent_second,
):
    seq_index = lax.axis_index("seq")
    micro_count, _, span, width_in = inputs.shape
    lat_count, width_lat = latents.shape
    positions = seq_index * span + jnp.arange(span, dtype=jnp.int32)
    usable = (positions < lengths[:, :, None]) & ((key_mask == 1) | (positions == 0))
    masters = (w_query, w_key, w_value, w_out, w_up, w_down)
    moments = (mom_query, mom_key, mom_value, mom_out, mom_up, mom_down)
    done = run_pass(
        inputs.reshape(-1, width_in),
        usable.astype(jnp.float32),
        cotangent.reshape(-1, width_lat),
        latents,
        lat_vectors,
        in_vectors,
        masters,
        moments,
    )
    summed = run_tail(done, latents, lat_vectors, moments)
    gradients = (
        summed.query_grad,
        summed.n_key,
        summed.n_value,
        summed.n_out,
        summed.n_up,
        summed.n_down,
    )
    currents = (
        summed.o_query,
        summed.o_key,
        summed.o_value,
        summed.o_out,
        summed.o_up,
        summed.o_down,
    )
    new = run_finish(
        moments,
        gradients,
        masters,
        currents,
        dict(latents=latents, first=latent_first, second=latent_second, grad=summed.latent_grad),
        dict(
            lat_vectors=lat_vectors,
            lat_grads=summed.lat_grads,
            lat_first=lat_first,
            lat_second=lat_second,
            in_vectors=in_vectors,
            vectors=summed.vectors_sum,
            in_first=in_first,
            in_second=in_second,
        ),
    )
    return (
        done.block_out.reshape(cotangent.shape),
        done.input_grad.reshape(inputs.shape),
        new.nm0,
        new.nm1,
        new.nm2,
        new.nm3,
        new.nm4,
        new.nm5,
        new.nw0,
        new.nw1,
        new.nw2,
        new.nw3,
        new.nw4,
        new.nw5,
        new.lat_first_new,
        new.lat_second_new,
        new.lat_new,
        new.in_first_new,
        new.in_second_new,
        new.in_new,
        new.nfirst,
        new.nsecond,
        new.nlatents,
    )


def update_masters(masters, currents):
    fans = (D_LAT, E_IN, E_IN, OUT_FAN, D_LAT, D_LAT)
    sides = (D_LAT, E_IN, E_IN, D_LAT, D_LAT, D_LAT)
    new_masters = []
    for master, current, fan_in, long_side in zip(masters, currents, fans, sides):
        step_rate = fan_in ** (-0.5)
        new_masters.append(
            (1.0 - 0.1 * step_rate) * master
            - step_rate * long_side**0.5 * current.astype(jnp.float32)
        )
    return new_masters


def local(
    inputs,
    key_mask,
    lengths,
    cotangent,
    latents,
    lat_vectors,
    in_vectors,
    w_query,
    w_key,
    w_value,
    w_out,
    w_up,
    w_down,
    mom_query,
    mom_key,
    mom_value,
    mom_out,
    mom_up,
    mom_down,
    lat_first,
    lat_second,
    in_first,
    in_second,
    latent_first,
    latent_second,
):
    query_low, key_low, value_low, out_low, up_low, down_low = (
        lax.all_gather(w_query.astype(jnp.bfloat16), "opt", axis=0, tiled=True),
        lax.all_gather(w_key.astype(jnp.bfloat16), "opt", axis=0, tiled=True),
        lax.all_gather(w_value.astype(jnp.bfloat16), "opt", axis=0, tiled=True),
        lax.all_gather(w_out.astype(jnp.bfloat16), "opt", axis=0, tiled=True),
        lax.all_gather(w_up.astype(jnp.bfloat16), "opt", axis=0, tiled=True),
        lax.all_gather(w_down.astype(jnp.bfloat16), "opt", axis=0, tiled=True),
    )
    pair_low = jnp.concatenate([key_low, value_low], axis=1)
    seq_index = lax.axis_index("seq")
    seq_size = lax.axis_size("seq")
    opt_index = lax.axis_index("opt")
    opt_size = lax.axis_size("opt")
    micro_count, doc_local, span, width_in = inputs.shape
    lat_count, width_lat = latents.shape
    own_rows = lat_count // seq_size
    row_start = seq_index * own_rows
    score_scale = HEAD_DIM ** (-0.5)
    lat_normed, lat_hat, lat_inv = layer_norm(latents, lat_vectors[0], lat_vectors[1])
    lat_low = lat_normed.astype(jnp.bfloat16)
    query_rows = jnp.dot(lat_low, query_low, preferred_element_type=jnp.float32).astype(
        jnp.bfloat16
    )
    query_heads = query_rows.reshape(lat_count, HEADS, HEAD_DIM)
    own_latents = lax.dynamic_slice_in_dim(latents, row_start, own_rows, 0)
    positions = seq_index * span + jnp.arange(span, dtype=jnp.int32)
    grad_query_rows = jnp.zeros((lat_count, width_in), jnp.float32)
    grad_pair = jnp.zeros((width_in, 2 * width_in), jnp.float32)
    grad_out_w = jnp.zeros((width_in, width_lat), jnp.float32)
    grad_up_w = jnp.zeros((width_lat, width_lat), jnp.float32)
    grad_down_w = jnp.zeros((width_lat, width_lat), jnp.float32)
    mlp_gain = jnp.zeros((width_lat,), jnp.float32)
    mlp_shift = jnp.zeros((width_lat,), jnp.float32)
    bias_up = jnp.zeros((width_lat,), jnp.float32)
    bias_down = jnp.zeros((width_lat,), jnp.float32)
    in_gain = jnp.zeros((width_in,), jnp.float32)
    in_shift = jnp.zeros((width_in,), jnp.float32)
    latent_rest = jnp.zeros((own_rows, width_lat), jnp.float32)
    block_parts = []
    input_parts = []
    for micro_step in range(micro_count):
        tokens = inputs[micro_step]
        usable = (positions[None, :] < lengths[micro_step][:, None]) & (
            (key_mask[micro_step] == 1) | (positions[None, :] == 0)
        )
        in_normed, in_hat, in_inv = layer_norm(
            tokens.astype(jnp.float32), in_vectors[0], in_vectors[1]
        )
        in_low = in_normed.astype(jnp.bfloat16)
        pair_rows = jnp.einsum(
            "bse,ef->bsf", in_low, pair_low, preferred_element_type=jnp.float32
        ).astype(jnp.bfloat16)
        key_heads = pair_rows[:, :, :width_in].reshape(doc_local, span, HEADS, HEAD_DIM)
        value_heads = pair_rows[:, :, width_in:].reshape(doc_local, span, HEADS, HEAD_DIM)
        masked = masked_scores(query_heads, key_heads, usable, score_scale)
        row_max = lax.pmax(jnp.max(masked, axis=-1), "seq")
        weights = jnp.exp(masked - row_max[..., None])
        weights_low = weights.astype(jnp.bfloat16)
        summed, row_sum = (
            lax.psum(
                jnp.einsum(
                    "bhns,bshd->bnhd", weights_low, value_heads, preferred_element_type=jnp.float32
                ).astype(jnp.bfloat16),
                "seq",
            ).astype(jnp.float32),
            lax.psum(jnp.sum(weights, axis=-1).astype(jnp.bfloat16), "seq").astype(jnp.float32),
        )
        sum_heads = jnp.transpose(row_sum, (0, 2, 1))[..., None]
        attended = summed / sum_heads
        own_att = (
            lax.dynamic_slice_in_dim(attended, row_start, own_rows, 1)
            .reshape(doc_local, own_rows, width_in)
            .astype(jnp.bfloat16)
        )
        hidden = own_latents[None] + jnp.einsum(
            "bne,ef->bnf", own_att, out_low, preferred_element_type=jnp.float32
        )
        mlp_normed, mlp_hat, mlp_inv = layer_norm(hidden, lat_vectors[2], lat_vectors[3])
        mlp_low = mlp_normed.astype(jnp.bfloat16)
        pre_act = (
            jnp.einsum("bnf,fg->bng", mlp_low, up_low, preferred_element_type=jnp.float32)
            + lat_vectors[4]
        )
        activated, gelu_pull = jax.vjp(exact_gelu, pre_act)
        act_low = activated.astype(jnp.bfloat16)
        block_parts.append(
            (
                hidden
                + jnp.einsum("bng,gk->bnk", act_low, down_low, preferred_element_type=jnp.float32)
                + lat_vectors[5]
            ).astype(jnp.bfloat16)
        )
        back_rows = cotangent[micro_step]
        grad_down_w = grad_down_w + jnp.einsum(
            "bng,bnk->gk", act_low, back_rows, preferred_element_type=jnp.float32
        )
        bias_down = bias_down + jnp.sum(back_rows.astype(jnp.float32), axis=(0, 1))
        grad_act = jnp.einsum(
            "bnk,gk->bng", back_rows, down_low, preferred_element_type=jnp.float32
        )
        grad_pre = gelu_pull(grad_act)[0].astype(jnp.bfloat16)
        grad_up_w = grad_up_w + jnp.einsum(
            "bnf,bng->fg", mlp_low, grad_pre, preferred_element_type=jnp.float32
        )
        bias_up = bias_up + jnp.sum(grad_pre.astype(jnp.float32), axis=(0, 1))
        grad_mlp = jnp.einsum("bng,fg->bnf", grad_pre, up_low, preferred_element_type=jnp.float32)
        mlp_gain = mlp_gain + jnp.sum(grad_mlp * mlp_hat, axis=(0, 1))
        mlp_shift = mlp_shift + jnp.sum(grad_mlp, axis=(0, 1))
        grad_hidden = back_rows.astype(jnp.float32) + norm_back(
            grad_mlp, mlp_hat, mlp_inv, lat_vectors[2]
        )
        latent_rest = latent_rest + jnp.sum(grad_hidden, axis=0)
        grad_branch = grad_hidden.astype(jnp.bfloat16)
        grad_out_w = grad_out_w + jnp.einsum(
            "bne,bnf->ef", own_att, grad_branch, preferred_element_type=jnp.float32
        )
        grad_own = jnp.einsum(
            "bnf,ef->bne", grad_branch, out_low, preferred_element_type=jnp.float32
        ).astype(jnp.bfloat16)
        grad_att = (
            lax.all_gather(grad_own, "seq", axis=1, tiled=True)
            .astype(jnp.float32)
            .reshape(doc_local, lat_count, HEADS, HEAD_DIM)
        )
        grad_summed = (grad_att / sum_heads).astype(jnp.bfloat16)
        inner = jnp.transpose(jnp.sum(grad_att * attended, axis=-1) / sum_heads[..., 0], (0, 2, 1))
        grad_prob = jnp.einsum(
            "bnhd,bshd->bhns", grad_summed, value_heads, preferred_element_type=jnp.float32
        )
        grad_scores = (weights * (grad_prob - inner[..., None])).astype(jnp.bfloat16)
        grad_query_rows = grad_query_rows + score_scale * jnp.einsum(
            "bhns,bshd->nhd", grad_scores, key_heads, preferred_element_type=jnp.float32
        ).reshape(lat_count, width_in)
        grad_keys = (
            score_scale
            * jnp.einsum(
                "bhns,nhd->bshd", grad_scores, query_heads, preferred_element_type=jnp.float32
            )
        ).astype(jnp.bfloat16)
        grad_values = jnp.einsum(
            "bhns,bnhd->bshd", weights_low, grad_summed, preferred_element_type=jnp.float32
        ).astype(jnp.bfloat16)
        grad_pairs = jnp.concatenate(
            [
                grad_keys.reshape(doc_local, span, width_in),
                grad_values.reshape(doc_local, span, width_in),
            ],
            axis=-1,
        )
        grad_pair = grad_pair + jnp.einsum(
            "bse,bsf->ef", in_low, grad_pairs, preferred_element_type=jnp.float32
        )
        grad_in = jnp.einsum(
            "bsf,ef->bse", grad_pairs, pair_low, preferred_element_type=jnp.float32
        )
        in_gain = in_gain + jnp.sum(grad_in * in_hat, axis=(0, 1))
        in_shift = in_shift + jnp.sum(grad_in, axis=(0, 1))
        input_parts.append(norm_back(grad_in, in_hat, in_inv, in_vectors[0]))
    grad_query_w = jnp.matmul(lat_low.astype(jnp.float32).T, grad_query_rows, precision=highest)
    grad_lat = jnp.matmul(grad_query_rows, query_low.astype(jnp.float32).T, precision=highest)
    zero_index = jnp.zeros((), jnp.int32)
    latent_grad = norm_back(grad_lat, lat_hat, lat_inv, lat_vectors[0]) + lax.dynamic_update_slice(
        jnp.zeros_like(latents), latent_rest, (row_start, zero_index)
    )
    lat_vec_grad = jnp.stack(
        [
            jnp.sum(grad_lat * lat_hat, axis=0),
            jnp.sum(grad_lat, axis=0),
            mlp_gain,
            mlp_shift,
            bias_up,
            bias_down,
        ]
    )
    in_vec_grad = jnp.stack([in_gain, in_shift])
    weight_grads = (
        grad_query_w,
        grad_pair[:, :width_in],
        grad_pair[:, width_in:],
        grad_out_w,
        grad_up_w,
        grad_down_w,
    )
    masters = (w_query, w_key, w_value, w_out, w_up, w_down)
    moments = (mom_query, mom_key, mom_value, mom_out, mom_up, mom_down)
    first_here = jnp.where(seq_index == 0, 0.95, 0.0)
    with_moment = []
    for gradient, moment in zip(weight_grads, moments):
        start = opt_index * moment.shape[0]
        rows = lax.dynamic_slice_in_dim(gradient, start, moment.shape[0], 0) + first_here * moment
        with_moment.append(
            lax.dynamic_update_slice(gradient, rows, (start, zero_index)).astype(jnp.bfloat16)
        )
    summed_low = lax.psum(tuple(with_moment), ("seq", "opt"))
    lat_vec_sum, in_vec_sum, latent_sum = lax.psum(
        (lat_vec_grad, in_vec_grad, latent_grad), ("seq", "opt")
    )
    moments_new = [
        lax.dynamic_slice_in_dim(summed, opt_index * moment.shape[0], moment.shape[0], 0).astype(
            jnp.float32
        )
        for summed, moment in zip(summed_low, moments)
    ]

    def padded(index):
        def pick():
            matrix = summed_low[index].T if index == 3 else summed_low[index]
            return jnp.pad(
                matrix, ((0, width_lat - matrix.shape[0]), (0, width_lat - matrix.shape[1]))
            )

        return pick

    slot = seq_index % 8
    own_matrix = lax.switch(jnp.minimum(slot, 5), [padded(index) for index in range(6)])
    own_result = newton(own_matrix)
    own_result = lax.cond(slot == 3, lambda: own_result.T, lambda: own_result)
    mine = jnp.stack(
        [
            lax.dynamic_slice_in_dim(own_result, opt_index * height, width_lat // opt_size, 0)
            for height in (width_in // opt_size, width_lat // opt_size)
        ]
    )
    is_wide = (slot == 0) | (slot >= 4)
    mine = jnp.where(is_wide, mine[1], mine[0])
    spread = lax.all_gather(mine, "seq", axis=0, tiled=False)
    currents = [
        spread[index, : moment.shape[0], : moment.shape[1]].astype(jnp.float32)
        for index, moment in enumerate(moments)
    ]
    new_masters = update_masters(masters, currents)
    lat_m, lat_v, lat_p = adam_update(lat_vectors, lat_vec_sum, lat_first, lat_second, 0.6, 0.0)
    in_m, in_v, in_p = adam_update(in_vectors, in_vec_sum, in_first, in_second, 0.6, 0.0)
    latent_m, latent_v, latent_p = adam_update(
        latents, latent_sum, latent_first, latent_second, 1.0, 0.1
    )
    block_out = jnp.stack(block_parts)
    input_grad = jnp.stack(input_parts)
    return (
        block_out,
        input_grad,
        moments_new[0],
        moments_new[1],
        moments_new[2],
        moments_new[3],
        moments_new[4],
        moments_new[5],
        new_masters[0],
        new_masters[1],
        new_masters[2],
        new_masters[3],
        new_masters[4],
        new_masters[5],
        lat_m,
        lat_v,
        lat_p,
        in_m,
        in_v,
        in_p,
        latent_m,
        latent_v,
        latent_p,
    )


def solution(mesh):
    small = (mesh.shape["seq"], mesh.shape["opt"]) == (8, 4)
    return jax.shard_map(
        local_small if small else local,
        mesh=mesh,
        in_specs=(
            P(None, "opt", "seq", None),
            P(None, "opt", "seq"),
            P(None, "opt"),
            P(None, "opt", "seq", None),
            P(),
            P(),
            P(),
            P("opt", None),
            P("opt", None),
            P("opt", None),
            P("opt", None),
            P("opt", None),
            P("opt", None),
            P("opt", None),
            P("opt", None),
            P("opt", None),
            P("opt", None),
            P("opt", None),
            P("opt", None),
            P(),
            P(),
            P(),
            P(),
            P(),
            P(),
        ),
        out_specs=(
            P(None, "opt", "seq", None),
            P(None, "opt", "seq", None),
            P("opt", None),
            P("opt", None),
            P("opt", None),
            P("opt", None),
            P("opt", None),
            P("opt", None),
            P("opt", None),
            P("opt", None),
            P("opt", None),
            P("opt", None),
            P("opt", None),
            P("opt", None),
            P(),
            P(),
            P(),
            P(),
            P(),
            P(),
            P(),
            P(),
            P(),
        ),
        check_vma=False,
    )
```

```python
import functools
import types

import jax
import jax.numpy as jnp
from jax import lax
from jax.experimental import pallas as pl
from jax.experimental.pallas import tpu as pltpu
from jax.sharding import PartitionSpec as P

D_LAT = 1280
HEADS = 8
HEAD_DIM = 96
E_IN = 768
STEP = 10
OUT_FAN = 4
TILE = 256
PARTS = (4, 4, 4, 4, 8, 8)
AHEAD = 2
POINTS = {1: (0, 0), 2: (4, 0), 3: (1, 0), 5: (0, 1), 6: (4, 1), 7: (1, 1)}
VMEM_LIMIT = 60 * 2**20
MESH = pl.DeviceIdType.MESH


highest = lax.Precision.HIGHEST
coef_one = 3.4445
coef_two = -4.775
coef_three = 2.0315


def layer_norm(values, scale_vec, offset):
    center = jnp.mean(values, axis=-1, keepdims=True)
    shifted = values - center
    inverse = lax.rsqrt(jnp.mean(shifted * shifted, axis=-1, keepdims=True) + 1e-05)
    normal_hat = shifted * inverse
    return (normal_hat * scale_vec + offset, normal_hat, inverse)


def norm_back(grad_out, normal_hat, inverse, scale_vec):
    scaled = grad_out * scale_vec
    return inverse * (
        scaled
        - jnp.mean(scaled, axis=-1, keepdims=True)
        - normal_hat * jnp.mean(scaled * normal_hat, axis=-1, keepdims=True)
    )


def exact_gelu(values):
    return jax.nn.gelu(values, approximate=False)


def masked_scores(query_heads, key_heads, usable, score_scale):
    scores = (
        jnp.einsum("nhd,bshd->bhns", query_heads, key_heads, preferred_element_type=jnp.float32)
        * score_scale
    )
    return jnp.where(usable[:, None, None, :], scores, -1e30)


def polynomial(low, gram, poly):
    side_tiles = gram.shape[0] // TILE

    def mirror(target, block, i):
        own = slice(i * TILE, (i + 1) * TILE)
        target[own, i * TILE :] = block
        for j in range(i + 1, side_tiles):
            part = block[:, (j - i) * TILE : (j - i + 1) * TILE]
            target[j * TILE : (j + 1) * TILE, own] = part.T

    for i in range(side_tiles):
        own = slice(i * TILE, (i + 1) * TILE)
        block = lax.dot_general(
            low[:, own],
            low[:, i * TILE :],
            (((0,), (0,)), ((), ())),
            preferred_element_type=jnp.float32,
        )
        mirror(gram, block.astype(jnp.bfloat16), i)
    for i in range(side_tiles):
        own = slice(i * TILE, (i + 1) * TILE)
        block = coef_three * jnp.dot(
            gram[own, :], gram[:, i * TILE :], preferred_element_type=jnp.float32
        ) + coef_two * gram[own, i * TILE :].astype(jnp.float32)
        mirror(poly, block.astype(jnp.bfloat16), i)


def newton_body(rows_ref, out_ref, wide, low, gram, poly, total):
    count, side = rows_ref.shape
    row_tiles = count // TILE
    total[0] = 0.0

    def add_squares(tile, carry):
        block = rows_ref[pl.ds(tile * TILE, TILE), :].astype(jnp.float32)
        total[0] = total[0] + jnp.sum(block * block)
        return carry

    lax.fori_loop(0, row_tiles, add_squares, 0)
    scale = 1.0 / (jnp.sqrt(jnp.full((1, 1), total[0], jnp.float32)) + 1e-07)

    def normalise(tile, carry):
        block = rows_ref[pl.ds(tile * TILE, TILE), :].astype(jnp.float32) * scale
        wide[pl.ds(tile * TILE, TILE), :] = block
        low[pl.ds(tile * TILE, TILE), :] = block.astype(jnp.bfloat16)
        return carry

    lax.fori_loop(0, row_tiles, normalise, 0)

    def sweep(index, carry):
        polynomial(low, gram, poly)

        def update(tile, inner):
            rows = pl.ds(tile * TILE, TILE)
            block = coef_one * wide[rows, :] + jnp.dot(
                low[rows, :], poly[...], preferred_element_type=jnp.float32
            )
            wide[rows, :] = block
            low[rows, :] = block.astype(jnp.bfloat16)
            return inner

        lax.fori_loop(0, row_tiles, update, 0)
        return carry

    lax.fori_loop(0, 5, sweep, 0)
    out_ref[...] = low[...]


def newton(rows):
    shape = rows.shape
    return pl.pallas_call(
        newton_body,
        out_shape=jax.ShapeDtypeStruct(shape, jnp.bfloat16),
        in_specs=[pl.BlockSpec(memory_space=pltpu.VMEM)],
        out_specs=pl.BlockSpec(memory_space=pltpu.VMEM),
        scratch_shapes=[
            pltpu.VMEM(shape, jnp.float32),
            pltpu.VMEM(shape, jnp.bfloat16),
            pltpu.VMEM((shape[1], shape[1]), jnp.bfloat16),
            pltpu.VMEM((shape[1], shape[1]), jnp.bfloat16),
            pltpu.SMEM((1,), jnp.float32),
        ],
        compiler_params=pltpu.CompilerParams(vmem_limit_bytes=60 * 2**20),
        name="newton",
    )(rows)


CORE, X, Y, Z0, Z1 = range(5)
LEAD, ROWS, COLS = range(3)
UP, DOWN, KEY, VALUE, OUT, QUERY = range(6)
ROUTES = (
    ((Y, ROWS), (Z0, ROWS), (Z1, ROWS)),
    ((Z0, ROWS), (Y, ROWS), (Z1, ROWS)),
    ((X, LEAD), (Y, ROWS), (Z0, ROWS), (Z1, ROWS)),
    ((Z0, ROWS), (X, LEAD), (Y, ROWS), (Z1, ROWS)),
    ((Y, ROWS), (Z0, ROWS), (Z1, ROWS)),
    ((CORE, COLS), (X, ROWS), (Y, ROWS), (Z0, ROWS), (Z1, ROWS)),
)
Y_FIRST = (UP, KEY, OUT)
SLOTS = (3, 0, 7, 4, 2, 5)


def partners(seq, opt):
    bits = (opt % 2, opt // 2, seq % 2, (seq // 2) % 2, seq // 4)
    steps = ((0, 1), (0, 2), (1, 0), (2, 0), (4, 0))
    targets = [
        (seq + (1 - 2 * bit) * along_seq, opt + (1 - 2 * bit) * along_opt)
        for bit, (along_seq, along_opt) in zip(bits, steps)
    ]
    return bits, targets


def greet(targets):
    barrier = pltpu.get_barrier_semaphore()
    for target in targets:
        pl.semaphore_signal(barrier, inc=1, device_id=target, device_id_type=MESH)
    pl.semaphore_wait(barrier, len(targets))


class Courier:
    def __init__(self, send_sem, recv_sem):
        self.send_sem, self.recv_sem, self.started = send_sem, recv_sem, []

    def send(self, source, target_ref, device):
        index = len(self.started)
        copy = pltpu.make_async_remote_copy(
            src_ref=source,
            dst_ref=target_ref,
            send_sem=self.send_sem.at[index],
            recv_sem=self.recv_sem.at[index],
            device_id=device,
            device_id_type=MESH,
        )
        copy.start()
        self.started.append(copy)
        return copy

    def finish(self):
        for copy in self.started:
            copy.wait_send()


class Loader:
    def __init__(self, sem):
        self.sem, self.count = sem, 0

    def start(self, source, target):
        copy = pltpu.make_async_copy(source, target, self.sem.at[self.count])
        self.count += 1
        copy.start()
        return copy


def rows_at(start, count, unit=16):
    return pl.ds(pl.multiple_of(start, unit), count)


def lanes_at(start, count):
    return pl.ds(pl.multiple_of(start, 128), count)


def clear(ref):
    def body(step, carry):
        ref[rows_at(step * 32, 32), :] = jnp.zeros((32, ref.shape[1]), ref.dtype)
        return carry

    lax.fori_loop(0, ref.shape[0] // 32, body, 0)


def dot_nn(left, right):
    return jnp.dot(left, right, preferred_element_type=jnp.float32)


def dot_nt(left, right):
    return lax.dot_general(
        left, right, (((1,), (1,)), ((), ())), preferred_element_type=jnp.float32
    )


def dot_tn(left, right):
    return lax.dot_general(
        left, right, (((0,), (0,)), ((), ())), preferred_element_type=jnp.float32
    )


def named(keys, refs):
    return types.SimpleNamespace(**dict(zip(keys, refs)))


def low(values):
    return values.astype(jnp.bfloat16)


def wide(values):
    return values.astype(jnp.float32)


def norm(values):
    shifted = values - jnp.mean(values, axis=-1, keepdims=True)
    inverse = lax.rsqrt(jnp.mean(shifted * shifted, axis=-1, keepdims=True) + 1e-05)
    return shifted * inverse, inverse


def cut(ref, kind, bit):
    if kind == LEAD:
        return ref.at[bit]
    rows, cols = ref.shape[-2:]
    lead = (slice(None),) * (len(ref.shape) - 2)
    if kind == ROWS:
        return ref.at[(*lead, rows_at(bit * (rows // 2), rows // 2), slice(None))]
    return ref.at[(*lead, slice(None), lanes_at(bit * (cols // 2), cols // 2))]


def half_shape(shape, kind):
    if kind == LEAD:
        return shape[1:]
    if kind == ROWS:
        return (*shape[:-2], shape[-2] // 2, shape[-1])
    return (*shape[:-1], shape[-1] // 2)


def add_into(total, term):
    def body(step, carry):
        at = rows_at(step * 16, 16)
        for lead in range(total.shape[0]) if len(total.shape) == 3 else (None,):
            where = (at, slice(None)) if lead is None else (lead, at, slice(None))
            total[where] = low(wide(total[where]) + wide(term[where]))
        return carry

    lax.fori_loop(0, total.shape[-2] // 16, body, 0)


class Halving:
    def __init__(self, courier, bits, targets, sums, stages):
        self.courier, self.bits, self.targets = courier, bits, targets
        self.sums, self.stages, self.pending = sums, stages, {}

    def give(self, which, stage):
        axis, kind = ROUTES[which][stage]
        self.pending[which] = self.courier.send(
            cut(self.sums[which], kind, 1 - self.bits[axis]),
            self.stages[which][stage],
            self.targets[axis],
        )

    def take(self, which, stage):
        axis, kind = ROUTES[which][stage]
        self.pending[which].wait_recv()
        add_into(self.stages[which][stage], cut(self.sums[which], kind, self.bits[axis]))
        self.sums[which] = self.stages[which][stage]


def chain_of(which, shape):
    chain = []
    for _, kind in ROUTES[which]:
        shape = half_shape(shape, kind)
        chain.append(shape)
    return chain


def head_lanes(first, shape):
    row = lax.broadcasted_iota(jnp.int32, shape, 0) - first
    column = lax.broadcasted_iota(jnp.int32, shape, 1)
    inside = (row >= 0) & (row < HEADS)
    inside &= (column >= row * HEAD_DIM) & (column < (row + 1) * HEAD_DIM)
    return inside.astype(jnp.float32)


def pass_body(keys, *refs):
    r = named(keys, refs)
    seq, opt = lax.axis_index("seq"), lax.axis_index("opt")
    bits, targets = partners(seq, opt)
    core, y = bits[CORE], bits[Y]
    opt_x = targets[X][1]
    ring = [((seq + step) % 8, opt) for step in range(1, 8)]
    micro, span = r.usable.shape[0], r.usable.shape[2]
    width = r.in_low.shape[1]
    lat_count, width_lat = r.latents.shape
    own = lat_count // 8
    scale = HEAD_DIM ** (-0.5)
    load = Loader(r.local)
    loads = [
        load.start(source, target)
        for source, target in (
            (r.w_key, r.f_key),
            (r.w_value, r.f_value),
            (r.w_query, r.f_query),
            (r.w_out, r.f_out),
            (r.w_up, r.f_up),
            (r.w_down, r.f_down),
        )
    ]
    clear(r.base)
    greet([targets[CORE], targets[X], *ring])
    courier = Courier(r.send, r.recv)

    def begin(full, rows, axis):
        block = full.at[rows_at(opt * rows, rows)]
        half = full.at[rows_at(opt * rows + bits[axis] * (rows // 2), rows // 2)]
        return [
            courier.send(half, half, targets[X]),
            courier.send(block, block, targets[CORE]),
        ]

    def relay(full, rows, axis, state):
        state[0].wait_recv()
        half = full.at[rows_at(opt_x * rows + bits[axis] * (rows // 2), rows // 2)]
        state.append(courier.send(half, half, targets[axis]))
        state.append(courier.send(half, half, targets[CORE]))

    def relay_more(full, rows, axis, state):
        state[2].wait_recv()
        half = full.at[rows_at(opt_x * rows + (1 - bits[axis]) * (rows // 2), rows // 2)]
        state.append(courier.send(half, half, targets[CORE]))

    def complete(state):
        for index in (1, 3, 4):
            state[index].wait_recv()

    def place(full, source):
        rows = source.shape[0]

        def body(step, carry):
            at = rows_at(step * 32, 32)
            full[rows_at(opt * rows + step * 32, 32), :] = low(source[at, :])
            return carry

        lax.fori_loop(0, rows // 32, body, 0)

    key_rows = r.f_key.shape[0]
    loads[0].wait()
    loads[1].wait()

    def place_pair(step, carry):
        at = rows_at(opt * key_rows + step * 32, 32)
        source = rows_at(step * 32, 32)
        r.pair_full[at, :width] = low(r.f_key[source, :])
        r.pair_full[at, width:] = low(r.f_value[source, :])
        return carry

    lax.fori_loop(0, key_rows // 32, place_pair, 0)
    pair_state = begin(r.pair_full, key_rows, Y)

    def norm_in(step, carry):
        at = rows_at(step * 64, 64)
        hat, inverse = norm(wide(r.tokens[at, :]))
        r.in_hat[at, :] = hat
        r.in_inv[at, :] = inverse
        r.in_low[at, :] = low(hat * r.in_vectors[0:1, :] + r.in_vectors[1:2, :])
        return carry

    lax.fori_loop(0, r.in_low.shape[0] // 64, norm_in, 0)
    def norm_lat(step, carry):
        at = rows_at(step * 32, 32)
        hat, _ = norm(r.latents[at, :])
        r.lat_low[at, :] = low(hat * r.lat_vectors[0:1, :] + r.lat_vectors[1:2, :])
        return carry

    lax.fori_loop(0, lat_count // 32, norm_lat, 0)
    query_rows, out_rows, up_rows = (
        r.f_query.shape[0],
        r.f_out.shape[0],
        r.f_up.shape[0],
    )
    for index in range(4):

        @pl.when(opt == index)
        def _(index=index):
            r.lat_block[...] = r.lat_low[:, index * up_rows : (index + 1) * up_rows]

    for index, (full, staged) in enumerate(
        (
            (r.query_full, r.f_query),
            (r.out_full, r.f_out),
            (r.up_full, r.f_up),
            (r.down_full, r.f_down),
        )
    ):
        loads[2 + index].wait()
        place(full, staged)
    relay(r.pair_full, key_rows, Y, pair_state)
    query_state = begin(r.query_full, query_rows, Z0)
    relay(r.query_full, query_rows, Z0, query_state)
    out_state = begin(r.out_full, out_rows, Y)
    relay_more(r.pair_full, key_rows, Y, pair_state)
    complete(pair_state)

    def project(step, carry):
        at = rows_at(step * 256, 256)
        r.pairs[at, :] = low(dot_nn(r.in_low[at, :], r.pair_full[...]))
        return carry

    lax.fori_loop(0, r.in_low.shape[0] // 256, project, 0)
    relay(r.out_full, out_rows, Y, out_state)
    up_state = begin(r.up_full, up_rows, Z0)
    relay_more(r.query_full, query_rows, Z0, query_state)
    complete(query_state)

    def project_query(step, carry):
        at = rows_at(step * 128, 128)
        r.queries[at, :] = low(dot_nn(r.lat_low[at, :], r.query_full[...]))
        return carry

    lax.fori_loop(0, lat_count // 128, project_query, 0)

    local_rows = rows_at(opt * (micro * own), micro * own)
    shared = []

    def hand_over(array):
        view = array.at[local_rows]
        shared.append(
            (array, courier.send(view, view, targets[X]), courier.send(view, view, targets[CORE]))
        )

    back_rows = r.cotangent[...]
    r.x_cot[local_rows, :] = back_rows

    to_owner = []
    for m in range(micro):
        at = slice(m * span, (m + 1) * span)
        usable = r.usable[m] > 0.5
        for h in range(HEADS):
            ch = slice(h * HEAD_DIM, (h + 1) * HEAD_DIM)
            ch_v = slice(width + h * HEAD_DIM, width + (h + 1) * HEAD_DIM)
            masked = jnp.where(
                usable, dot_nt(r.queries[:, ch], r.pairs[at, ch]) * scale, -1e30
            )
            top = jnp.max(masked, axis=1, keepdims=True)
            weights = jnp.exp(masked - top)
            sums = jnp.sum(weights, axis=1, keepdims=True)
            r.weights[m * HEADS + h] = weights
            lane = m * HEADS + h
            r.top[:, lane : lane + 1] = top
            r.lse[:, lane : lane + 1] = top + jnp.log(sums)
            r.part[m, :, ch] = low(dot_nn(low(weights), r.pairs[at, ch_v]) / sums)
        for target in ring:
            rows = rows_at(target[0] * own, own)
            to_owner.append(
                courier.send(r.part.at[m, rows], r.part_in.at[seq, m], target)
            )
        if m == 0:
            relay(r.up_full, up_rows, Z0, up_state)
            down_state = begin(r.down_full, up_rows, Y)
            relay_more(r.out_full, out_rows, Y, out_state)
    for target in ring:
        rows = rows_at(target[0] * own, own)
        to_owner.append(courier.send(r.lse.at[rows], r.lse_in.at[seq], target))
    mine = rows_at(seq * own, own)
    r.part_in[seq] = r.part[:, mine, :]
    r.lse_in[seq] = r.lse[mine, :]
    relay(r.down_full, up_rows, Y, down_state)
    hand_over(r.x_cot)
    relay_more(r.up_full, up_rows, Z0, up_state)
    relay_more(r.down_full, up_rows, Y, down_state)
    for copy in to_owner:
        copy.wait_recv()

    peak = r.lse_in[0]
    for peer in range(1, 8):
        peak = jnp.maximum(peak, r.lse_in[peer])
    total = jnp.exp(r.lse_in[0] - peak)
    for peer in range(1, 8):
        total = total + jnp.exp(r.lse_in[peer] - peak)
    lse_all = peak + jnp.log(total)
    spread_heads = [head_lanes(m * HEADS, (128, width)) for m in range(micro)]
    collect_heads = [head_lanes((micro + m) * HEADS, (128, width)) for m in range(micro)]
    for m in range(micro):
        rows = slice(m * own, (m + 1) * own)
        for peer in range(8):
            share = jnp.dot(
                jnp.exp(r.lse_in[peer] - lse_all),
                spread_heads[m],
                precision=highest,
                preferred_element_type=jnp.float32,
            ) * wide(r.part_in[peer, m])
            r.attended[rows, :] = share if peer == 0 else r.attended[rows, :] + share
    att_low = low(r.attended[...])
    r.x_att[local_rows, :] = att_low
    hand_over(r.x_att)
    back_rows = r.cotangent[...]
    complete(out_state)
    own_latents = jnp.concatenate([r.latents[mine, :]] * micro, axis=0)
    r.hidden[...] = own_latents + dot_nn(att_low, r.out_full[...])
    mlp_hat, mlp_inv = norm(r.hidden[...])
    r.mlp_hat[...] = mlp_hat
    mlp_low = low(mlp_hat * r.lat_vectors[2:3, :] + r.lat_vectors[3:4, :])
    r.x_mlp[local_rows, :] = mlp_low
    hand_over(r.x_mlp)
    complete(up_state)
    pre_act = dot_nn(mlp_low, r.up_full[...]) + r.lat_vectors[4:5, :]
    cdf = 0.5 * (1.0 + lax.erf(pre_act * 0.7071067811865476))
    act_low = low(pre_act * cdf)
    r.slope[...] = cdf + pre_act * jnp.exp(-0.5 * pre_act * pre_act) * 0.3989422804014327
    r.x_act[local_rows, :] = act_low
    hand_over(r.x_act)
    complete(down_state)
    grad_pre = low(dot_nt(back_rows, r.down_full[...]) * r.slope[...])
    r.x_pre[local_rows, :] = grad_pre
    hand_over(r.x_pre)
    grad_mlp = dot_nt(grad_pre, r.up_full[...])
    mlp_hat = r.mlp_hat[...]
    r.vectors[...] = jnp.zeros_like(r.vectors)
    r.vectors[0:1, :] = jnp.sum(grad_mlp * mlp_hat, axis=0, keepdims=True)
    r.vectors[1:2, :] = jnp.sum(grad_mlp, axis=0, keepdims=True)
    r.vectors[2:3, :] = jnp.sum(wide(grad_pre), axis=0, keepdims=True)
    r.vectors[3:4, :] = jnp.sum(wide(back_rows), axis=0, keepdims=True)
    scaled = grad_mlp * r.lat_vectors[2:3, :]
    grad_hidden = wide(back_rows) + mlp_inv * (
        scaled
        - jnp.mean(scaled, axis=-1, keepdims=True)
        - mlp_hat * jnp.mean(scaled * mlp_hat, axis=-1, keepdims=True)
    )
    rest = grad_hidden[:own]
    for m in range(1, micro):
        rest = rest + grad_hidden[m * own : (m + 1) * own]
    r.rest[...] = low(rest)
    grad_branch = low(grad_hidden)
    r.x_branch[local_rows, :] = grad_branch
    hand_over(r.x_branch)
    grad_own = low(dot_nt(grad_branch, r.out_full[...]))
    products = wide(grad_own) * r.attended[...]
    back = jnp.where(
        lax.broadcasted_iota(jnp.int32, lse_all.shape, 1) < micro * HEADS, lse_all, 0.0
    )
    for m in range(micro):
        rows = slice(m * own, (m + 1) * own)
        r.grad_att[m, mine, :] = grad_own[rows]
        back = back + lax.dot_general(
            products[rows],
            collect_heads[m],
            (((1,), (1,)), ((), ())),
            precision=highest,
            preferred_element_type=jnp.float32,
        )
    r.back[mine, :] = back
    returns = []
    for target in ring:
        for view in (r.grad_att.at[:, mine], r.back.at[mine]):
            returns.append(courier.send(view, view, target))
    r.block_out[...] = low(
        r.hidden[...] + dot_nn(act_low, r.down_full[...]) + r.lat_vectors[5:6, :]
    )
    passed = []
    for array, across, _ in shared:
        across.wait_recv()
        view = array.at[rows_at(opt_x * (micro * own), micro * own)]
        passed.append(courier.send(view, view, targets[CORE]))
    for _, _, beside in shared:
        beside.wait_recv()
    for copy in passed:
        copy.wait_recv()
    half = lanes_at(core * (width_lat // 2), width_lat // 2)
    for target, left, right in (
        (r.grad_up, r.x_mlp, r.x_pre),
        (r.grad_down, r.x_act, r.x_cot),
        (r.grad_out, r.x_att, r.x_branch),
    ):
        rows = target.shape[0]
        for tile in range(rows // 128):
            cols = lanes_at(bits[X] * rows + tile * 128, 128)
            target[tile * 128 : (tile + 1) * 128, :] = low(dot_tn(left[:, cols], right[:, half]))
    halving = Halving(
        courier,
        bits,
        targets,
        {UP: r.grad_up, DOWN: r.grad_down, OUT: r.grad_out},
        {
            UP: (r.up_0, r.up_1, r.piece_up),
            DOWN: (r.down_0, r.down_1, r.piece_down),
            OUT: (r.out_0, r.out_1, r.piece_out),
        },
    )
    for which in (UP, DOWN, OUT):
        halving.give(which, 0)
    for moment, staged, slot in zip(
        (r.mom_query, r.mom_key, r.mom_value, r.mom_out, r.mom_up, r.mom_down),
        (r.f_query, r.f_key, r.f_value, r.f_out, r.f_up, r.f_down),
        SLOTS,
    ):

        @pl.when(seq == slot)
        def _(moment=moment, staged=staged):
            copy = pltpu.make_async_copy(moment, staged, r.moment_sem)
            copy.start()
            copy.wait()
            r.base[rows_at(opt * up_rows, staged.shape[0]), : staged.shape[1]] = low(
                0.95 * staged[...]
            )

    own_base = r.base.at[rows_at(opt * up_rows, up_rows)]
    base_across = courier.send(own_base, own_base, targets[X])
    base_beside = courier.send(own_base, own_base, targets[CORE])
    for copy in returns:
        copy.wait_recv()

    for h in range(HEADS):
        if h in POINTS:
            which, stage = POINTS[h]
            halving.take(which, stage)
            halving.give(which, stage + 1)
        ch = slice(h * HEAD_DIM, (h + 1) * HEAD_DIM)
        ch_v = slice(width + h * HEAD_DIM, width + (h + 1) * HEAD_DIM)
        grad_query = None
        for m in range(micro):
            at = slice(m * span, (m + 1) * span)
            lane = m * HEADS + h
            lane_in = (micro + m) * HEADS + h
            prob = r.weights[lane] * jnp.exp(
                r.top[:, lane : lane + 1] - r.back[:, lane : lane + 1]
            )
            grad_att = r.grad_att[m, :, ch]
            grad_prob = dot_nt(grad_att, r.pairs[at, ch_v])
            grad_scores = low(prob * (grad_prob - r.back[:, lane_in : lane_in + 1]))
            part = dot_nn(grad_scores, r.pairs[at, ch])
            grad_query = part if grad_query is None else grad_query + part
            r.grad_pairs[at, ch] = low(scale * dot_tn(grad_scores, r.queries[:, ch]))
            r.grad_pairs[at, ch_v] = low(dot_tn(low(prob), grad_att))
        r.grad_query[:, ch] = low(scale * grad_query)

    part_width = width // 2

    def pair_product(targets_two, which):
        for kind, target in enumerate(targets_two):
            cols = lanes_at(kind * width + which * part_width, part_width)
            right = r.grad_pairs[:, cols]
            for tile in range(width // TILE):
                rows = slice(tile * TILE, (tile + 1) * TILE)
                target[rows, :] = low(dot_tn(r.in_low[:, rows], right))

    base_across.wait_recv()
    other_base = r.base.at[rows_at(opt_x * up_rows, up_rows)]
    base_last = courier.send(other_base, other_base, targets[CORE])
    base_beside.wait_recv()
    pair_product((r.pair_other.at[0], r.pair_other.at[1]), 1 - core)
    pair_copy = courier.send(r.pair_other, r.pair_in, targets[CORE])
    pair_product((r.grad_key, r.grad_value), core)
    r.in_sums[...] = jnp.zeros_like(r.in_sums)

    def norm_in_back(step, carry):
        at = rows_at(step * 128, 128)
        grad_in = dot_nt(r.grad_pairs[at, :], r.pair_full[...])
        hat = r.in_hat[at, :]
        r.in_sums[0:1, :] = r.in_sums[0:1, :] + jnp.sum(grad_in * hat, axis=0, keepdims=True)
        r.in_sums[1:2, :] = r.in_sums[1:2, :] + jnp.sum(grad_in, axis=0, keepdims=True)
        scaled = grad_in * r.in_vectors[0:1, :]
        r.input_grad[at, :] = r.in_inv[at, :] * (
            scaled
            - jnp.mean(scaled, axis=-1, keepdims=True)
            - hat * jnp.mean(scaled * hat, axis=-1, keepdims=True)
        )
        return carry

    lax.fori_loop(0, r.in_low.shape[0] // 128, norm_in_back, 0)
    r.vectors[4:6, :width] = r.in_sums[0:2, :]
    base_last.wait_recv()
    pair_copy.wait_recv()
    add_into(r.grad_key, r.pair_in.at[0])
    add_into(r.grad_value, r.pair_in.at[1])
    for which in (UP, OUT, DOWN):
        halving.take(which, 2)
    courier.finish()


def run_pass(tokens, usable, cotangent, latents, lat_vectors, in_vectors, weights, moments):
    f32, bf16 = jnp.float32, jnp.bfloat16
    w_query, w_key, w_value, w_out, w_up, w_down = weights
    operands = dict(
        tokens=tokens,
        usable=usable,
        cotangent=cotangent,
        latents=latents,
        lat_vectors=lat_vectors,
        in_vectors=in_vectors,
        w_query=w_query,
        w_key=w_key,
        w_value=w_value,
        w_out=w_out,
        w_up=w_up,
        w_down=w_down,
        mom_query=moments[0],
        mom_key=moments[1],
        mom_value=moments[2],
        mom_out=moments[3],
        mom_up=moments[4],
        mom_down=moments[5],
    )
    count, width = tokens.shape
    micro, _, span = usable.shape
    lat_count, width_lat = latents.shape
    own = lat_count // 8
    rows = micro * own
    outputs = dict(
        block_out=((rows, width_lat), bf16),
        input_grad=((count, width), f32),
        grad_key=((width, width // 2), bf16),
        grad_value=((width, width // 2), bf16),
        grad_query=((lat_count, width), bf16),
        vectors=((8, width_lat), f32),
        rest=((own, width_lat), bf16),
        lat_low=((lat_count, width_lat), bf16),
        lat_block=((lat_count, width_lat // 4), bf16),
        query_full=((width_lat, width), bf16),
        base=((width_lat, width_lat), bf16),
    )
    scratch = dict(
        grad_up=((width_lat // 2, width_lat // 2), bf16),
        grad_down=((width_lat // 2, width_lat // 2), bf16),
        grad_out=((width // 2, width_lat // 2), bf16),
        f_query=(w_query.shape, f32),
        f_key=(w_key.shape, f32),
        f_value=(w_value.shape, f32),
        f_out=(w_out.shape, f32),
        f_up=(w_up.shape, f32),
        f_down=(w_down.shape, f32),
        pair_full=((width, 2 * width), bf16),
        out_full=((width, width_lat), bf16),
        up_full=((width_lat, width_lat), bf16),
        down_full=((width_lat, width_lat), bf16),
        in_low=((count, width), bf16),
        in_hat=((count, width), f32),
        in_inv=((count, 1), f32),
        in_sums=((8, width), f32),
        pairs=((count, 2 * width), bf16),
        queries=((lat_count, width), bf16),
        weights=((micro * HEADS, lat_count, span), f32),
        top=((lat_count, 128), f32),
        lse=((lat_count, 128), f32),
        part=((micro, lat_count, width), bf16),
        part_in=((8, micro, own, width), bf16),
        lse_in=((8, own, 128), f32),
        attended=((rows, width), f32),
        hidden=((rows, width_lat), f32),
        mlp_hat=((rows, width_lat), f32),
        slope=((rows, width_lat), f32),
        x_att=((4 * rows, width), bf16),
        x_branch=((4 * rows, width_lat), bf16),
        x_mlp=((4 * rows, width_lat), bf16),
        x_pre=((4 * rows, width_lat), bf16),
        x_act=((4 * rows, width_lat), bf16),
        x_cot=((4 * rows, width_lat), bf16),
        grad_att=((micro, lat_count, width), bf16),
        back=((lat_count, 128), f32),
        grad_pairs=((count, 2 * width), bf16),
        pair_other=((2, width, width // 2), bf16),
        pair_in=((2, width, width // 2), bf16),
    )
    for which, name in ((UP, "up"), (DOWN, "down"), (OUT, "out")):
        chain = chain_of(which, scratch["grad_" + name][0])
        for stage, shape in enumerate(chain[:-1]):
            scratch[f"{name}_{stage}"] = (shape, bf16)
        outputs["piece_" + name] = (chain[-1], bf16)
    copies = 5 * 5 + 7 * micro + 7 + 14 + 18 + 1 + 3 + 9
    sems = dict(
        send=pltpu.SemaphoreType.DMA((copies,)),
        recv=pltpu.SemaphoreType.DMA((copies,)),
        local=pltpu.SemaphoreType.DMA((6,)),
        moment_sem=pltpu.SemaphoreType.DMA,
    )
    keys = (*operands, *outputs, *scratch, *sems)
    vmem, anywhere = pl.BlockSpec(memory_space=pltpu.VMEM), pl.BlockSpec(memory_space=pl.ANY)
    results = pl.pallas_call(
        functools.partial(pass_body, keys),
        out_shape=[jax.ShapeDtypeStruct(*spec) for spec in outputs.values()],
        in_specs=[vmem] * 6 + [anywhere] * 12,
        out_specs=[vmem] * len(outputs),
        scratch_shapes=[*(pltpu.VMEM(*spec) for spec in scratch.values()), *sems.values()],
        compiler_params=pltpu.CompilerParams(
            collective_id=2, has_side_effects=True, vmem_limit_bytes=VMEM_LIMIT
        ),
        name="pass",
    )(*operands.values())
    return named(outputs, results)


def tail_body(keys, *refs):
    r = named(keys, refs)
    seq, opt = lax.axis_index("seq"), lax.axis_index("opt")
    bits, targets = partners(seq, opt)
    core, z0, z1, y, x = bits[CORE], bits[Z0], bits[Z1], bits[Y], bits[X]
    ring = [((seq + step) % 8, opt) for step in range(1, 8)]
    height = r.lat_block.shape[1]
    load = Loader(r.local)
    loads = [
        load.start(source, target)
        for source, target in (
            (r.base, r.h_base),
            (r.lat_low, r.h_lat_low),
            (r.query_full, r.h_query_full),
            (r.latents, r.h_latents),
        )
    ]
    clear(r.g_full.at[0])
    clear(r.g_full.at[1])
    beyond = [((seq + step) % 8, targets[X][1]) for step in range(8)]
    greet([targets[CORE], *ring, *beyond])
    courier = Courier(r.send, r.recv)
    sums = {UP: r.up, DOWN: r.down, OUT: r.out, KEY: r.key, VALUE: r.value, QUERY: r.query}
    halving = Halving(
        courier,
        bits,
        targets,
        sums,
        {
            KEY: (r.key_0, r.key_1, r.key_2, r.key_3),
            VALUE: (r.value_0, r.value_1, r.value_2, r.value_3),
            QUERY: (r.query_0, r.query_1, r.query_2, r.query_3, r.query_4),
        },
    )
    for which in (QUERY, KEY, VALUE):
        halving.give(which, 0)
    def piece_place(which, seq_from, x_from):
        bit_y, bit_z0, bit_z1 = seq_from % 2, (seq_from // 2) % 2, seq_from // 4
        high, mid = (bit_y, bit_z0) if which in Y_FIRST else (bit_z0, bit_y)
        rows = sums[which].shape[0]
        return rows_at(x_from * (2 * height) + high * height + (mid * 2 + bit_z1) * rows, rows)

    def piece_copy(index, which, seq_from, x_from, same):
        cols = sums[which].shape[1]
        place = piece_place(which, seq_from, x_from)
        return pltpu.make_async_remote_copy(
            src_ref=sums[which],
            dst_ref=r.g_full.at[core, place, pl.ds(0, cols)],
            send_sem=r.piece_send.at[index, 0 if same else 1],
            recv_sem=r.piece_recv.at[0 if same else 1, seq_from],
            device_id=(SLOTS[index], opt if same else targets[X][1]),
            device_id_type=MESH,
        )

    def offer(index, which):
        piece_copy(index, which, seq, x, False).start()

        @pl.when(seq != SLOTS[index])
        def _():
            piece_copy(index, which, seq, x, True).start()

        @pl.when(seq == SLOTS[index])
        def _():
            cols = sums[which].shape[1]
            r.g_full[core, piece_place(which, seq, x), :cols] = sums[which][...]

    owned = ((1, KEY), (2, VALUE), (3, OUT), (4, UP), (5, DOWN))
    for index, which in owned[2:]:
        offer(index, which)
    big = (seq == SLOTS[4]) | (seq == SLOTS[5])
    exchange = pltpu.make_async_remote_copy(
        src_ref=r.g_full.at[core],
        dst_ref=r.g_full.at[core],
        send_sem=r.join_sem.at[0],
        recv_sem=r.join_sem.at[1],
        device_id=targets[CORE],
        device_id_type=MESH,
    )

    def collect(some):
        for index, which in some:

            @pl.when(seq == SLOTS[index])
            def _(index=index, which=which):
                for seq_from in range(8):
                    if seq_from != SLOTS[index]:
                        piece_copy(index, which, seq_from, x, True).wait_recv()
                    piece_copy(index, which, seq_from, 1 - x, False).wait_recv()

    r.vectors_sum[...] = r.vectors[...]
    vector_copy = courier.send(r.vectors, r.vectors_in.at[0], targets[CORE])
    rest_width = r.rest.shape[1] // 2
    column = lanes_at(core * rest_width, rest_width)
    rest_copy = courier.send(
        r.rest.at[:, lanes_at((1 - core) * rest_width, rest_width)], r.rest_in.at[0], targets[CORE]
    )
    halving.take(QUERY, 0)
    halving.give(QUERY, 1)
    vector_copy.wait_recv()
    r.vectors_sum[...] = r.vectors_sum[...] + r.vectors_in[0]
    rest_copy.wait_recv()
    r.rest_sum[...] = low(wide(r.rest[:, column]) + wide(r.rest_in[0]))
    rest_copy = courier.send(r.rest_sum, r.rest_in.at[1], targets[X])
    for stage in range(4):
        if stage == 3:
            collect(owned[3:])

            @pl.when(big)
            def _():
                exchange.start()

        axis = (X, Y, Z0, Z1)[stage]
        r.vectors_out[stage] = r.vectors_sum[...]
        vector_copy = courier.send(
            r.vectors_out.at[stage], r.vectors_in.at[stage + 1], targets[axis]
        )
        if stage > 0:
            rest_copy.wait_recv()
            if stage == 1:
                r.rest_all[z1, z0, y, :, column] = low(wide(r.rest_sum[...]) + wide(r.rest_in[1]))
            every = slice(None)
            lead = ((z1, z0, y), (every, z0, y), (every, every, y))[stage - 1]
            view = r.rest_all.at[(*lead, every, column)]
            rest_copy = courier.send(view, view, targets[(Z1, Z0, Y)[stage - 1]])
        for which in (QUERY, KEY, VALUE):
            own_stage = stage + 1 if which == QUERY else stage
            halving.take(which, own_stage)
            if stage < 3:
                halving.give(which, own_stage + 1)
        vector_copy.wait_recv()
        r.vectors_sum[...] = r.vectors_sum[...] + r.vectors_in[stage + 1]
    rest_copy.wait_recv()
    view = r.rest_all.at[:, :, :, :, column]
    rest_copy = courier.send(view, view, targets[CORE])

    for index, which in owned[:2]:
        offer(index, which)
    rows, width = sums[QUERY].shape
    query_column = lanes_at(core * width, width)
    start = (x * 8 + y * 4 + z0 * 2 + z1) * rows
    r.query_all[rows_at(start, rows), query_column] = sums[QUERY][...]
    view = r.query_all.at[rows_at(start, rows), query_column]
    query_copies = [courier.send(view, view, target) for target in ring]

    gathered = (r.g_up, r.g_down, r.g_key, r.g_value, r.g_out)
    full = (r.n_up, r.n_down, r.n_key, r.n_value, r.n_out)
    for which in range(5):
        high, mid = (y, z0) if which in Y_FIRST else (z0, y)
        rows = sums[which].shape[0]
        gathered[which][rows_at((high * 4 + mid * 2 + z1) * rows, rows), :] = sums[which][...]

    def gather(which, step):
        first_axis, last_axis = (Y, Z0) if which in Y_FIRST else (Z0, Y)
        high, mid = bits[first_axis], bits[last_axis]
        rows = sums[which].shape[0]
        if step < 3:
            base, count = ((high * 4 + mid * 2 + z1, 1), (high * 4 + mid * 2, 2), (high * 4, 4))[
                step
            ]
            source = target = gathered[which].at[rows_at(base * rows, count * rows)]
        else:
            cols = sums[which].shape[1]
            source = gathered[which].at[rows_at((1 - core) * (4 * rows), 4 * rows)]
            target = full[which].at[:, lanes_at(core * cols, cols)]
        return pltpu.make_async_remote_copy(
            src_ref=source,
            dst_ref=target,
            send_sem=r.gather_send.at[which, step],
            recv_sem=r.gather_recv.at[which, step],
            device_id=targets[(Z1, last_axis, first_axis, CORE)[step]],
            device_id_type=MESH,
        )

    for which in range(5):
        gather(which, 0).start()
    for copy in query_copies:
        copy.wait_recv()
    many_rows = 8 * sums[QUERY].shape[0]
    view = r.query_all.at[rows_at(x * many_rows, many_rows), query_column]
    query_across = courier.send(view, view, targets[X])
    collect(owned[:3])

    @pl.when(jnp.logical_not(big))
    def _():
        exchange.start()

    query_across.wait_recv()
    view = r.query_all.at[:, query_column]
    query_beside = courier.send(view, view, targets[CORE])
    exchange.wait_recv()

    for copy in loads:
        copy.wait()
    side = r.whole.shape[1]
    tiles = side // TILE
    small = (seq == SLOTS[0]) | (seq == SLOTS[1]) | (seq == SLOTS[2]) | (seq == SLOTS[3])
    both = 2 * width
    turned = r.out.shape[0] * 4
    r.total[0] = 0.0

    def joined(at, lanes, block):
        r.wide[at, lanes] = block
        r.total[0] = r.total[0] + jnp.sum(block * block)

    def over_tiles(body):
        def step(tile, carry):
            body(rows_at(tile * TILE, TILE), tile)
            return carry

        lax.fori_loop(0, tiles, step, 0)

    @pl.when(big)
    def _():
        def body(at, tile):
            for index in range(2):
                lanes = slice(index * (side // 2), (index + 1) * (side // 2))
                joined(at, lanes, wide(r.h_base[at, lanes]) + wide(r.g_full[index, at, :]))

        over_tiles(body)

    @pl.when((seq == SLOTS[1]) | (seq == SLOTS[2]))
    def _():
        def body(at, tile):
            for index in range(2):
                lanes = slice(index * width, (index + 1) * width)
                joined(at, lanes, wide(r.h_base[at, lanes]) + wide(r.g_full[index, at, :width]))

        over_tiles(body)

    query_beside.wait_recv()
    rest_copy.wait_recv()

    @pl.when(seq == SLOTS[0])
    def _():
        def body(at, tile):
            lanes = slice(0, both)
            joined(
                at,
                lanes,
                wide(r.h_base[at, lanes])
                + dot_tn(r.h_lat_low[:, lanes_at(tile * TILE, TILE)], r.query_all[...]),
            )

        over_tiles(body)

    @pl.when(seq == SLOTS[3])
    def _():
        for block in range(4):
            at = slice(block * height, block * height + turned)
            for index in range(2):
                lanes = slice(index * (side // 2), (index + 1) * (side // 2))
                part = wide(r.h_base[at, lanes]) + wide(r.g_full[index, at, :])
                joined(lanes, slice(block * turned, (block + 1) * turned), part.T)

    scale = 1.0 / (jnp.sqrt(jnp.full((1, 1), r.total[0], jnp.float32)) + 1e-07)

    def normalise(cols):
        def body(at, tile):
            block = r.wide[at, :cols] * scale
            r.wide[at, :cols] = block
            r.whole[at, :cols] = low(block)

        over_tiles(body)

    def update(at, cols):
        block = coef_one * r.wide[at, :cols] + dot_nn(r.whole[at, :cols], r.poly[:cols, :cols])
        r.wide[at, :cols] = block
        r.whole[at, :cols] = low(block)

    def gathers(step, action):
        for which in range(5):
            action(gather(which, step))

    def gather_take(step):
        gathers(step, lambda copy: copy.wait_recv())

    def gather_give(step):
        gathers(step, lambda copy: copy.start())
        if step == 3:
            for which in range(5):
                rows, cols = gathered[which].shape
                full[which][:, lanes_at(core * cols, cols)] = gathered[which][
                    rows_at(core * (rows // 2), rows // 2), :
                ]

    outs = (r.o_query, r.o_key, r.o_value, r.o_out, r.o_up, r.o_down)
    z, depth = seq // 2, 4

    def copy(which, part, way):
        out = outs[which]
        cols = out.shape[1] * 4 // PARTS[which]
        rows = out.shape[0] // 4
        across = out.shape[1] // cols
        view = out.at[pl.ds(part // across * rows, rows), pl.ds(part % across * cols, cols)]
        return pltpu.make_async_remote_copy(
            src_ref=view,
            dst_ref=view,
            send_sem=r.spread_send.at[way, which * max(PARTS) + part],
            recv_sem=r.spread_recv.at[which * max(PARTS) + part],
            device_id=((seq + 2, opt), (seq - 2, opt), targets[Y])[way],
            device_id_type=MESH,
        )

    def for_ways(which, mine, action):
        slot_y, slot_z = SLOTS[which] % 2, SLOTS[which] // 2
        turn = (y == slot_y) & ((z == slot_z) if mine else (z != slot_z))
        on = (
            turn & (z >= slot_z) & (z < depth - 1),
            turn & (z <= slot_z) & (z > 0),
            turn,
        )
        for way in range(3):

            @pl.when(on[way])
            def _(way=way):
                action(way)

    def send_own(which):
        for part in range(PARTS[which]):
            if part >= AHEAD:
                for_ways(which, True, lambda way: copy(which, part - AHEAD, way).wait_send())
            for_ways(which, True, lambda way: copy(which, part, way).start())

    def pass_on(group, first, last):
        for part in range(first, last):
            for which in group:

                @pl.when((y == SLOTS[which] % 2) & (z != SLOTS[which] // 2))
                def _(which=which, part=part):
                    copy(which, part, 2).wait_recv()

                for_ways(which, False, lambda way: copy(which, part, way).start())

    def latent_gradients():
        r.lat_grads[...] = jnp.zeros_like(r.lat_grads)
        r.lat_grads[2:6, :] = r.vectors_sum[0:4, :]

        def latent_rows(step, carry):
            at = rows_at(step * 32, 32)
            hat, inverse = norm(r.h_latents[at, :])
            grad = dot_nt(r.query_all[at, :], r.h_query_full[...])
            r.lat_grads[0:1, :] = r.lat_grads[0:1, :] + jnp.sum(grad * hat, axis=0, keepdims=True)
            r.lat_grads[1:2, :] = r.lat_grads[1:2, :] + jnp.sum(grad, axis=0, keepdims=True)
            scaled = grad * r.lat_vectors[0:1, :]
            r.latent_grad[at, :] = wide(r.rest_all[step // 4, (step // 2) % 2, step % 2]) + inverse * (
                scaled
                - jnp.mean(scaled, axis=-1, keepdims=True)
                - hat * jnp.mean(scaled * hat, axis=-1, keepdims=True)
            )
            return carry

        lax.fori_loop(0, r.latents.shape[0] // 32, latent_rows, 0)
        r.query_grad[...] = dot_tn(r.lat_block[...], r.query_all[...])

    few, many = (0, 1, 2, 3), (4, 5)
    own_first = opt * height
    gather_take(0)
    gather_give(1)

    @pl.when(big)
    def _():
        normalise(side)

        def sweep(index, carry):
            @pl.when(index == 1)
            def _():
                gather_take(1)
                gather_give(2)

            @pl.when(index == 3)
            def _():
                pass_on(few, 0, 2)

            @pl.when(index == 4)
            def _():
                gather_take(2)
                gather_give(3)
                pass_on(few, 2, 4)

            polynomial(r.whole, r.gram, r.poly)

            @pl.when(index < 4)
            def _():
                update(slice(0, side), side)

            return carry

        lax.fori_loop(0, 5, sweep, 0)
        update(rows_at(own_first, height), side)

    @pl.when(small)
    def _():
        normalise(both)

        def sweep(index, carry):
            polynomial(r.whole.at[:, :both], r.gram.at[:both, :both], r.poly.at[:both, :both])
            update(slice(0, side), both)
            return carry

        lax.fori_loop(0, 5, sweep, 0)

    for which in few + many:

        @pl.when(seq == SLOTS[which])
        def _(which=which):
            rows, cols = outs[which].shape
            if which == 3:
                for block in range(4):

                    @pl.when(opt == block)
                    def _(block=block):
                        lanes = slice(block * rows, (block + 1) * rows)
                        outs[which][...] = low(wide(r.whole[:, lanes]).T)
            else:
                outs[which][...] = r.whole[rows_at(own_first, rows), :cols]

    @pl.when(jnp.logical_not(big))
    def _():
        gather_take(1)
        gather_give(2)
        for which in few:
            send_own(which)
        pass_on(few, 0, 4)
        gather_take(2)
        gather_give(3)

    for which in many:
        send_own(which)
    gather_take(3)
    latent_gradients()
    pass_on(many, 0, 8)
    for which in few + many:
        for part in range(PARTS[which]):

            @pl.when(y != SLOTS[which] % 2)
            def _(which=which, part=part):
                copy(which, part, 2).wait_recv()

    for which in few + many:
        for part in range(PARTS[which]):
            for_ways(which, False, lambda way: copy(which, part, way).wait_send())
            if part >= PARTS[which] - AHEAD:
                for_ways(which, True, lambda way: copy(which, part, way).wait_send())
    for index, which in owned:
        piece_copy(index, which, seq, x, False).wait_send()

        @pl.when(seq != SLOTS[index])
        def _(index=index, which=which):
            piece_copy(index, which, seq, x, True).wait_send()

    for step in range(4):
        gathers(step, lambda copy: copy.wait_send())
    exchange.wait_send()
    courier.finish()


def run_tail(done, latents, lat_vectors, moments):
    f32, bf16 = jnp.float32, jnp.bfloat16
    mom_query, mom_key, mom_value, mom_out, mom_up, mom_down = moments
    width_lat = latents.shape[1]
    key, value = (
        grad.reshape(2, grad.shape[0] // 2, grad.shape[1])
        for grad in (done.grad_key, done.grad_value)
    )
    operands = dict(
        base=done.base,
        lat_low=done.lat_low,
        query_full=done.query_full,
        latents=latents,
        vectors=done.vectors,
        rest=done.rest,
        lat_block=done.lat_block,
        lat_vectors=lat_vectors,
        up=done.piece_up,
        down=done.piece_down,
        out=done.piece_out,
        key=key,
        value=value,
        query=done.grad_query,
    )
    outputs = dict(
        vectors_sum=(done.vectors.shape, f32),
        lat_grads=((8, width_lat), f32),
        latent_grad=(latents.shape, f32),
        query_grad=(mom_query.shape, f32),
        n_up=(mom_up.shape, bf16),
        n_down=(mom_down.shape, bf16),
        n_key=(mom_key.shape, bf16),
        n_value=(mom_value.shape, bf16),
        n_out=(mom_out.shape, bf16),
        o_query=(mom_query.shape, bf16),
        o_key=(mom_key.shape, bf16),
        o_value=(mom_value.shape, bf16),
        o_out=(mom_out.shape, bf16),
        o_up=(mom_up.shape, bf16),
        o_down=(mom_down.shape, bf16),
    )
    half_rest = (done.rest.shape[0], done.rest.shape[1] // 2)
    scratch = dict(
        h_base=(done.base.shape, bf16),
        h_lat_low=(done.lat_low.shape, bf16),
        h_query_full=(done.query_full.shape, bf16),
        h_latents=(latents.shape, f32),
        vectors_in=((5, *done.vectors.shape), f32),
        vectors_out=((4, *done.vectors.shape), f32),
        rest_in=((2, *half_rest), bf16),
        rest_sum=(half_rest, bf16),
        rest_all=((2, 2, 2, *done.rest.shape), bf16),
        query_all=(done.grad_query.shape, bf16),
        g_full=((2, width_lat, width_lat // 2), bf16),
        g_up=((width_lat // 2, width_lat // 2), bf16),
        g_down=((width_lat // 2, width_lat // 2), bf16),
        g_key=(key.shape[1:], bf16),
        g_value=(value.shape[1:], bf16),
        g_out=((2 * mom_out.shape[0], width_lat // 2), bf16),
        wide=((width_lat, width_lat), f32),
        whole=((width_lat, width_lat), bf16),
        gram=((width_lat, width_lat), bf16),
        poly=((width_lat, width_lat), bf16),
    )
    for which, name, array in (
        (KEY, "key", key),
        (VALUE, "value", value),
        (QUERY, "query", done.grad_query),
    ):
        for stage, shape in enumerate(chain_of(which, array.shape)):
            scratch[f"{name}_{stage}"] = (shape, bf16)
    copies = 48
    count = len(SLOTS) * max(PARTS)
    dma = pltpu.SemaphoreType.DMA
    sems = dict(
        send=dma((copies,)),
        recv=dma((copies,)),
        piece_send=dma((6, 2)),
        join_sem=dma((2,)),
        piece_recv=dma((2, 8)),
        gather_send=dma((5, 4)),
        gather_recv=dma((5, 4)),
        spread_send=dma((3, count)),
        spread_recv=dma((count,)),
        total=pltpu.SMEM((1,), f32),
        local=dma((4,)),
    )
    keys = (*operands, *outputs, *scratch, *sems)
    vmem, anywhere = pl.BlockSpec(memory_space=pltpu.VMEM), pl.BlockSpec(memory_space=pl.ANY)
    results = pl.pallas_call(
        functools.partial(tail_body, keys),
        out_shape=[jax.ShapeDtypeStruct(*spec) for spec in outputs.values()],
        in_specs=[anywhere] * 4 + [vmem] * (len(operands) - 4),
        out_specs=[vmem] * len(outputs),
        scratch_shapes=[*(pltpu.VMEM(*spec) for spec in scratch.values()), *sems.values()],
        compiler_params=pltpu.CompilerParams(
            collective_id=0, has_side_effects=True, vmem_limit_bytes=VMEM_LIMIT
        ),
        name="tail",
    )(*operands.values())
    return named(outputs, results)


def finish_body(keys, rates, *refs):
    r = named(keys, refs)
    count = len(rates)
    load = Loader(r.load_sem)
    into = lambda name, index: getattr(r, f"{name}{index}")
    loads = []
    for index in range(count):
        loads.append(
            [
                load.start(into(name, index), into("v" + name, index))
                for name in ("m", "g", "w", "o")
            ]
        )
    states = [
        load.start(source, target)
        for source, target in (
            (r.latents, r.vlatents),
            (r.first, r.vfirst),
            (r.second, r.vsecond),
            (r.grad, r.vgrad),
        )
    ]
    store = Loader(r.store_sem)
    stores = []

    def over_rows(ref, body):
        def step(index, carry):
            body(rows_at(index * 32, 32))
            return carry

        lax.fori_loop(0, ref.shape[0] // 32, step, 0)

    for index, (keep, rate) in enumerate(rates):
        moment, grad, weight, turn = (into("v" + name, index) for name in ("m", "g", "w", "o"))
        loads[index][0].wait()
        loads[index][1].wait()

        def new_moment(at, moment=moment, grad=grad):
            moment[at, :] = 0.95 * moment[at, :] + wide(grad[at, :])

        over_rows(moment, new_moment)
        stores.append(store.start(moment, into("nm", index)))
        loads[index][2].wait()
        loads[index][3].wait()

        def new_weight(at, weight=weight, turn=turn, keep=keep, rate=rate):
            weight[at, :] = keep * weight[at, :] - rate * wide(turn[at, :])

        over_rows(weight, new_weight)
        stores.append(store.start(weight, into("nw", index)))
    for copy in states:
        copy.wait()

    def new_latents(at):
        first, second, new = adam_update(
            r.vlatents[at, :], r.vgrad[at, :], r.vfirst[at, :], r.vsecond[at, :], 1.0, 0.1
        )
        r.vfirst[at, :], r.vsecond[at, :], r.vlatents[at, :] = first, second, new

    over_rows(r.vlatents, new_latents)
    for source, target in (
        (r.vfirst, r.nfirst),
        (r.vsecond, r.nsecond),
        (r.vlatents, r.nlatents),
    ):
        stores.append(store.start(source, target))
    r.lat_first_new[...], r.lat_second_new[...], r.lat_new[...] = adam_update(
        r.lat_vectors[...], r.lat_grads[:6, :], r.lat_first[...], r.lat_second[...], 0.6, 0.0
    )
    width = r.in_vectors.shape[1]
    r.in_first_new[...], r.in_second_new[...], r.in_new[...] = adam_update(
        r.in_vectors[...], r.vectors[4:6, :width], r.in_first[...], r.in_second[...], 0.6, 0.0
    )
    for copy in stores:
        copy.wait()


def run_finish(moments, gradients, masters, turns, latent_state, vector_state):
    f32 = jnp.float32
    fans = (D_LAT, E_IN, E_IN, OUT_FAN, D_LAT, D_LAT)
    sides = (D_LAT, E_IN, E_IN, D_LAT, D_LAT, D_LAT)
    rates = [
        (1.0 - 0.1 * fan ** (-0.5), fan ** (-0.5) * side**0.5) for fan, side in zip(fans, sides)
    ]
    large = {}
    for index, arrays in enumerate(zip(moments, gradients, masters, turns)):
        for name, array in zip(("m", "g", "w", "o"), arrays):
            large[f"{name}{index}"] = array
    large.update(latent_state)
    operands = {**large, **vector_state}
    outputs, scratch = {}, {}
    for index, moment in enumerate(moments):
        outputs[f"nm{index}"] = outputs[f"nw{index}"] = (moment.shape, f32)
    latents = latent_state["latents"].shape
    outputs.update(nfirst=(latents, f32), nsecond=(latents, f32), nlatents=(latents, f32))
    in_place = len(outputs)
    lat, inner = vector_state["lat_first"].shape, vector_state["in_first"].shape
    outputs.update(lat_first_new=(lat, f32), lat_second_new=(lat, f32), lat_new=(lat, f32))
    outputs.update(in_first_new=(inner, f32), in_second_new=(inner, f32), in_new=(inner, f32))
    for name, array in large.items():
        scratch["v" + name] = pltpu.VMEM(array.shape, array.dtype)
    scratch["load_sem"] = pltpu.SemaphoreType.DMA((len(large),))
    scratch["store_sem"] = pltpu.SemaphoreType.DMA((in_place,))
    vmem, anywhere = pl.BlockSpec(memory_space=pltpu.VMEM), pl.BlockSpec(memory_space=pl.ANY)
    results = pl.pallas_call(
        functools.partial(finish_body, (*operands, *outputs, *scratch), rates),
        out_shape=[jax.ShapeDtypeStruct(*spec) for spec in outputs.values()],
        in_specs=[anywhere] * len(large) + [vmem] * len(vector_state),
        out_specs=[anywhere] * in_place + [vmem] * 6,
        scratch_shapes=list(scratch.values()),
        compiler_params=pltpu.CompilerParams(vmem_limit_bytes=VMEM_LIMIT),
        name="finish",
    )(*operands.values())
    return named(outputs, results)


def adam_update(param, gradient, first, second, step_rate, decay):
    first_new = 0.9 * first + 0.1 * gradient
    second_new = 0.95 * second + 0.05 * gradient * gradient
    ratio = first_new / (1.0 - 0.9**STEP) / (jnp.sqrt(second_new / (1.0 - 0.95**STEP)) + 1e-08)
    return (first_new, second_new, param - step_rate * (ratio + decay * param))


def local_small(
    inputs,
    key_mask,
    lengths,
    cotangent,
    latents,
    lat_vectors,
    in_vectors,
    w_query,
    w_key,
    w_value,
    w_out,
    w_up,
    w_down,
    mom_query,
    mom_key,
    mom_value,
    mom_out,
    mom_up,
    mom_down,
    lat_first,
    lat_second,
    in_first,
    in_second,
    latent_first,
    latent_second,
):
    seq_index = lax.axis_index("seq")
    micro_count, _, span, width_in = inputs.shape
    lat_count, width_lat = latents.shape
    positions = seq_index * span + jnp.arange(span, dtype=jnp.int32)
    usable = (positions < lengths[:, :, None]) & ((key_mask == 1) | (positions == 0))
    masters = (w_query, w_key, w_value, w_out, w_up, w_down)
    moments = (mom_query, mom_key, mom_value, mom_out, mom_up, mom_down)
    done = run_pass(
        inputs.reshape(-1, width_in),
        usable.astype(jnp.float32),
        cotangent.reshape(-1, width_lat),
        latents,
        lat_vectors,
        in_vectors,
        masters,
        moments,
    )
    summed = run_tail(done, latents, lat_vectors, moments)
    gradients = (
        summed.query_grad,
        summed.n_key,
        summed.n_value,
        summed.n_out,
        summed.n_up,
        summed.n_down,
    )
    currents = (
        summed.o_query,
        summed.o_key,
        summed.o_value,
        summed.o_out,
        summed.o_up,
        summed.o_down,
    )
    new = run_finish(
        moments,
        gradients,
        masters,
        currents,
        dict(latents=latents, first=latent_first, second=latent_second, grad=summed.latent_grad),
        dict(
            lat_vectors=lat_vectors,
            lat_grads=summed.lat_grads,
            lat_first=lat_first,
            lat_second=lat_second,
            in_vectors=in_vectors,
            vectors=summed.vectors_sum,
            in_first=in_first,
            in_second=in_second,
        ),
    )
    return (
        done.block_out.reshape(cotangent.shape),
        done.input_grad.reshape(inputs.shape),
        new.nm0,
        new.nm1,
        new.nm2,
        new.nm3,
        new.nm4,
        new.nm5,
        new.nw0,
        new.nw1,
        new.nw2,
        new.nw3,
        new.nw4,
        new.nw5,
        new.lat_first_new,
        new.lat_second_new,
        new.lat_new,
        new.in_first_new,
        new.in_second_new,
        new.in_new,
        new.nfirst,
        new.nsecond,
        new.nlatents,
    )


def update_masters(masters, currents):
    fans = (D_LAT, E_IN, E_IN, OUT_FAN, D_LAT, D_LAT)
    sides = (D_LAT, E_IN, E_IN, D_LAT, D_LAT, D_LAT)
    new_masters = []
    for master, current, fan_in, long_side in zip(masters, currents, fans, sides):
        step_rate = fan_in ** (-0.5)
        new_masters.append(
            (1.0 - 0.1 * step_rate) * master
            - step_rate * long_side**0.5 * current.astype(jnp.float32)
        )
    return new_masters


def local(
    inputs,
    key_mask,
    lengths,
    cotangent,
    latents,
    lat_vectors,
    in_vectors,
    w_query,
    w_key,
    w_value,
    w_out,
    w_up,
    w_down,
    mom_query,
    mom_key,
    mom_value,
    mom_out,
    mom_up,
    mom_down,
    lat_first,
    lat_second,
    in_first,
    in_second,
    latent_first,
    latent_second,
):
    query_low, key_low, value_low, out_low, up_low, down_low = (
        lax.all_gather(w_query.astype(jnp.bfloat16), "opt", axis=0, tiled=True),
        lax.all_gather(w_key.astype(jnp.bfloat16), "opt", axis=0, tiled=True),
        lax.all_gather(w_value.astype(jnp.bfloat16), "opt", axis=0, tiled=True),
        lax.all_gather(w_out.astype(jnp.bfloat16), "opt", axis=0, tiled=True),
        lax.all_gather(w_up.astype(jnp.bfloat16), "opt", axis=0, tiled=True),
        lax.all_gather(w_down.astype(jnp.bfloat16), "opt", axis=0, tiled=True),
    )
    pair_low = jnp.concatenate([key_low, value_low], axis=1)
    seq_index = lax.axis_index("seq")
    seq_size = lax.axis_size("seq")
    opt_index = lax.axis_index("opt")
    opt_size = lax.axis_size("opt")
    micro_count, doc_local, span, width_in = inputs.shape
    lat_count, width_lat = latents.shape
    own_rows = lat_count // seq_size
    row_start = seq_index * own_rows
    score_scale = HEAD_DIM ** (-0.5)
    lat_normed, lat_hat, lat_inv = layer_norm(latents, lat_vectors[0], lat_vectors[1])
    lat_low = lat_normed.astype(jnp.bfloat16)
    query_rows = jnp.dot(lat_low, query_low, preferred_element_type=jnp.float32).astype(
        jnp.bfloat16
    )
    query_heads = query_rows.reshape(lat_count, HEADS, HEAD_DIM)
    own_latents = lax.dynamic_slice_in_dim(latents, row_start, own_rows, 0)
    positions = seq_index * span + jnp.arange(span, dtype=jnp.int32)
    grad_query_rows = jnp.zeros((lat_count, width_in), jnp.float32)
    grad_pair = jnp.zeros((width_in, 2 * width_in), jnp.float32)
    grad_out_w = jnp.zeros((width_in, width_lat), jnp.float32)
    grad_up_w = jnp.zeros((width_lat, width_lat), jnp.float32)
    grad_down_w = jnp.zeros((width_lat, width_lat), jnp.float32)
    mlp_gain = jnp.zeros((width_lat,), jnp.float32)
    mlp_shift = jnp.zeros((width_lat,), jnp.float32)
    bias_up = jnp.zeros((width_lat,), jnp.float32)
    bias_down = jnp.zeros((width_lat,), jnp.float32)
    in_gain = jnp.zeros((width_in,), jnp.float32)
    in_shift = jnp.zeros((width_in,), jnp.float32)
    latent_rest = jnp.zeros((own_rows, width_lat), jnp.float32)
    block_parts = []
    input_parts = []
    for micro_step in range(micro_count):
        tokens = inputs[micro_step]
        usable = (positions[None, :] < lengths[micro_step][:, None]) & (
            (key_mask[micro_step] == 1) | (positions[None, :] == 0)
        )
        in_normed, in_hat, in_inv = layer_norm(
            tokens.astype(jnp.float32), in_vectors[0], in_vectors[1]
        )
        in_low = in_normed.astype(jnp.bfloat16)
        pair_rows = jnp.einsum(
            "bse,ef->bsf", in_low, pair_low, preferred_element_type=jnp.float32
        ).astype(jnp.bfloat16)
        key_heads = pair_rows[:, :, :width_in].reshape(doc_local, span, HEADS, HEAD_DIM)
        value_heads = pair_rows[:, :, width_in:].reshape(doc_local, span, HEADS, HEAD_DIM)
        masked = masked_scores(query_heads, key_heads, usable, score_scale)
        row_max = lax.pmax(jnp.max(masked, axis=-1), "seq")
        weights = jnp.exp(masked - row_max[..., None])
        weights_low = weights.astype(jnp.bfloat16)
        summed, row_sum = (
            lax.psum(
                jnp.einsum(
                    "bhns,bshd->bnhd", weights_low, value_heads, preferred_element_type=jnp.float32
                ).astype(jnp.bfloat16),
                "seq",
            ).astype(jnp.float32),
            lax.psum(jnp.sum(weights, axis=-1).astype(jnp.bfloat16), "seq").astype(jnp.float32),
        )
        sum_heads = jnp.transpose(row_sum, (0, 2, 1))[..., None]
        attended = summed / sum_heads
        own_att = (
            lax.dynamic_slice_in_dim(attended, row_start, own_rows, 1)
            .reshape(doc_local, own_rows, width_in)
            .astype(jnp.bfloat16)
        )
        hidden = own_latents[None] + jnp.einsum(
            "bne,ef->bnf", own_att, out_low, preferred_element_type=jnp.float32
        )
        mlp_normed, mlp_hat, mlp_inv = layer_norm(hidden, lat_vectors[2], lat_vectors[3])
        mlp_low = mlp_normed.astype(jnp.bfloat16)
        pre_act = (
            jnp.einsum("bnf,fg->bng", mlp_low, up_low, preferred_element_type=jnp.float32)
            + lat_vectors[4]
        )
        activated, gelu_pull = jax.vjp(exact_gelu, pre_act)
        act_low = activated.astype(jnp.bfloat16)
        block_parts.append(
            (
                hidden
                + jnp.einsum("bng,gk->bnk", act_low, down_low, preferred_element_type=jnp.float32)
                + lat_vectors[5]
            ).astype(jnp.bfloat16)
        )
        back_rows = cotangent[micro_step]
        grad_down_w = grad_down_w + jnp.einsum(
            "bng,bnk->gk", act_low, back_rows, preferred_element_type=jnp.float32
        )
        bias_down = bias_down + jnp.sum(back_rows.astype(jnp.float32), axis=(0, 1))
        grad_act = jnp.einsum(
            "bnk,gk->bng", back_rows, down_low, preferred_element_type=jnp.float32
        )
        grad_pre = gelu_pull(grad_act)[0].astype(jnp.bfloat16)
        grad_up_w = grad_up_w + jnp.einsum(
            "bnf,bng->fg", mlp_low, grad_pre, preferred_element_type=jnp.float32
        )
        bias_up = bias_up + jnp.sum(grad_pre.astype(jnp.float32), axis=(0, 1))
        grad_mlp = jnp.einsum("bng,fg->bnf", grad_pre, up_low, preferred_element_type=jnp.float32)
        mlp_gain = mlp_gain + jnp.sum(grad_mlp * mlp_hat, axis=(0, 1))
        mlp_shift = mlp_shift + jnp.sum(grad_mlp, axis=(0, 1))
        grad_hidden = back_rows.astype(jnp.float32) + norm_back(
            grad_mlp, mlp_hat, mlp_inv, lat_vectors[2]
        )
        latent_rest = latent_rest + jnp.sum(grad_hidden, axis=0)
        grad_branch = grad_hidden.astype(jnp.bfloat16)
        grad_out_w = grad_out_w + jnp.einsum(
            "bne,bnf->ef", own_att, grad_branch, preferred_element_type=jnp.float32
        )
        grad_own = jnp.einsum(
            "bnf,ef->bne", grad_branch, out_low, preferred_element_type=jnp.float32
        ).astype(jnp.bfloat16)
        grad_att = (
            lax.all_gather(grad_own, "seq", axis=1, tiled=True)
            .astype(jnp.float32)
            .reshape(doc_local, lat_count, HEADS, HEAD_DIM)
        )
        grad_summed = (grad_att / sum_heads).astype(jnp.bfloat16)
        inner = jnp.transpose(jnp.sum(grad_att * attended, axis=-1) / sum_heads[..., 0], (0, 2, 1))
        grad_prob = jnp.einsum(
            "bnhd,bshd->bhns", grad_summed, value_heads, preferred_element_type=jnp.float32
        )
        grad_scores = (weights * (grad_prob - inner[..., None])).astype(jnp.bfloat16)
        grad_query_rows = grad_query_rows + score_scale * jnp.einsum(
            "bhns,bshd->nhd", grad_scores, key_heads, preferred_element_type=jnp.float32
        ).reshape(lat_count, width_in)
        grad_keys = (
            score_scale
            * jnp.einsum(
                "bhns,nhd->bshd", grad_scores, query_heads, preferred_element_type=jnp.float32
            )
        ).astype(jnp.bfloat16)
        grad_values = jnp.einsum(
            "bhns,bnhd->bshd", weights_low, grad_summed, preferred_element_type=jnp.float32
        ).astype(jnp.bfloat16)
        grad_pairs = jnp.concatenate(
            [
                grad_keys.reshape(doc_local, span, width_in),
                grad_values.reshape(doc_local, span, width_in),
            ],
            axis=-1,
        )
        grad_pair = grad_pair + jnp.einsum(
            "bse,bsf->ef", in_low, grad_pairs, preferred_element_type=jnp.float32
        )
        grad_in = jnp.einsum(
            "bsf,ef->bse", grad_pairs, pair_low, preferred_element_type=jnp.float32
        )
        in_gain = in_gain + jnp.sum(grad_in * in_hat, axis=(0, 1))
        in_shift = in_shift + jnp.sum(grad_in, axis=(0, 1))
        input_parts.append(norm_back(grad_in, in_hat, in_inv, in_vectors[0]))
    grad_query_w = jnp.matmul(lat_low.astype(jnp.float32).T, grad_query_rows, precision=highest)
    grad_lat = jnp.matmul(grad_query_rows, query_low.astype(jnp.float32).T, precision=highest)
    zero_index = jnp.zeros((), jnp.int32)
    latent_grad = norm_back(grad_lat, lat_hat, lat_inv, lat_vectors[0]) + lax.dynamic_update_slice(
        jnp.zeros_like(latents), latent_rest, (row_start, zero_index)
    )
    lat_vec_grad = jnp.stack(
        [
            jnp.sum(grad_lat * lat_hat, axis=0),
            jnp.sum(grad_lat, axis=0),
            mlp_gain,
            mlp_shift,
            bias_up,
            bias_down,
        ]
    )
    in_vec_grad = jnp.stack([in_gain, in_shift])
    weight_grads = (
        grad_query_w,
        grad_pair[:, :width_in],
        grad_pair[:, width_in:],
        grad_out_w,
        grad_up_w,
        grad_down_w,
    )
    masters = (w_query, w_key, w_value, w_out, w_up, w_down)
    moments = (mom_query, mom_key, mom_value, mom_out, mom_up, mom_down)
    first_here = jnp.where(seq_index == 0, 0.95, 0.0)
    with_moment = []
    for gradient, moment in zip(weight_grads, moments):
        start = opt_index * moment.shape[0]
        rows = lax.dynamic_slice_in_dim(gradient, start, moment.shape[0], 0) + first_here * moment
        with_moment.append(
            lax.dynamic_update_slice(gradient, rows, (start, zero_index)).astype(jnp.bfloat16)
        )
    summed_low = lax.psum(tuple(with_moment), ("seq", "opt"))
    lat_vec_sum, in_vec_sum, latent_sum = lax.psum(
        (lat_vec_grad, in_vec_grad, latent_grad), ("seq", "opt")
    )
    moments_new = [
        lax.dynamic_slice_in_dim(summed, opt_index * moment.shape[0], moment.shape[0], 0).astype(
            jnp.float32
        )
        for summed, moment in zip(summed_low, moments)
    ]

    def padded(index):
        def pick():
            matrix = summed_low[index].T if index == 3 else summed_low[index]
            return jnp.pad(
                matrix, ((0, width_lat - matrix.shape[0]), (0, width_lat - matrix.shape[1]))
            )

        return pick

    slot = seq_index % 8
    own_matrix = lax.switch(jnp.minimum(slot, 5), [padded(index) for index in range(6)])
    own_result = newton(own_matrix)
    own_result = lax.cond(slot == 3, lambda: own_result.T, lambda: own_result)
    mine = jnp.stack(
        [
            lax.dynamic_slice_in_dim(own_result, opt_index * height, width_lat // opt_size, 0)
            for height in (width_in // opt_size, width_lat // opt_size)
        ]
    )
    is_wide = (slot == 0) | (slot >= 4)
    mine = jnp.where(is_wide, mine[1], mine[0])
    spread = lax.all_gather(mine, "seq", axis=0, tiled=False)
    currents = [
        spread[index, : moment.shape[0], : moment.shape[1]].astype(jnp.float32)
        for index, moment in enumerate(moments)
    ]
    new_masters = update_masters(masters, currents)
    lat_m, lat_v, lat_p = adam_update(lat_vectors, lat_vec_sum, lat_first, lat_second, 0.6, 0.0)
    in_m, in_v, in_p = adam_update(in_vectors, in_vec_sum, in_first, in_second, 0.6, 0.0)
    latent_m, latent_v, latent_p = adam_update(
        latents, latent_sum, latent_first, latent_second, 1.0, 0.1
    )
    block_out = jnp.stack(block_parts)
    input_grad = jnp.stack(input_parts)
    return (
        block_out,
        input_grad,
        moments_new[0],
        moments_new[1],
        moments_new[2],
        moments_new[3],
        moments_new[4],
        moments_new[5],
        new_masters[0],
        new_masters[1],
        new_masters[2],
        new_masters[3],
        new_masters[4],
        new_masters[5],
        lat_m,
        lat_v,
        lat_p,
        in_m,
        in_v,
        in_p,
        latent_m,
        latent_v,
        latent_p,
    )


def solution(mesh):
    small = (mesh.shape["seq"], mesh.shape["opt"]) == (8, 4)
    return jax.shard_map(
        local_small if small else local,
        mesh=mesh,
        in_specs=(
            P(None, "opt", "seq", None),
            P(None, "opt", "seq"),
            P(None, "opt"),
            P(None, "opt", "seq", None),
            P(),
            P(),
            P(),
            P("opt", None),
            P("opt", None),
            P("opt", None),
            P("opt", None),
            P("opt", None),
            P("opt", None),
            P("opt", None),
            P("opt", None),
            P("opt", None),
            P("opt", None),
            P("opt", None),
            P("opt", None),
            P(),
            P(),
            P(),
            P(),
            P(),
            P(),
        ),
        out_specs=(
            P(None, "opt", "seq", None),
            P(None, "opt", "seq", None),
            P("opt", None),
            P("opt", None),
            P("opt", None),
            P("opt", None),
            P("opt", None),
            P("opt", None),
            P("opt", None),
            P("opt", None),
            P("opt", None),
            P("opt", None),
            P("opt", None),
            P("opt", None),
            P(),
            P(),
            P(),
            P(),
            P(),
            P(),
            P(),
            P(),
            P(),
        ),
        check_vma=False,
    )
```
